256 devices in a mesh: range: 16 (over z, core), az: 16 (over y, x).
Axes of the slice: x: 4, y: 4, z: 8, core: 2. Of those that a mesh axis runs over, the one named last changes fastest.
Arguments:
- return_integer_lag: int32 [16, 128, 8], P('az'), may hold values from 0 to 32703
- return_fractional_lag: float32 [16, 128, 8], P('az'), may hold values from 0 to 8
- return_field_strength: float32 [16, 128, 8], P('az'), may hold values from 0.1 to 0.6
- sector_emit_offset: int32 [16], P('az'), may hold values from 0 to 63
- sector_active_returns: int32 [16], P('az'), may hold values from 1 to 8, as said below
- ambient_photon_flux: float32 [128], replicated, may hold values from 0.2 to 1
- coded_emission_spectrum: float32 [128, 2, 16384], P('range', None, 'az'), may hold values from -6 to 6
Outputs:
- histogram: float32 [16, 128, 16384], P('az', None, 'range')
The draws below stay inside these ranges and needn't reach their ends.
Inputs may be any that keep to these rules, and one draw needn't show every extreme that they name: `sector_active_returns`: slots below a column's count are live; some column has all 8 slots live and some column only one.
All inputs are finite; a program needn't handle non-finite values.
Results may differ from the reference program's by a relative error of at most 0.0003.
Values sent between devices are 32-bit elements; how exact they have to be, the bound alone decides.
A program may use at most 64 MiB of HBM per device.

```python
import math
import jax
import jax.numpy as jnp
from jax import lax

LASER_RAYS = 128
TIME_SLOTS = 16384
RETURN_SLOTS = 8
MAX_EMIT_OFFSET = 64
SCAN_SECTORS = 16


def draw_sector_active_returns(key, part):
    key = jax.random.fold_in(key, 11)
    subkeys = jax.random.split(key, 3)
    counts = jax.random.randint(subkeys[0], (SCAN_SECTORS,), 1, RETURN_SLOTS + 1, dtype=jnp.int32)
    fullest = jax.random.randint(subkeys[1], (), 0, SCAN_SECTORS, dtype=jnp.int32)
    sparsest = (fullest + 1 + jax.random.randint(subkeys[2], (), 0, SCAN_SECTORS - 1, dtype=jnp.int32)) % SCAN_SECTORS
    counts = counts.at[fullest].set(RETURN_SLOTS)
    return counts.at[sparsest].set(1)


def plant(values, own_key, smallest, largest):
    dims = values.shape
    index_at = [jax.random.randint(jax.random.fold_in(own_key, axis), (), 0, dims[axis]) for axis in range(len(dims))]
    values = values.at[tuple(index_at)].set(smallest)
    longest = dims.index(max(dims))
    index_at[longest] = (index_at[longest] + 1) % dims[longest]
    return values.at[tuple(index_at)].set(largest)


def shard_levels(own_key, shape, cuts, least, top_value):
    loudness = 1.0
    for dim, parts in cuts:
        heights = jax.random.uniform(jax.random.fold_in(jax.random.fold_in(own_key, 6), dim), (parts,), jnp.float32, least / len(cuts), top_value / len(cuts))
        loudness = loudness * jnp.repeat(jnp.exp(heights), shape[dim] // parts).reshape((-1,) + (1,) * (len(shape) - 1 - dim))
    return loudness


def bell_draw(rng, extent, spread, bound, cuts=(), held_as=jnp.bfloat16):
    drawn = spread * jax.random.normal(rng, extent, jnp.float32)
    if cuts:
        drawn = drawn * shard_levels(rng, extent, cuts, -0.22, 0.18)
    return jnp.clip(drawn, -bound, bound).astype(held_as)


def setup_inputs(seed: int = 0) -> dict:
    keys = jax.random.split(jax.random.key(seed), 8)
    return {
        "return_integer_lag": plant(jax.random.randint(keys[0], (SCAN_SECTORS, LASER_RAYS, RETURN_SLOTS), 0, 2 * TIME_SLOTS - MAX_EMIT_OFFSET), jax.random.fold_in(keys[0], 1), 0, (2 * TIME_SLOTS - MAX_EMIT_OFFSET) - 1).astype(jnp.int32),
        "return_fractional_lag": jnp.clip(8.0 * jax.random.uniform(keys[1], (SCAN_SECTORS, LASER_RAYS, RETURN_SLOTS), jnp.float32) ** shard_levels(keys[1], (SCAN_SECTORS, LASER_RAYS, RETURN_SLOTS), ((0, 16),), -0.2, 0.2), 0.0, 8.0),
        "return_field_strength": jnp.clip(jnp.exp(math.log(0.6) - 1.7917595 * jax.random.uniform(keys[2], (SCAN_SECTORS, LASER_RAYS, RETURN_SLOTS), jnp.float32) ** shard_levels(keys[2], (SCAN_SECTORS, LASER_RAYS, RETURN_SLOTS), ((0, 16),), -0.2, 0.2)), 0.1, 0.6),
        "sector_emit_offset": plant(jax.random.randint(keys[3], (SCAN_SECTORS,), 0, MAX_EMIT_OFFSET), jax.random.fold_in(keys[3], 1), 0, MAX_EMIT_OFFSET - 1).astype(jnp.int32),
        "sector_active_returns": draw_sector_active_returns(jax.random.fold_in(keys[7], 71), 0),
        "ambient_photon_flux": jnp.clip(jnp.exp(jax.random.uniform(keys[5], (LASER_RAYS,), jnp.float32, math.log(0.2), math.log(1.0))), 0.2, 1.0),
        "coded_emission_spectrum": bell_draw(keys[6], (LASER_RAYS, 2, TIME_SLOTS), 1.0, 6.0, ((0, 16), (2, 16)), jnp.float32),
    }


def column_light(bins_col, fracs_col, amps_col, offset_col, count_col, coded_emission_spectrum, far_trip):
    return_travel_times = bins_col + offset_col
    live_slot = jnp.arange(RETURN_SLOTS, dtype=jnp.int32)[None, :] < count_col
    near_trip = return_travel_times < TIME_SLOTS
    chosen = jnp.logical_not(near_trip) if far_trip else near_trip
    weights = jnp.where(live_slot & chosen, amps_col, 0.0)
    frequency = jnp.arange(TIME_SLOTS, dtype=jnp.int32)
    signed = (frequency - TIME_SLOTS * (frequency >= TIME_SLOTS // 2).astype(jnp.int32)).astype(jnp.float32)
    whole_turns = ((frequency[None, None, :] * return_travel_times[:, :, None]) % TIME_SLOTS).astype(jnp.float32) / TIME_SLOTS
    angles = 2.0 * jnp.pi * (whole_turns + signed[None, None, :] * fracs_col[:, :, None] / TIME_SLOTS)
    real_sum = jnp.sum(weights[:, :, None] * jnp.cos(angles), axis=1)
    imag_sum = -jnp.sum(weights[:, :, None] * jnp.sin(angles), axis=1)
    filt_real = coded_emission_spectrum[:, 0] * real_sum - coded_emission_spectrum[:, 1] * imag_sum
    filt_imag = coded_emission_spectrum[:, 0] * imag_sum + coded_emission_spectrum[:, 1] * real_sum
    field = jnp.fft.ifft(filt_real + 1j * filt_imag, axis=-1)
    return (jnp.real(field) ** 2 + jnp.imag(field) ** 2) * TIME_SLOTS


def reference(return_integer_lag, return_fractional_lag, return_field_strength, sector_emit_offset, sector_active_returns, ambient_photon_flux, coded_emission_spectrum):
    def far_column(sector_index):
        return column_light(return_integer_lag[sector_index], return_fractional_lag[sector_index], return_field_strength[sector_index],
                            sector_emit_offset[sector_index], sector_active_returns[sector_index], coded_emission_spectrum, True)

    far_all = lax.map(far_column, jnp.arange(SCAN_SECTORS, dtype=jnp.int32))

    def finish(sector_index):
        near_light = column_light(return_integer_lag[sector_index], return_fractional_lag[sector_index], return_field_strength[sector_index],
                                  sector_emit_offset[sector_index], sector_active_returns[sector_index], coded_emission_spectrum, False)
        before_light = far_all[(sector_index + SCAN_SECTORS - 1) % SCAN_SECTORS]
        flux = (ambient_photon_flux[:, None] + near_light + before_light) / TIME_SLOTS
        before = jnp.cumsum(flux, axis=-1) - flux
        return TIME_SLOTS * (-jnp.expm1(-flux)) * jnp.exp(-before)

    return lax.map(finish, jnp.arange(SCAN_SECTORS, dtype=jnp.int32))
```

```python
import functools
import math

import jax
import jax.numpy as jnp
from jax import lax
from jax.experimental import pallas as pl
from jax.experimental.pallas import tpu as pltpu
from jax.sharding import PartitionSpec as P

TIME_SLOTS = 16384
SIDE = 128
BEAMS = 8
SLOTS = 8
GROUP = 16
MESH = pl.DeviceIdType.MESH
F32 = jnp.float32
BF16 = jnp.bfloat16


def iota(shape, dim):
    return lax.broadcasted_iota(jnp.int32, shape, dim)


def cos_sin(turns):
    x = (turns - jnp.round(turns)) * math.pi
    y = x * x
    s = -1.0 / 39916800 * y + 1.0 / 362880
    s = s * y - 1.0 / 5040
    s = s * y + 1.0 / 120
    s = s * y - 1.0 / 6
    s = (s * y + 1.0) * x
    c = 1.0 / 479001600 * y - 1.0 / 3628800
    c = c * y + 1.0 / 40320
    c = c * y - 1.0 / 720
    c = c * y + 1.0 / 24
    c = c * y - 0.5
    c = c * y + 1.0
    return 1.0 - 2.0 * s * s, 2.0 * s * c


def split(x):
    hi = x.astype(BF16)
    return hi, (x - hi.astype(F32)).astype(BF16)


def dot(a, b):
    return jnp.dot(a, b, preferred_element_type=F32)


def dot3(a_hi, a_lo, b_hi, b_lo):
    return dot(a_hi, b_hi) + dot(a_hi, b_lo) + dot(a_lo, b_hi)


def blocks(a, b, c, d):
    return jnp.concatenate(
        [jnp.concatenate([a, b], axis=1), jnp.concatenate([c, d], axis=1)], axis=0
    )


def dft_tables():
    row, col = iota((SIDE, SIDE), 0), iota((SIDE, SIDE), 1)
    c, s = cos_sin(((row * col) & (SIDE - 1)).astype(F32) * (1.0 / SIDE))
    left = split(blocks(c, -s, s, c))
    right = split(blocks(c, s, -s, c))
    twist = cos_sin((row * col).astype(F32) * (1.0 / TIME_SLOTS))
    return left, right, twist


def prefix_tables():
    row, col = iota((SIDE, SIDE), 0), iota((SIDE, SIDE), 1)
    upper = jnp.where(row < col, 1.0, 0.0).astype(F32)
    ones = jnp.ones((SIDE, SIDE), F32)
    lower = jnp.where(col < row, 1.0, 0.0).astype(F32)
    inner = blocks(upper, ones, upper, ones).astype(BF16)
    outer = jnp.concatenate([lower, lower], axis=1).astype(BF16)
    return inner, outer


def as_column(near, far):
    near_rows = jnp.concatenate(
        [jnp.broadcast_to(near[b : b + 1], (2 * SLOTS, SLOTS)) for b in range(BEAMS)], axis=0
    )
    far_rows = jnp.concatenate(
        [jnp.broadcast_to(far[b : b + 1], (2 * SLOTS, SLOTS)) for b in range(BEAMS)], axis=0
    )
    row, col = iota((SIDE, SLOTS), 0), iota((SIDE, SLOTS), 1)
    rows = jnp.where((row & SLOTS) == 0, near_rows, far_rows)
    return jnp.sum(jnp.where((row & (SLOTS - 1)) == col, rows, 0.0), axis=1, keepdims=True)


def as_row(column):
    row, col = iota((SIDE, SIDE), 0), iota((SIDE, SIDE), 1)
    wide = jnp.broadcast_to(column, (SIDE, SIDE))
    return jnp.sum(jnp.where(row == col, wide, 0.0), axis=0, keepdims=True)


def phase_tables(near, far):
    delay, frac, amp = [as_column(n, f) for n, f in zip(near, far)]
    row, col = iota((SIDE, SIDE), 0), iota((SIDE, SIDE), 1)
    whole = (col * delay.astype(jnp.int32)) & (TIME_SLOTS - 1)
    inner_c, inner_s = cos_sin((whole.astype(F32) + col.astype(F32) * frac) * (1.0 / TIME_SLOTS))
    inner_c, inner_s = inner_c * amp, inner_s * amp
    near_row = (row & SLOTS) == 0
    parts = []
    for x in (inner_c, inner_s):
        parts.append(
            jnp.concatenate([jnp.where(near_row, x, 0.0), jnp.where(near_row, 0.0, x)], axis=1)
        )
    right = split(jnp.concatenate(parts, axis=0))
    signed = row - jnp.where(row >= SIDE // 2, SIDE, 0)
    whole = (signed * as_row(delay).astype(jnp.int32)) & (SIDE - 1)
    outer_c, outer_s = cos_sin((whole.astype(F32) + signed.astype(F32) * as_row(frac)) * (1.0 / SIDE))
    left = split(blocks(outer_c, -outer_s, -outer_s, -outer_c))
    return left, right


def spectrum(left, right, beam):
    mine = ((iota((2 * SIDE, 2 * SIDE), 0) & (SIDE - 1)) >> 4) == beam
    hi, lo = [jnp.where(mine, x.astype(F32), 0.0).astype(BF16) for x in right]
    return dot3(left[0], left[1], hi, lo)


def light_of(spec, pulse_real, pulse_imag, left, right, twist):
    spec_real, spec_imag = spec[:SIDE], spec[SIDE:]
    wide_real = jnp.concatenate([pulse_real, pulse_real], axis=1)
    wide_imag = jnp.concatenate([pulse_imag, pulse_imag], axis=1)
    filt = jnp.concatenate(
        [wide_real * spec_real - wide_imag * spec_imag, wide_real * spec_imag + wide_imag * spec_real],
        axis=0,
    )
    section = dot3(left[0], left[1], *split(filt))
    rows = []
    for trip in range(2):
        real = section[:SIDE, trip * SIDE : (trip + 1) * SIDE]
        imag = section[SIDE:, trip * SIDE : (trip + 1) * SIDE]
        rows.append(
            jnp.concatenate(
                [real * twist[0] - imag * twist[1], real * twist[1] + imag * twist[0]], axis=1
            )
        )
    hi, lo = split(jnp.concatenate(rows, axis=0))
    field = dot(hi, right[0]) + dot(hi, right[1]) + dot(lo, right[0])
    power = field * field
    power = power[:SIDE] + power[SIDE:]
    return power[:, :SIDE] + power[:, SIDE:]


def pile_up(power, ambient, inner, outer):
    flux = (power * (1.0 / TIME_SLOTS) + ambient) * (1.0 / TIME_SLOTS)
    flux = jnp.transpose(flux)
    hi, lo = split(flux)
    sums = dot(jnp.concatenate([hi, lo], axis=1), inner)
    within, totals = sums[:, :SIDE], sums[:, SIDE:]
    hi, lo = split(totals)
    before = within + dot(outer, jnp.concatenate([hi, lo], axis=0))
    series = 1.0 - flux * (1.0 / 6)
    for k in (5, 4, 3, 2):
        series = 1.0 - flux * (1.0 / k) * series
    detected = jnp.where(flux < 0.1, flux * series, 1.0 - jnp.exp(-flux))
    return TIME_SLOTS * detected * jnp.exp(-before)


def kernel(
    chunk,
    lag_ref, frac_ref, amp_ref, offset_ref, count_ref, ambient_ref, pulse_ref,
    out_ref,
    own, gathered, echo_out, echo_in, spec, left_tab, right_tab, twist_tab, inner_tab, outer_tab,
    ready, arrived,
    pulse_send, pulse_recv, echo_send, echo_recv, hist_send, hist_recv,
):
    me_range, me_az = lax.axis_index("range"), lax.axis_index("az")
    chunks = BEAMS // chunk
    barrier = pltpu.get_barrier_semaphore()

    def greet(k, carry):
        pl.semaphore_signal(barrier, inc=1, device_id={"az": lax.rem(me_az + k, GROUP)}, device_id_type=MESH)
        pl.semaphore_signal(barrier, inc=1, device_id={"range": lax.rem(me_range + k, GROUP)}, device_id_type=MESH)
        return carry

    lax.fori_loop(1, GROUP, greet, 0)

    for b in range(BEAMS):
        for part in range(2):
            for q in range(8):
                own[b, part, q : q + 1, :] = pulse_ref[b, part : part + 1, q * SIDE : (q + 1) * SIDE]
    first = pl.multiple_of(me_range * BEAMS, BEAMS)
    delay = lag_ref[0, pl.ds(first, BEAMS), :] + offset_ref[0]
    frac = frac_ref[0, pl.ds(first, BEAMS), :]
    amp = amp_ref[0, pl.ds(first, BEAMS), :]
    live = iota((BEAMS, SLOTS), 1) < count_ref[0]
    near_trip = delay < TIME_SLOTS
    near_amp = jnp.where(live & near_trip, amp, 0.0)
    far_amp = jnp.where(live & jnp.logical_not(near_trip), amp, 0.0)
    delay = delay.astype(F32)
    echo_out[...] = jnp.zeros_like(echo_out)
    echo_out[0, :, :SLOTS] = delay
    echo_out[1, :, :SLOTS] = frac
    echo_out[2, :, :SLOTS] = far_amp

    pl.semaphore_wait(barrier, 2 * (GROUP - 1))

    echo_copy = pltpu.make_async_remote_copy(
        src_ref=echo_out, dst_ref=echo_in, send_sem=echo_send, recv_sem=echo_recv,
        device_id={"az": lax.rem(me_az + 1, GROUP)}, device_id_type=MESH,
    )
    echo_copy.start()

    def send_pulses(i, carry):
        c = i // (GROUP - 1)
        k = lax.rem(i, GROUP - 1) + 1
        beams = pl.ds(c * chunk, chunk)
        pltpu.make_async_remote_copy(
            src_ref=own.at[beams], dst_ref=gathered.at[me_az, beams],
            send_sem=pulse_send, recv_sem=pulse_recv.at[c],
            device_id={"az": lax.rem(me_az + k, GROUP)}, device_id_type=MESH,
        ).start()
        return carry

    lax.fori_loop(0, chunks * (GROUP - 1), send_pulses, 0)
    gathered[me_az] = own[...]

    left, right, twist = dft_tables()
    for i in range(2):
        left_tab[i] = left[i]
        right_tab[i] = right[i]
        twist_tab[i] = twist[i]
    inner_tab[...], outer_tab[...] = prefix_tables()

    echo_copy.wait_recv()
    far = tuple(echo_in[i, :, :SLOTS] for i in range(3))
    echo_left, echo_right = phase_tables((delay, frac, near_amp), far)
    for b in range(BEAMS):
        spec[b] = spectrum(echo_left, echo_right, b)

    def work(c, carry):
        beams = pl.ds(c * chunk, chunk)
        some = gathered.at[pl.ds(0, GROUP - 1), beams]
        pltpu.make_async_remote_copy(
            src_ref=some, dst_ref=some, send_sem=pulse_send, recv_sem=pulse_recv.at[c],
            device_id={"az": me_az}, device_id_type=MESH,
        ).wait_recv()
        for j in range(chunk):
            b = c * chunk + j
            pulse_real = gathered[:, b, 0].reshape(SIDE, SIDE)
            pulse_imag = gathered[:, b, 1].reshape(SIDE, SIDE)
            power = light_of(
                spec[b], pulse_real, pulse_imag,
                (left_tab[0], left_tab[1]), (right_tab[0], right_tab[1]), (twist_tab[0], twist_tab[1]),
            )
            hist = pile_up(power, ambient_ref[first + b], inner_tab[...], outer_tab[...])
            for g in range(GROUP):
                ready[pl.ds(pl.multiple_of((g * BEAMS + b) * 8, 8), 8), :] = hist[g * 8 : (g + 1) * 8]
        here = pl.ds(pl.multiple_of((me_range * BEAMS + c * chunk) * 8, 8), chunk * 8)

        def send(k, carry):
            peer = lax.rem(me_range + k, GROUP)
            there = pl.ds(pl.multiple_of((peer * BEAMS + c * chunk) * 8, 8), chunk * 8)
            pltpu.make_async_remote_copy(
                src_ref=ready.at[there], dst_ref=arrived.at[here],
                send_sem=hist_send, recv_sem=hist_recv,
                device_id={"range": peer}, device_id_type=MESH,
            ).start()
            return carry

        lax.fori_loop(1, GROUP, send, 0)
        arrived[here, :] = ready[here, :]
        return carry

    lax.fori_loop(0, chunks, work, 0)

    most = pl.ds(0, (GROUP - 1) * BEAMS * 8)
    done = pltpu.make_async_remote_copy(
        src_ref=ready.at[most], dst_ref=arrived.at[most], send_sem=hist_send, recv_sem=hist_recv,
        device_id={"range": me_range}, device_id_type=MESH,
    )
    done.wait_recv()
    for g in range(GROUP):
        for s in range(8):
            out_ref[0, g * 8 : (g + 1) * 8, s * SIDE : (s + 1) * SIDE] = arrived[
                pl.ds(g * 64 + s, 8, stride=8), :
            ]
    done.wait_send()
    echo_copy.wait_send()
    pltpu.make_async_remote_copy(
        src_ref=gathered.at[pl.ds(0, GROUP - 1)], dst_ref=gathered.at[pl.ds(0, GROUP - 1)],
        send_sem=pulse_send, recv_sem=pulse_recv.at[0],
        device_id={"az": me_az}, device_id_type=MESH,
    ).wait_send()


def per_device(*arrays):
    chunk = 2
    vmem = pl.BlockSpec(memory_space=pltpu.VMEM)
    smem = pl.BlockSpec(memory_space=pltpu.SMEM)
    dma = pltpu.SemaphoreType.DMA
    return pl.pallas_call(
        functools.partial(kernel, chunk),
        out_shape=jax.ShapeDtypeStruct((1, GROUP * BEAMS, TIME_SLOTS // GROUP), F32),
        in_specs=[vmem, vmem, vmem, smem, smem, smem, vmem],
        out_specs=vmem,
        scratch_shapes=[
            pltpu.VMEM((BEAMS, 2, 8, SIDE), F32),
            pltpu.VMEM((GROUP, BEAMS, 2, 8, SIDE), F32),
            pltpu.VMEM((3, BEAMS, SIDE), F32),
            pltpu.VMEM((3, BEAMS, SIDE), F32),
            pltpu.VMEM((BEAMS, 2 * SIDE, 2 * SIDE), F32),
            pltpu.VMEM((2, 2 * SIDE, 2 * SIDE), BF16),
            pltpu.VMEM((2, 2 * SIDE, 2 * SIDE), BF16),
            pltpu.VMEM((2, SIDE, SIDE), F32),
            pltpu.VMEM((2 * SIDE, 2 * SIDE), BF16),
            pltpu.VMEM((SIDE, 2 * SIDE), BF16),
            pltpu.VMEM((GROUP * BEAMS * 8, SIDE), F32),
            pltpu.VMEM((GROUP * BEAMS * 8, SIDE), F32),
            dma, dma((BEAMS // chunk,)), dma, dma, dma, dma,
        ],
        compiler_params=pltpu.CompilerParams(
            collective_id=0, has_side_effects=True, vmem_limit_bytes=40 * 1024 * 1024
        ),
    )(*arrays)


def solution(mesh):
    in_specs = (
        P("az", None, None),
        P("az", None, None),
        P("az", None, None),
        P("az"),
        P("az"),
        P(),
        P("range", None, "az"),
    )
    out_specs = P("az", None, "range")
    return jax.shard_map(
        per_device, mesh=mesh, in_specs=in_specs, out_specs=out_specs, check_vma=False
    )
```

```python
import math

import jax
import jax.numpy as jnp
from jax import lax
from jax.experimental import pallas as pl
from jax.experimental.pallas import tpu as pltpu
from jax.sharding import PartitionSpec as P

TIME_SLOTS = 16384
SIDE = 128
BEAMS = 8
SLOTS = 8
GROUP = 16
SIDE_AZ = 4
MESH = pl.DeviceIdType.MESH
F32 = jnp.float32
BF16 = jnp.bfloat16


def iota(shape, dim):
    return lax.broadcasted_iota(jnp.int32, shape, dim)


def cos_sin(turns):
    x = (turns - jnp.round(turns)) * math.pi
    y = x * x
    s = -1.0 / 39916800 * y + 1.0 / 362880
    s = s * y - 1.0 / 5040
    s = s * y + 1.0 / 120
    s = s * y - 1.0 / 6
    s = (s * y + 1.0) * x
    c = 1.0 / 479001600 * y - 1.0 / 3628800
    c = c * y + 1.0 / 40320
    c = c * y - 1.0 / 720
    c = c * y + 1.0 / 24
    c = c * y - 0.5
    c = c * y + 1.0
    return 1.0 - 2.0 * s * s, 2.0 * s * c


def split(x):
    hi = x.astype(BF16)
    return hi, (x - hi.astype(F32)).astype(BF16)


def dot(a, b):
    return jnp.dot(a, b, preferred_element_type=F32)


def dot3(a_hi, a_lo, b_hi, b_lo):
    return dot(a_hi, b_hi) + dot(a_hi, b_lo) + dot(a_lo, b_hi)


def blocks(a, b, c, d):
    return jnp.concatenate(
        [jnp.concatenate([a, b], axis=1), jnp.concatenate([c, d], axis=1)], axis=0
    )


def dft_tables():
    row, col = iota((SIDE, SIDE), 0), iota((SIDE, SIDE), 1)
    c, s = cos_sin(((row * col) & (SIDE - 1)).astype(F32) * (1.0 / SIDE))
    left = split(blocks(c, -s, s, c))
    right = split(blocks(c, s, -s, c))
    twist = cos_sin((row * col).astype(F32) * (1.0 / TIME_SLOTS))
    return left, right, twist


def prefix_tables():
    row, col = iota((SIDE, SIDE), 0), iota((SIDE, SIDE), 1)
    upper = jnp.where(row < col, 1.0, 0.0).astype(F32)
    ones = jnp.ones((SIDE, SIDE), F32)
    lower = jnp.where(col < row, 1.0, 0.0).astype(F32)
    inner = blocks(upper, ones, upper, ones).astype(BF16)
    outer = jnp.concatenate([lower, lower], axis=1).astype(BF16)
    return inner, outer


def as_column(near, far):
    rows = jnp.concatenate([near, far] * BEAMS, axis=0)
    row, col = iota((SIDE, SIDE), 0), iota((SIDE, SIDE), 1)
    return jnp.sum(jnp.where((row >> 4) == col, rows, 0.0), axis=1, keepdims=True)


def as_row(column):
    row, col = iota((SIDE, SIDE), 0), iota((SIDE, SIDE), 1)
    wide = jnp.broadcast_to(column, (SIDE, SIDE))
    return jnp.sum(jnp.where(row == col, wide, 0.0), axis=0, keepdims=True)


def phase_tables(near, far):
    delay, frac, amp = [as_column(n, f) for n, f in zip(near, far)]
    row, col = iota((SIDE, SIDE), 0), iota((SIDE, SIDE), 1)
    whole = (col * delay.astype(jnp.int32)) & (TIME_SLOTS - 1)
    inner_c, inner_s = cos_sin((whole.astype(F32) + col.astype(F32) * frac) * (1.0 / TIME_SLOTS))
    inner_c, inner_s = inner_c * amp, inner_s * amp
    near_row = (row & SLOTS) == 0
    parts = []
    for x in (inner_c, inner_s):
        parts.append(
            jnp.concatenate([jnp.where(near_row, x, 0.0), jnp.where(near_row, 0.0, x)], axis=1)
        )
    right = split(jnp.concatenate(parts, axis=0))
    signed = row - jnp.where(row >= SIDE // 2, SIDE, 0)
    whole = (signed * as_row(delay).astype(jnp.int32)) & (SIDE - 1)
    outer_c, outer_s = cos_sin((whole.astype(F32) + signed.astype(F32) * as_row(frac)) * (1.0 / SIDE))
    left = split(blocks(outer_c, -outer_s, -outer_s, -outer_c))
    return left, right


def spectrum(left, right, beam):
    mine = ((iota((2 * SIDE, 2 * SIDE), 0) & (SIDE - 1)) >> 4) == beam
    hi, lo = [jnp.where(mine, x.astype(F32), 0.0).astype(BF16) for x in right]
    return dot3(left[0], left[1], hi, lo)


def light_of(spec, pulse_real, pulse_imag, left, right, twist):
    spec_real, spec_imag = spec[:SIDE], spec[SIDE:]
    wide_real = jnp.concatenate([pulse_real, pulse_real], axis=1)
    wide_imag = jnp.concatenate([pulse_imag, pulse_imag], axis=1)
    filt = jnp.concatenate(
        [wide_real * spec_real - wide_imag * spec_imag, wide_real * spec_imag + wide_imag * spec_real],
        axis=0,
    )
    section = dot3(left[0], left[1], *split(filt))
    rows = []
    for trip in range(2):
        real = section[:SIDE, trip * SIDE : (trip + 1) * SIDE]
        imag = section[SIDE:, trip * SIDE : (trip + 1) * SIDE]
        rows.append(
            jnp.concatenate(
                [real * twist[0] - imag * twist[1], real * twist[1] + imag * twist[0]], axis=1
            )
        )
    hi, lo = split(jnp.concatenate(rows, axis=0))
    field = dot(hi, right[0]) + dot(hi, right[1]) + dot(lo, right[0])
    power = field * field
    power = power[:SIDE] + power[SIDE:]
    return power[:, :SIDE] + power[:, SIDE:]


def pile_up(power, ambient, inner, outer):
    flux = (power * (1.0 / TIME_SLOTS) + ambient) * (1.0 / TIME_SLOTS)
    flux = jnp.transpose(flux)
    hi, lo = split(flux)
    sums = dot(jnp.concatenate([hi, lo], axis=1), inner)
    within, totals = sums[:, :SIDE], sums[:, SIDE:]
    hi, lo = split(totals)
    before = within + dot(outer, jnp.concatenate([hi, lo], axis=0))
    series = 1.0 - flux * (1.0 / 6)
    for k in (5, 4, 3, 2):
        series = 1.0 - flux * (1.0 / k) * series
    detected = jnp.where(flux < 0.1, flux * series, 1.0 - jnp.exp(-flux))
    return TIME_SLOTS * detected * jnp.exp(-before)


def kernel(
    lag_hbm, frac_hbm, amp_hbm, offset_hbm, count_hbm, ambient_hbm, pulse_hbm,
    out_ref,
    lag_ref, frac_ref, amp_ref, offset_ref, count_ref, ambient_ref, pulse_ref,
    gathered, echo_out, echo_in, spec, left_tab, right_tab, twist_tab, inner_tab, outer_tab,
    ready, arrived,
    in_sem, first_send, first_recv, second_send, second_recv, echo_send, echo_recv,
    hist_send, hist_recv, go_sem,
):
    me_range, me_az = lax.axis_index("range"), lax.axis_index("az")
    y, x = me_az // SIDE_AZ, lax.rem(me_az, SIDE_AZ)
    chief = GROUP - 1

    def row_peer(k):
        return y * SIDE_AZ + lax.rem(x + k, SIDE_AZ)

    def column_peer(k):
        return lax.rem(y + k, SIDE_AZ) * SIDE_AZ + x

    def remote(src, dst, send, recv, **where):
        return pltpu.make_async_remote_copy(
            src_ref=src, dst_ref=dst, send_sem=send, recv_sem=recv, device_id=where, device_id_type=MESH
        )

    fetches = [
        pltpu.make_async_copy(src, dst, in_sem.at[i])
        for i, (src, dst) in enumerate(
            (
                (pulse_hbm, pulse_ref), (lag_hbm, lag_ref), (frac_hbm, frac_ref), (amp_hbm, amp_ref),
                (offset_hbm, offset_ref), (count_hbm, count_ref), (ambient_hbm, ambient_ref),
            )
        )
    ]
    for fetch in fetches:
        fetch.start()

    barrier = pltpu.get_barrier_semaphore()
    for k in range(1, SIDE_AZ):
        for peer in (row_peer(k), column_peer(k)):
            pl.semaphore_signal(barrier, inc=1, device_id={"az": peer}, device_id_type=MESH)
    pl.semaphore_signal(
        barrier, inc=1, device_id={"az": lax.rem(me_az + GROUP - 1, GROUP)}, device_id_type=MESH
    )

    @pl.when(me_range != chief)
    def _():
        pl.semaphore_signal(barrier, inc=1, device_id={"range": chief}, device_id_type=MESH)

    fetches[0].wait()
    for b in range(BEAMS):
        for part in range(2):
            for q in range(8):
                gathered[y, x, b, part, q : q + 1, :] = pulse_ref[
                    b, part : part + 1, q * SIDE : (q + 1) * SIDE
                ]
    for fetch in fetches[1:]:
        fetch.wait()
    back = lax.rem(SIDE - me_range * BEAMS, SIDE)
    delay = (lag_ref[0] + offset_ref[0]).astype(F32)
    live = iota((SLOTS, SIDE), 0) < count_ref[0]
    near_trip = delay < TIME_SLOTS
    amp = amp_ref[0]
    near_amp = jnp.where(live & near_trip, amp, 0.0)
    far_amp = jnp.where(live & jnp.logical_not(near_trip), amp, 0.0)
    delay, frac, near_amp, far_amp = [
        pltpu.roll(v, back, 1) for v in (delay, frac_ref[0], near_amp, far_amp)
    ]
    echo_out[0] = delay
    echo_out[1] = frac
    echo_out[2] = far_amp

    @pl.when(me_range == chief)
    def _():
        pl.semaphore_wait(barrier, 2 * SIDE_AZ - 1 + GROUP - 1)

    @pl.when(me_range != chief)
    def _():
        pl.semaphore_wait(barrier, 2 * SIDE_AZ - 1)

    echo_copy = remote(echo_out, echo_in, echo_send, echo_recv, az=lax.rem(me_az + 1, GROUP))
    echo_copy.start()

    def first_step(pair, carry):
        b = 2 * pair
        for k in (1, 3, 2):
            mine = gathered.at[y, x, b]
            remote(mine, mine, first_send, first_recv.at[b], az=row_peer(k)).start()
            mine = gathered.at[y, x, b + 1]
            remote(mine, mine, first_send, first_recv.at[b + 1], az=column_peer(k)).start()
        return carry

    lax.fori_loop(0, BEAMS // 2, first_step, 0)

    @pl.when(me_range == chief)
    def _():
        def tell(k, carry):
            pl.semaphore_signal(go_sem, inc=1, device_id={"range": k}, device_id_type=MESH)
            return carry

        lax.fori_loop(0, GROUP - 1, tell, 0)

    left, right, twist = dft_tables()
    for i in range(2):
        left_tab[i] = left[i]
        right_tab[i] = right[i]
        twist_tab[i] = twist[i]
    inner_tab[...], outer_tab[...] = prefix_tables()

    def second_step(pair, carry):
        b = 2 * pair
        for j in range(2):
            three = gathered.at[0, pl.ds(0, SIDE_AZ - 1), b + j]
            remote(three, three, first_send, first_recv.at[b + j], az=me_az).wait_recv()
        for k in (1, 3, 2):
            row = gathered.at[y, :, b]
            remote(row, row, second_send, second_recv.at[b], az=column_peer(k)).start()
            column = gathered.at[:, x, b + 1]
            remote(column, column, second_send, second_recv.at[b + 1], az=row_peer(k)).start()
        return carry

    lax.fori_loop(0, BEAMS // 2, second_step, 0)

    echo_copy.wait_recv()
    far = tuple(echo_in[i] for i in range(3))
    echo_left, echo_right = phase_tables((delay, frac, near_amp), far)
    for b in range(BEAMS):
        spec[b] = spectrum(echo_left, echo_right, b)

    def send_tiles(peer, first_beam, count):
        here = pl.ds(pl.multiple_of((me_range * BEAMS + first_beam) * 8, 8), count * 8)
        there = pl.ds(pl.multiple_of((peer * BEAMS + first_beam) * 8, 8), count * 8)

        @pl.when(peer != me_range)
        def _():
            remote(ready.at[there], arrived.at[here], hist_send, hist_recv, range=peer).start()

    def work(pair, carry):
        for j in range(2):
            b = 2 * pair + j
            twelve = gathered.at[pl.ds(0, SIDE_AZ - 1), :, b]
            remote(twelve, twelve, second_send, second_recv.at[b], az=me_az).wait_recv()
        for j in range(2):
            b = 2 * pair + j
            pulse_real = gathered[:, :, b, 0].reshape(SIDE, SIDE)
            pulse_imag = gathered[:, :, b, 1].reshape(SIDE, SIDE)
            power = light_of(
                spec[b], pulse_real, pulse_imag,
                (left_tab[0], left_tab[1]), (right_tab[0], right_tab[1]), (twist_tab[0], twist_tab[1]),
            )
            mine = iota((1, SIDE), 1) == me_range * BEAMS + b
            ambient = jnp.sum(jnp.where(mine, ambient_ref[...], 0.0), axis=1, keepdims=True)
            hist = pile_up(power, ambient, inner_tab[...], outer_tab[...])
            for g in range(GROUP):
                ready[pl.ds(pl.multiple_of((g * BEAMS + b) * 8, 8), 8), :] = hist[g * 8 : (g + 1) * 8]

        @pl.when((pair == 0) & (me_range != chief))
        def _():
            pl.semaphore_wait(go_sem, 1)

        def send(peer, carry):
            send_tiles(peer, 2 * pair, 2)
            return carry

        lax.fori_loop(0, GROUP // 2, send, 0)
        return carry

    lax.fori_loop(0, BEAMS // 2, work, 0)

    def send_late(peer, carry):
        send_tiles(peer, 0, BEAMS)
        return carry

    lax.fori_loop(GROUP // 2, GROUP, send_late, 0)
    own = pl.ds(pl.multiple_of(me_range * BEAMS * 8, 8), BEAMS * 8)
    arrived[own, :] = ready[own, :]

    most = pl.ds(0, (GROUP - 1) * BEAMS * 8)
    done = remote(ready.at[most], arrived.at[most], hist_send, hist_recv, az=me_az)
    done.wait_recv()
    for g in range(GROUP):
        for s in range(8):
            out_ref[0, g * 8 : (g + 1) * 8, s * SIDE : (s + 1) * SIDE] = arrived[
                pl.ds(g * 64 + s, 8, stride=8), :
            ]
    done.wait_send()
    echo_copy.wait_send()
    three = gathered.at[0, pl.ds(0, SIDE_AZ - 1)]
    remote(three, three, first_send, first_recv.at[0], az=me_az).wait_send()
    twelve = gathered.at[pl.ds(0, SIDE_AZ - 1)]
    remote(twelve, twelve, second_send, second_recv.at[0], az=me_az).wait_send()


def per_device(lag, frac, amp, offset, count, ambient, pulse):
    lag, frac, amp = [jnp.swapaxes(v, 1, 2) for v in (lag, frac, amp)]
    hbm = pl.BlockSpec(memory_space=pltpu.HBM)
    dma = pltpu.SemaphoreType.DMA
    return pl.pallas_call(
        kernel,
        out_shape=jax.ShapeDtypeStruct((1, GROUP * BEAMS, TIME_SLOTS // GROUP), F32),
        in_specs=[hbm] * 7,
        out_specs=pl.BlockSpec(memory_space=pltpu.VMEM),
        scratch_shapes=[
            pltpu.VMEM((1, SLOTS, SIDE), jnp.int32),
            pltpu.VMEM((1, SLOTS, SIDE), F32),
            pltpu.VMEM((1, SLOTS, SIDE), F32),
            pltpu.SMEM((1,), jnp.int32),
            pltpu.SMEM((1,), jnp.int32),
            pltpu.VMEM((1, SIDE), F32),
            pltpu.VMEM((BEAMS, 2, TIME_SLOTS // GROUP), F32),
            pltpu.VMEM((SIDE_AZ, SIDE_AZ, BEAMS, 2, 8, SIDE), F32),
            pltpu.VMEM((3, SLOTS, SIDE), F32),
            pltpu.VMEM((3, SLOTS, SIDE), F32),
            pltpu.VMEM((BEAMS, 2 * SIDE, 2 * SIDE), F32),
            pltpu.VMEM((2, 2 * SIDE, 2 * SIDE), BF16),
            pltpu.VMEM((2, 2 * SIDE, 2 * SIDE), BF16),
            pltpu.VMEM((2, SIDE, SIDE), F32),
            pltpu.VMEM((2 * SIDE, 2 * SIDE), BF16),
            pltpu.VMEM((SIDE, 2 * SIDE), BF16),
            pltpu.VMEM((GROUP * BEAMS * 8, SIDE), F32),
            pltpu.VMEM((GROUP * BEAMS * 8, SIDE), F32),
            dma((7,)), dma, dma((BEAMS,)), dma, dma((BEAMS,)), dma, dma, dma, dma,
            pltpu.SemaphoreType.REGULAR,
        ],
        compiler_params=pltpu.CompilerParams(
            collective_id=0, has_side_effects=True, vmem_limit_bytes=40 * 1024 * 1024
        ),
    )(lag, frac, amp, offset, count, ambient.reshape(1, SIDE), pulse)


def solution(mesh):
    in_specs = (
        P("az", None, None),
        P("az", None, None),
        P("az", None, None),
        P("az"),
        P("az"),
        P(),
        P("range", None, "az"),
    )
    out_specs = P("az", None, "range")
    return jax.shard_map(
        per_device, mesh=mesh, in_specs=in_specs, out_specs=out_specs, check_vma=False
    )
```

```python
import math

import jax
import jax.numpy as jnp
from jax import lax
from jax.experimental import pallas as pl
from jax.experimental.pallas import tpu as pltpu
from jax.sharding import PartitionSpec as P

TIME_SLOTS = 16384
SIDE = 128
BEAMS = 8
SLOTS = 8
GROUP = 16
HALF = 8
EXTRA = 4
TOGETHER = 4
ALL = BEAMS + EXTRA
EARLY_ORDER = (1, 0, 7, 6, 3, 2, 5, 4)
SIDE_AZ = 4
MESH = pl.DeviceIdType.MESH
F32 = jnp.float32
BF16 = jnp.bfloat16


def iota(shape, dim):
    return lax.broadcasted_iota(jnp.int32, shape, dim)


def cos_sin(turns):
    x = (turns - jnp.round(turns)) * math.pi
    y = x * x
    s = -1.0 / 39916800 * y + 1.0 / 362880
    s = s * y - 1.0 / 5040
    s = s * y + 1.0 / 120
    s = s * y - 1.0 / 6
    s = (s * y + 1.0) * x
    c = 1.0 / 479001600 * y - 1.0 / 3628800
    c = c * y + 1.0 / 40320
    c = c * y - 1.0 / 720
    c = c * y + 1.0 / 24
    c = c * y - 0.5
    c = c * y + 1.0
    return 1.0 - 2.0 * s * s, 2.0 * s * c


def split(x):
    hi = x.astype(BF16)
    return hi, (x - hi.astype(F32)).astype(BF16)


def dot(a, b):
    return jnp.dot(a, b, preferred_element_type=F32)


def dot3(a_hi, a_lo, b_hi, b_lo):
    return dot(a_hi, b_hi) + dot(a_hi, b_lo) + dot(a_lo, b_hi)


def blocks(a, b, c, d):
    return jnp.concatenate(
        [jnp.concatenate([a, b], axis=1), jnp.concatenate([c, d], axis=1)], axis=0
    )


def dft_tables():
    row, col = iota((SIDE, SIDE), 0), iota((SIDE, SIDE), 1)
    c, s = cos_sin(((row * col) & (SIDE - 1)).astype(F32) * (1.0 / SIDE))
    left = split(blocks(c, -s, s, c))
    right = split(blocks(c, s, -s, c))
    twist = cos_sin((row * col).astype(F32) * (1.0 / TIME_SLOTS))
    return left, right, twist


def prefix_tables():
    row, col = iota((SIDE, SIDE), 0), iota((SIDE, SIDE), 1)
    upper = jnp.where(row < col, 1.0, 0.0).astype(F32)
    ones = jnp.ones((SIDE, SIDE), F32)
    lower = jnp.where(col < row, 1.0, 0.0).astype(F32)
    inner = blocks(upper, ones, upper, ones).astype(BF16)
    outer = jnp.concatenate([lower, lower], axis=1).astype(BF16)
    return inner, outer


def as_column(near, far, shift):
    rows = jnp.concatenate([near, far] * BEAMS, axis=0)
    row, col = iota((SIDE, SIDE), 0), iota((SIDE, SIDE), 1)
    return jnp.sum(jnp.where((row >> 4) + shift == col, rows, 0.0), axis=1, keepdims=True)


def as_row(column):
    row, col = iota((SIDE, SIDE), 0), iota((SIDE, SIDE), 1)
    wide = jnp.broadcast_to(column, (SIDE, SIDE))
    return jnp.sum(jnp.where(row == col, wide, 0.0), axis=0, keepdims=True)


def phase_tables(near, far, shift=0):
    delay, frac, amp = [as_column(n, f, shift) for n, f in zip(near, far)]
    row, col = iota((SIDE, SIDE), 0), iota((SIDE, SIDE), 1)
    whole = (col * delay.astype(jnp.int32)) & (TIME_SLOTS - 1)
    inner_c, inner_s = cos_sin((whole.astype(F32) + col.astype(F32) * frac) * (1.0 / TIME_SLOTS))
    inner_c, inner_s = inner_c * amp, inner_s * amp
    near_row = (row & SLOTS) == 0
    parts = []
    for x in (inner_c, inner_s):
        parts.append(
            jnp.concatenate([jnp.where(near_row, x, 0.0), jnp.where(near_row, 0.0, x)], axis=1)
        )
    right = split(jnp.concatenate(parts, axis=0))
    signed = row - jnp.where(row >= SIDE // 2, SIDE, 0)
    whole = (signed * as_row(delay).astype(jnp.int32)) & (SIDE - 1)
    outer_c, outer_s = cos_sin((whole.astype(F32) + signed.astype(F32) * as_row(frac)) * (1.0 / SIDE))
    left = split(blocks(outer_c, -outer_s, -outer_s, -outer_c))
    return left, right


def spectrum(left, right, beam):
    mine = ((iota((2 * SIDE, 2 * SIDE), 0) & (SIDE - 1)) >> 4) == beam
    hi, lo = [jnp.where(mine, x.astype(F32), 0.0).astype(BF16) for x in right]
    return dot3(left[0], left[1], hi, lo)


def side_by_side(*parts):
    return jnp.concatenate(parts, axis=1)


def stacked(*parts):
    return jnp.concatenate(parts, axis=0)


def group_histogram(specs, pulses, ambients, left, right, twist, inner, outer):
    count = len(specs)
    rows = []
    for spec, (pulse_real, pulse_imag) in zip(specs, pulses):
        real, imag = spec[:SIDE], spec[SIDE:]
        wide_real, wide_imag = side_by_side(pulse_real, pulse_real), side_by_side(pulse_imag, pulse_imag)
        hi, lo = split(stacked(wide_real * real - wide_imag * imag, wide_real * imag + wide_imag * real))
        section = dot(left, stacked(hi, lo, hi))
        for trip in range(2):
            real = section[:SIDE, trip * SIDE : (trip + 1) * SIDE]
            imag = section[SIDE:, trip * SIDE : (trip + 1) * SIDE]
            rows.append(side_by_side(real * twist[0] - imag * twist[1], real * twist[1] + imag * twist[0]))
    hi, lo = split(stacked(*rows))
    field = dot(side_by_side(hi, lo, hi), right)
    fluxes = []
    for j in range(count):
        power = field[2 * SIDE * j : 2 * SIDE * (j + 1)]
        power = power * power
        power = power[:SIDE] + power[SIDE:]
        power = power[:, :SIDE] + power[:, SIDE:]
        fluxes.append(jnp.transpose((power * (1.0 / TIME_SLOTS) + ambients[j]) * (1.0 / TIME_SLOTS)))
    flux = stacked(*fluxes)
    hi, lo = split(flux)
    sums = dot(side_by_side(hi, lo), inner)
    hi, lo = split(side_by_side(*[sums[SIDE * j : SIDE * (j + 1), SIDE:] for j in range(count)]))
    carried = dot(outer, stacked(hi, lo))
    before = stacked(
        *[sums[SIDE * j : SIDE * (j + 1), :SIDE] + carried[:, SIDE * j : SIDE * (j + 1)] for j in range(count)]
    )
    series = 1.0 - flux * 0.25
    series = 1.0 - flux * (1.0 / 3) * series
    series = 1.0 - flux * 0.5 * series
    detected = jnp.where(flux < 1.0 / 32, flux * series, 1.0 - jnp.exp(-flux))
    return TIME_SLOTS * detected * jnp.exp(-before)


def kernel(
    lag_hbm, frac_hbm, amp_hbm, packed_hbm, ambient_hbm, pulse_hbm,
    out_ref,
    lag_ref, frac_ref, amp_ref, packed_ref, ambient_ref, pulse_ref,
    gathered, echo_out, echo_in, spec, left_tab, right_tab, twist_tab, inner_tab, outer_tab,
    ready, arrived,
    in_sem, shard_send, shard_recv, first_send, first_recv, second_send, second_recv, echo_send, echo_recv,
    hist_send, hist_recv, go_sem,
):
    me_range, me_az = lax.axis_index("range"), lax.axis_index("az")
    y, x = me_az // SIDE_AZ, lax.rem(me_az, SIDE_AZ)
    chief = GROUP - 1
    early = me_range < HALF
    late = jnp.logical_not(early)
    partner = lax.rem(me_range + HALF, GROUP)

    def row_peer(k):
        return y * SIDE_AZ + lax.rem(x + k, SIDE_AZ)

    def column_peer(k):
        return lax.rem(y + k, SIDE_AZ) * SIDE_AZ + x

    def remote(src, dst, send, recv, **where):
        return pltpu.make_async_remote_copy(
            src_ref=src, dst_ref=dst, send_sem=send, recv_sem=recv, device_id=where, device_id_type=MESH
        )

    fetches = [
        pltpu.make_async_copy(src, dst, in_sem.at[i])
        for i, (src, dst) in enumerate(
            (
                (pulse_hbm, pulse_ref), (lag_hbm, lag_ref), (frac_hbm, frac_ref), (amp_hbm, amp_ref),
                (packed_hbm, packed_ref), (ambient_hbm, ambient_ref),
            )
        )
    ]
    for fetch in fetches:
        fetch.start()

    barrier = pltpu.get_barrier_semaphore()
    for k in range(1, SIDE_AZ):
        for peer in (row_peer(k), column_peer(k)):
            pl.semaphore_signal(barrier, inc=1, device_id={"az": peer}, device_id_type=MESH)
    pl.semaphore_signal(
        barrier, inc=1, device_id={"az": lax.rem(me_az + GROUP - 1, GROUP)}, device_id_type=MESH
    )

    @pl.when(me_range != chief)
    def _():
        pl.semaphore_signal(barrier, inc=1, device_id={"range": chief}, device_id_type=MESH)

    @pl.when(early)
    def _():
        pl.semaphore_signal(barrier, inc=1, device_id={"range": partner}, device_id_type=MESH)

    fetches[0].wait()
    for b in range(BEAMS):
        for part in range(2):
            for q in range(8):
                gathered[y, x, b, part, q : q + 1, :] = pulse_ref[
                    b, part : part + 1, q * SIDE : (q + 1) * SIDE
                ]
    for fetch in fetches[1:]:
        fetch.wait()
    back = lax.rem(SIDE - me_range * BEAMS, SIDE)
    delay = (lag_ref[0] + (packed_ref[...] >> 4)).astype(F32)
    live = iota((SLOTS, SIDE), 0) < (packed_ref[...] & 15)
    near_trip = delay < TIME_SLOTS
    amp = amp_ref[0]
    near_amp = jnp.where(live & near_trip, amp, 0.0)
    far_amp = jnp.where(live & jnp.logical_not(near_trip), amp, 0.0)
    delay, frac, near_amp, far_amp = [
        pltpu.roll(v, back, 1) for v in (delay, frac_ref[0], near_amp, far_amp)
    ]
    echo_out[0] = delay
    echo_out[1] = frac
    echo_out[2] = far_amp
    echo_out[3] = near_amp

    greeted = 2 * SIDE_AZ - 1
    pl.semaphore_wait(
        barrier,
        greeted + jnp.where(early, 0, 1) + jnp.where(me_range == chief, GROUP - 1, 0),
    )

    shard = remote(
        gathered.at[y, x, pl.ds(BEAMS - EXTRA, EXTRA)], gathered.at[y, x, pl.ds(BEAMS, EXTRA)],
        shard_send, shard_recv, range=partner,
    )
    pl.when(late)(shard.start)

    echo_copy = remote(
        echo_out.at[pl.ds(0, 3)], echo_in, echo_send, echo_recv, az=lax.rem(me_az + 1, GROUP)
    )
    echo_copy.start()

    def first_step(pair, carry):
        b = 2 * pair
        for k in (1, 3, 2):
            mine = gathered.at[y, x, b]
            remote(mine, mine, first_send, first_recv.at[b], az=row_peer(k)).start()
            mine = gathered.at[y, x, b + 1]
            remote(mine, mine, first_send, first_recv.at[b + 1], az=column_peer(k)).start()
        return carry

    lax.fori_loop(0, BEAMS // 2, first_step, 0)

    @pl.when(me_range == chief)
    def _():
        def tell(k, carry):
            pl.semaphore_signal(go_sem, inc=1, device_id={"range": k}, device_id_type=MESH)
            return carry

        lax.fori_loop(0, GROUP - 1, tell, 0)

    left, right, twist = dft_tables()
    left_tab[...] = side_by_side(left[0], left[0], left[1])
    right_tab[...] = stacked(right[0], right[0], right[1])
    twist_tab[0], twist_tab[1] = twist
    inner_tab[...], outer_tab[...] = prefix_tables()

    def second_step(pair, carry):
        b = 2 * pair
        for j in range(2):
            three = gathered.at[0, pl.ds(0, SIDE_AZ - 1), b + j]
            remote(three, three, first_send, first_recv.at[b + j], az=me_az).wait_recv()
        for k in (1, 3, 2):
            row = gathered.at[y, :, b]
            remote(row, row, second_send, second_recv.at[b], az=column_peer(k)).start()
            column = gathered.at[:, x, b + 1]
            remote(column, column, second_send, second_recv.at[b + 1], az=row_peer(k)).start()
        return carry

    lax.fori_loop(0, BEAMS // 2, second_step, 0)

    echo_copy.wait_recv()

    def spectra(shift, beams, place):
        near = (echo_out[0], echo_out[1], echo_out[3])
        far = (echo_in[0], echo_in[1], echo_in[2])
        echo_left, echo_right = phase_tables(near, far, shift)
        for i, b in enumerate(beams):
            spec[place + i] = spectrum(echo_left, echo_right, b)

    spectra(0, range(BEAMS), 0)

    @pl.when(early)
    def _():
        spectra(HALF * BEAMS, range(BEAMS - EXTRA, BEAMS), BEAMS)

    def tiles_of(row, count):
        return pl.ds(pl.multiple_of(row * 8, 8), count * 8)

    def tiles(ref, row, count):
        return ref.at[tiles_of(row, count)]

    def send_tiles(peer, b, row, count):
        @pl.when(peer != me_range)
        def _():
            remote(
                tiles(ready, peer * ALL + b, count), tiles(arrived, row, count),
                hist_send, hist_recv, range=peer,
            ).start()

    def work(group, carry):
        b0 = group * TOGETHER
        own = group * TOGETHER < BEAMS
        row = me_range * BEAMS + jnp.where(own, b0, b0 - EXTRA + HALF * BEAMS)
        specs, pulses, ambients = [], [], []
        for j in range(TOGETHER):
            twelve = gathered.at[pl.ds(0, SIDE_AZ - 1), :, b0 + j]
            remote(twelve, twelve, second_send, second_recv.at[b0 + j], az=me_az).wait_recv()
        for j in range(TOGETHER):
            specs.append(spec[b0 + j])
            pulses.append([gathered[:, :, b0 + j, part].reshape(SIDE, SIDE) for part in range(2)])
            mine = iota((1, SIDE), 1) == row + j
            ambients.append(jnp.sum(jnp.where(mine, ambient_ref[...], 0.0), axis=1, keepdims=True))
        hist = group_histogram(
            specs, pulses, ambients, left_tab[...], right_tab[...], (twist_tab[0], twist_tab[1]),
            inner_tab[...], outer_tab[...],
        )
        for j in range(TOGETHER):
            for g in range(GROUP):
                ready[pl.ds(pl.multiple_of((g * ALL + b0 + j) * 8, 8), 8), :] = hist[
                    j * SIDE + g * 8 : j * SIDE + (g + 1) * 8
                ]

        @pl.when((group == 0) & (me_range != chief))
        def _():
            pl.semaphore_wait(go_sem, 1)

        @pl.when(early | (b0 < BEAMS - EXTRA))
        def _():
            for peer in EARLY_ORDER:
                send_tiles(peer, b0, row, TOGETHER)

        @pl.when(b0 == BEAMS - TOGETHER)
        def _():
            def send(peer, carry):
                send_tiles(peer, 0, me_range * BEAMS, BEAMS)
                return carry

            lax.fori_loop(HALF, GROUP, send, 0)

        @pl.when(early & (group == 0))
        def _():
            shard.wait_recv()
            lax.fori_loop(BEAMS // 2, ALL // 2, first_step, 0)

        @pl.when(early & (group == 1))
        def _():
            lax.fori_loop(BEAMS // 2, ALL // 2, second_step, 0)

        return carry

    lax.fori_loop(0, jnp.where(early, ALL // TOGETHER, BEAMS // TOGETHER), work, 0)

    arrived[tiles_of(me_range * BEAMS, BEAMS), :] = ready[tiles_of(me_range * ALL, BEAMS), :]

    @pl.when(early)
    def _():
        arrived[tiles_of(partner * BEAMS + BEAMS - EXTRA, EXTRA), :] = ready[
            tiles_of(me_range * ALL + BEAMS, EXTRA), :
        ]

    def settled(ref, send, recv, count):
        some = tiles(ref, 0, count)
        return remote(some, some, send, recv, az=me_az)

    @pl.when(early)
    def _():
        settled(arrived, hist_send, hist_recv, GROUP * BEAMS - ALL).wait_recv()

    @pl.when(late)
    def _():
        settled(arrived, hist_send, hist_recv, GROUP * BEAMS - BEAMS).wait_recv()

    for g in range(GROUP):
        for s in range(8):
            out_ref[0, g * 8 : (g + 1) * 8, s * SIDE : (s + 1) * SIDE] = arrived[
                pl.ds(g * 64 + s, 8, stride=8), :
            ]
    @pl.when(early)
    def _():
        settled(ready, hist_send, hist_recv, (GROUP - 1) * BEAMS + (HALF - 1) * EXTRA).wait_send()

    @pl.when(late)
    def _():
        settled(ready, hist_send, hist_recv, (GROUP - 1) * BEAMS - HALF * EXTRA).wait_send()
        shard.wait_send()

    echo_copy.wait_send()

    def sent(beams):
        three = gathered.at[0, pl.ds(0, SIDE_AZ - 1), beams]
        remote(three, three, first_send, first_recv.at[0], az=me_az).wait_send()
        twelve = gathered.at[pl.ds(0, SIDE_AZ - 1), :, beams]
        remote(twelve, twelve, second_send, second_recv.at[0], az=me_az).wait_send()

    sent(pl.ds(0, BEAMS))

    @pl.when(early)
    def _():
        sent(pl.ds(BEAMS, EXTRA))


def per_device(lag, frac, amp, offset, count, ambient, pulse):
    lag, frac, amp = [jnp.swapaxes(v, 1, 2) for v in (lag, frac, amp)]
    hbm = pl.BlockSpec(memory_space=pltpu.HBM)
    dma = pltpu.SemaphoreType.DMA
    return pl.pallas_call(
        kernel,
        out_shape=jax.ShapeDtypeStruct((1, GROUP * BEAMS, TIME_SLOTS // GROUP), F32),
        in_specs=[hbm] * 6,
        out_specs=pl.BlockSpec(memory_space=pltpu.VMEM),
        scratch_shapes=[
            pltpu.VMEM((1, SLOTS, SIDE), jnp.int32),
            pltpu.VMEM((1, SLOTS, SIDE), F32),
            pltpu.VMEM((1, SLOTS, SIDE), F32),
            pltpu.VMEM((1, 1), jnp.int32),
            pltpu.VMEM((1, SIDE), F32),
            pltpu.VMEM((BEAMS, 2, TIME_SLOTS // GROUP), F32),
            pltpu.VMEM((SIDE_AZ, SIDE_AZ, ALL, 2, 8, SIDE), F32),
            pltpu.VMEM((4, SLOTS, SIDE), F32),
            pltpu.VMEM((3, SLOTS, SIDE), F32),
            pltpu.VMEM((ALL, 2 * SIDE, 2 * SIDE), F32),
            pltpu.VMEM((2 * SIDE, 6 * SIDE), BF16),
            pltpu.VMEM((6 * SIDE, 2 * SIDE), BF16),
            pltpu.VMEM((2, SIDE, SIDE), F32),
            pltpu.VMEM((2 * SIDE, 2 * SIDE), BF16),
            pltpu.VMEM((SIDE, 2 * SIDE), BF16),
            pltpu.VMEM((GROUP * ALL * 8, SIDE), F32),
            pltpu.VMEM((GROUP * BEAMS * 8, SIDE), F32),
            dma((6,)), dma, dma, dma, dma((ALL,)), dma, dma((ALL,)), dma, dma, dma, dma,
            pltpu.SemaphoreType.REGULAR,
        ],
        compiler_params=pltpu.CompilerParams(
            collective_id=0, has_side_effects=True, vmem_limit_bytes=40 * 1024 * 1024
        ),
    )(lag, frac, amp, (offset * 16 + count).reshape(1, 1), ambient.reshape(1, SIDE), pulse)


def solution(mesh):
    in_specs = (
        P("az", None, None),
        P("az", None, None),
        P("az", None, None),
        P("az"),
        P("az"),
        P(),
        P("range", None, "az"),
    )
    out_specs = P("az", None, "range")
    return jax.shard_map(
        per_device, mesh=mesh, in_specs=in_specs, out_specs=out_specs, check_vma=False
    )
```

```python
import math

import jax
import jax.numpy as jnp
from jax import lax
from jax.experimental import pallas as pl
from jax.experimental.pallas import tpu as pltpu
from jax.sharding import PartitionSpec as P

TIME_SLOTS = 16384
SIDE = 128
BEAMS = 8
SLOTS = 8
GROUP = 16
EARLY_ORDER = (1, 0, 7, 6, 3, 2, 5, 4)
LATE_ORDER = (8, 9, 14, 15, 10, 11, 12, 13)
SIDE_AZ = 4
MESH = pl.DeviceIdType.MESH
F32 = jnp.float32
BF16 = jnp.bfloat16


def iota(shape, dim):
    return lax.broadcasted_iota(jnp.int32, shape, dim)


def cos_sin(turns):
    x = (turns - jnp.round(turns)) * math.pi
    y = x * x
    s = -1.0 / 39916800 * y + 1.0 / 362880
    s = s * y - 1.0 / 5040
    s = s * y + 1.0 / 120
    s = s * y - 1.0 / 6
    s = (s * y + 1.0) * x
    c = 1.0 / 479001600 * y - 1.0 / 3628800
    c = c * y + 1.0 / 40320
    c = c * y - 1.0 / 720
    c = c * y + 1.0 / 24
    c = c * y - 0.5
    c = c * y + 1.0
    return 1.0 - 2.0 * s * s, 2.0 * s * c


def split(x):
    hi = x.astype(BF16)
    return hi, (x - hi.astype(F32)).astype(BF16)


def dot(a, b):
    return jnp.dot(a, b, preferred_element_type=F32)


def dot3(a_hi, a_lo, b_hi, b_lo):
    return dot(a_hi, b_hi) + dot(a_hi, b_lo) + dot(a_lo, b_hi)


def blocks(a, b, c, d):
    return jnp.concatenate(
        [jnp.concatenate([a, b], axis=1), jnp.concatenate([c, d], axis=1)], axis=0
    )


def dft_tables():
    row, col = iota((SIDE, SIDE), 0), iota((SIDE, SIDE), 1)
    c, s = cos_sin(((row * col) & (SIDE - 1)).astype(F32) * (1.0 / SIDE))
    left = split(blocks(c, -s, s, c))
    right = split(blocks(c, s, -s, c))
    twist = cos_sin((row * col).astype(F32) * (1.0 / TIME_SLOTS))
    return left, right, twist


def prefix_tables():
    row, col = iota((SIDE, SIDE), 0), iota((SIDE, SIDE), 1)
    upper = jnp.where(row < col, 1.0, 0.0).astype(F32)
    ones = jnp.ones((SIDE, SIDE), F32)
    lower = jnp.where(col < row, 1.0, 0.0).astype(F32)
    inner = blocks(upper, ones, upper, ones).astype(BF16)
    outer = jnp.concatenate([lower, lower], axis=1).astype(BF16)
    return inner, outer


def as_column(rows, lane):
    return jnp.sum(jnp.where(iota(rows.shape, 1) == lane, rows, 0.0), axis=1, keepdims=True)


def as_row(column):
    row, col = iota((SIDE, SIDE), 0), iota((SIDE, SIDE), 1)
    wide = jnp.broadcast_to(column, (SIDE, SIDE))
    return jnp.sum(jnp.where(row == col, wide, 0.0), axis=0, keepdims=True)


def phase_tables(delay, frac, amp):
    row, col = iota((SIDE, SIDE), 0), iota((SIDE, SIDE), 1)
    whole = (col * delay.astype(jnp.int32)) & (TIME_SLOTS - 1)
    inner_c, inner_s = cos_sin((whole.astype(F32) + col.astype(F32) * frac) * (1.0 / TIME_SLOTS))
    inner_c, inner_s = inner_c * amp, inner_s * amp
    near_row = (row & SLOTS) == 0
    parts = []
    for x in (inner_c, inner_s):
        parts.append(
            jnp.concatenate([jnp.where(near_row, x, 0.0), jnp.where(near_row, 0.0, x)], axis=1)
        )
    right = split(jnp.concatenate(parts, axis=0))
    signed = row - jnp.where(row >= SIDE // 2, SIDE, 0)
    whole = (signed * as_row(delay).astype(jnp.int32)) & (SIDE - 1)
    outer_c, outer_s = cos_sin((whole.astype(F32) + signed.astype(F32) * as_row(frac)) * (1.0 / SIDE))
    left = split(blocks(outer_c, -outer_s, -outer_s, -outer_c))
    return left, right


def spectrum(left, right, beam):
    mine = ((iota((2 * SIDE, 2 * SIDE), 0) & (SIDE - 1)) >> 4) == beam
    hi, lo = [jnp.where(mine, x.astype(F32), 0.0).astype(BF16) for x in right]
    return dot3(left[0], left[1], hi, lo)


def side_by_side(*parts):
    return jnp.concatenate(parts, axis=1)


def stacked(*parts):
    return jnp.concatenate(parts, axis=0)


def group_histogram(specs, pulses, ambients, left, right, twist, inner, outer):
    count = len(specs)
    rows = []
    for spec, (pulse_real, pulse_imag) in zip(specs, pulses):
        real, imag = spec[:SIDE], spec[SIDE:]
        wide_real, wide_imag = side_by_side(pulse_real, pulse_real), side_by_side(pulse_imag, pulse_imag)
        hi, lo = split(stacked(wide_real * real - wide_imag * imag, wide_real * imag + wide_imag * real))
        section = dot(left, stacked(hi, lo, hi))
        for trip in range(2):
            real = section[:SIDE, trip * SIDE : (trip + 1) * SIDE]
            imag = section[SIDE:, trip * SIDE : (trip + 1) * SIDE]
            rows.append(side_by_side(real * twist[0] - imag * twist[1], real * twist[1] + imag * twist[0]))
    hi, lo = split(stacked(*rows))
    field = dot(side_by_side(hi, lo, hi), right)
    fluxes = []
    for j in range(count):
        power = field[2 * SIDE * j : 2 * SIDE * (j + 1)]
        power = power * power
        power = power[:SIDE] + power[SIDE:]
        power = power[:, :SIDE] + power[:, SIDE:]
        fluxes.append(jnp.transpose((power * (1.0 / TIME_SLOTS) + ambients[j]) * (1.0 / TIME_SLOTS)))
    flux = stacked(*fluxes)
    hi, lo = split(flux)
    sums = dot(side_by_side(hi, lo), inner)
    hi, lo = split(side_by_side(*[sums[SIDE * j : SIDE * (j + 1), SIDE:] for j in range(count)]))
    carried = dot(outer, stacked(hi, lo))
    before = stacked(
        *[sums[SIDE * j : SIDE * (j + 1), :SIDE] + carried[:, SIDE * j : SIDE * (j + 1)] for j in range(count)]
    )
    series = 1.0 - flux * 0.25
    series = 1.0 - flux * (1.0 / 3) * series
    series = 1.0 - flux * 0.5 * series
    detected = jnp.where(flux < 1.0 / 32, flux * series, 1.0 - jnp.exp(-flux))
    return TIME_SLOTS * detected * jnp.exp(-before)


def kernel(
    lag_hbm, frac_hbm, amp_hbm, packed_hbm, ambient_hbm, pulse_hbm,
    out_ref,
    lag_ref, frac_ref, amp_ref, packed_ref, ambient_ref, pulse_ref,
    own, gathered, echo_left, echo_right, left_tab, right_tab, twist_tab, inner_tab, outer_tab,
    ready, arrived,
    in_sem, pulse_send, pulse_recv, hist_send, hist_recv, go_sem, near_sem,
):
    me_range, me_az = lax.axis_index("range"), lax.axis_index("az")
    y, x = me_az // SIDE_AZ, lax.rem(me_az, SIDE_AZ)
    chief = GROUP - 1

    def remote(src, dst, send, recv, **where):
        return pltpu.make_async_remote_copy(
            src_ref=src, dst_ref=dst, send_sem=send, recv_sem=recv, device_id=where, device_id_type=MESH
        )

    fetches = [
        pltpu.make_async_copy(src, dst, in_sem.at[i])
        for i, (src, dst) in enumerate(
            (
                (pulse_hbm, pulse_ref), (lag_hbm, lag_ref), (frac_hbm, frac_ref), (amp_hbm, amp_ref),
                (packed_hbm, packed_ref), (ambient_hbm, ambient_ref),
            )
        )
    ]
    for fetch in fetches:
        fetch.start()

    barrier = pltpu.get_barrier_semaphore()

    def greet(k, carry):
        pl.semaphore_signal(
            barrier, inc=1, device_id={"az": lax.rem(me_az + k, GROUP)}, device_id_type=MESH
        )
        return carry

    lax.fori_loop(1, GROUP, greet, 0)

    @pl.when(me_range != chief)
    def _():
        pl.semaphore_signal(barrier, inc=1, device_id={"range": chief}, device_id_type=MESH)

    fetches[0].wait()
    for b in range(BEAMS):
        for part in range(2):
            for q in range(8):
                own[b, part, q : q + 1, :] = pulse_ref[b, part : part + 1, q * SIDE : (q + 1) * SIDE]
    for fetch in fetches[1:]:
        fetch.wait()
    first = me_range * BEAMS
    delay = (lag_ref[0] + (packed_ref[...] >> 4)).astype(F32)
    live = iota((SLOTS, SIDE), 0) < (packed_ref[...] & 15)
    amp = jnp.where(live, amp_ref[0], 0.0)
    delay, frac, amp = [
        pltpu.roll(v, lax.rem(2 * SIDE + BEAMS * i - first, SIDE), 1)
        for i, v in enumerate((delay, frac_ref[0], amp))
    ]
    lane = iota((SLOTS, SIDE), 1)
    echo = jnp.where(lane < BEAMS, delay, jnp.where(lane < 2 * BEAMS, frac, amp))
    for b in range(0, BEAMS, 2):
        own[b, 2] = echo

    pl.semaphore_wait(barrier, GROUP - 1 + jnp.where(me_range == chief, GROUP - 1, 0))

    def share(k, carry):
        peer = lax.rem(me_az + k, GROUP)
        beam = 2 * lax.rem(peer, SIDE_AZ)
        remote(own.at[beam], gathered.at[0, me_az], pulse_send, pulse_recv.at[0], az=peer).start()
        return carry

    def share_next(k, carry):
        peer = lax.rem(me_az + k, GROUP)
        beam = 2 * lax.rem(peer, SIDE_AZ) + 1
        parts = pl.ds(0, 2)
        remote(
            own.at[beam, parts], gathered.at[1, me_az, parts], pulse_send, pulse_recv.at[1], az=peer
        ).start()
        return carry

    lax.fori_loop(1, GROUP, share, 0)
    lax.fori_loop(1, GROUP, share_next, 0)

    @pl.when(me_range == chief)
    def _():
        def tell(k, carry):
            pl.semaphore_signal(go_sem, inc=1, device_id={"range": k}, device_id_type=MESH)
            return carry

        lax.fori_loop(0, GROUP - 1, tell, 0)

    gathered[0, me_az] = own[2 * x]
    gathered[1, me_az] = own[2 * x + 1]

    left, right, twist = dft_tables()
    left_tab[...] = side_by_side(left[0], left[0], left[1])
    right_tab[...] = stacked(right[0], right[0], right[1])
    twist_tab[0], twist_tab[1] = twist
    inner_tab[...], outer_tab[...] = prefix_tables()

    @pl.when(me_range != chief)
    def _():
        pl.semaphore_wait(go_sem, 1)

    for k in range(1, SIDE_AZ):
        pl.semaphore_signal(
            near_sem, inc=1, device_id={"az": y * SIDE_AZ + lax.rem(x + k, SIDE_AZ)}, device_id_type=MESH
        )

    some = gathered.at[0, pl.ds(0, GROUP - 1)]
    remote(some, some, pulse_send, pulse_recv.at[0], az=me_az).wait_recv()
    rows = []
    for i in range(SIDE_AZ):
        rows.append(gathered[0, y * SIDE_AZ + i, 2])
        rows.append(gathered[0, lax.rem(y * SIDE_AZ + i + GROUP - 1, GROUP), 2])
    rows = stacked(*(rows * 2))
    place = 2 * x + (iota((SIDE, SIDE), 0) >> 6)
    delay, frac, amp = [as_column(rows, place + BEAMS * i) for i in range(3)]
    far = (iota((SIDE, 1), 0) & SLOTS) != 0
    amp = jnp.where(far == (delay >= TIME_SLOTS), amp, 0.0)
    (echo_left[0], echo_left[1]), (echo_right[0], echo_right[1]) = phase_tables(delay, frac, amp)

    def tiles_of(row, count):
        return pl.ds(pl.multiple_of(row * 8, 8), count * 8)

    def tiles(ref, row, count):
        return ref.at[tiles_of(row, count)]

    def send_tile(j, i, peer):
        @pl.when((peer != me_range) | (i != x))
        def _():
            remote(
                tiles(ready, (j * SIDE_AZ + i) * GROUP + peer, 1),
                tiles(arrived, me_range * BEAMS + 2 * x + j, 1),
                hist_send, hist_recv, range=peer, az=y * SIDE_AZ + i,
            ).start()

    def send_tiles(j, order):
        def column(k, carry):
            i = lax.rem(x + k, SIDE_AZ)
            for peer in order:
                send_tile(j, i, peer)
            return carry

        lax.fori_loop(0, SIDE_AZ, column, 0)

    def work(j, carry):
        @pl.when(j == 1)
        def _():
            some = gathered.at[1, pl.ds(0, GROUP - 1), pl.ds(0, 2)]
            remote(some, some, pulse_send, pulse_recv.at[1], az=me_az).wait_recv()

        e_left, e_right = (echo_left[0], echo_left[1]), (echo_right[0], echo_right[1])
        specs = [spectrum(e_left, e_right, j * SIDE_AZ + i) for i in range(SIDE_AZ)]
        pulse = [gathered[j, :, part].reshape(SIDE, SIDE) for part in range(2)]
        mine = iota((1, SIDE), 1) == first + 2 * x + j
        ambient = jnp.sum(jnp.where(mine, ambient_ref[...], 0.0), axis=1, keepdims=True)
        hist = group_histogram(
            specs, [pulse] * SIDE_AZ, [ambient] * SIDE_AZ, left_tab[...], right_tab[...],
            (twist_tab[0], twist_tab[1]), inner_tab[...], outer_tab[...],
        )
        ready[tiles_of(j * SIDE_AZ * GROUP, SIDE_AZ * GROUP), :] = hist

        @pl.when(j == 0)
        def _():
            pl.semaphore_wait(near_sem, SIDE_AZ - 1)

        send_tiles(j, EARLY_ORDER)
        return carry

    lax.fori_loop(0, 2, work, 0)
    send_tiles(0, LATE_ORDER)
    send_tiles(1, LATE_ORDER)
    for j in range(2):
        arrived[tiles_of(me_range * BEAMS + 2 * x + j, 1), :] = ready[
            tiles_of((j * SIDE_AZ + x) * GROUP + me_range, 1), :
        ]

    some = tiles(arrived, 0, GROUP * BEAMS - 2)
    done = remote(some, some, hist_send, hist_recv, az=me_az)
    done.wait_recv()
    for g in range(GROUP):
        for s in range(8):
            out_ref[0, g * 8 : (g + 1) * 8, s * SIDE : (s + 1) * SIDE] = arrived[
                pl.ds(g * 64 + s, 8, stride=8), :
            ]
    done.wait_send()
    some = gathered.at[0, pl.ds(0, GROUP - 1)]
    remote(some, some, pulse_send, pulse_recv.at[0], az=me_az).wait_send()
    some = gathered.at[1, pl.ds(0, GROUP - 1), pl.ds(0, 2)]
    remote(some, some, pulse_send, pulse_recv.at[1], az=me_az).wait_send()


def per_device(lag, frac, amp, offset, count, ambient, pulse):
    lag, frac, amp = [jnp.swapaxes(v, 1, 2) for v in (lag, frac, amp)]
    hbm = pl.BlockSpec(memory_space=pltpu.HBM)
    dma = pltpu.SemaphoreType.DMA
    return pl.pallas_call(
        kernel,
        out_shape=jax.ShapeDtypeStruct((1, GROUP * BEAMS, TIME_SLOTS // GROUP), F32),
        in_specs=[hbm] * 6,
        out_specs=pl.BlockSpec(memory_space=pltpu.VMEM),
        scratch_shapes=[
            pltpu.VMEM((1, SLOTS, SIDE), jnp.int32),
            pltpu.VMEM((1, SLOTS, SIDE), F32),
            pltpu.VMEM((1, SLOTS, SIDE), F32),
            pltpu.VMEM((1, 1), jnp.int32),
            pltpu.VMEM((1, SIDE), F32),
            pltpu.VMEM((BEAMS, 2, TIME_SLOTS // GROUP), F32),
            pltpu.VMEM((BEAMS, 3, 8, SIDE), F32),
            pltpu.VMEM((2, GROUP, 3, 8, SIDE), F32),
            pltpu.VMEM((2, 2 * SIDE, 2 * SIDE), BF16),
            pltpu.VMEM((2, 2 * SIDE, 2 * SIDE), BF16),
            pltpu.VMEM((2 * SIDE, 6 * SIDE), BF16),
            pltpu.VMEM((6 * SIDE, 2 * SIDE), BF16),
            pltpu.VMEM((2, SIDE, SIDE), F32),
            pltpu.VMEM((2 * SIDE, 2 * SIDE), BF16),
            pltpu.VMEM((SIDE, 2 * SIDE), BF16),
            pltpu.VMEM((GROUP * BEAMS * 8, SIDE), F32),
            pltpu.VMEM((GROUP * BEAMS * 8, SIDE), F32),
            dma((6,)), dma, dma((2,)), dma, dma,
            pltpu.SemaphoreType.REGULAR, pltpu.SemaphoreType.REGULAR,
        ],
        compiler_params=pltpu.CompilerParams(
            collective_id=0, has_side_effects=True, vmem_limit_bytes=40 * 1024 * 1024
        ),
    )(lag, frac, amp, (offset * 16 + count).reshape(1, 1), ambient.reshape(1, SIDE), pulse)


def solution(mesh):
    in_specs = (
        P("az", None, None),
        P("az", None, None),
        P("az", None, None),
        P("az"),
        P("az"),
        P(),
        P("range", None, "az"),
    )
    out_specs = P("az", None, "range")
    return jax.shard_map(
        per_device, mesh=mesh, in_specs=in_specs, out_specs=out_specs, check_vma=False
    )
```

```python
import math

import jax
import jax.numpy as jnp
from jax import lax
from jax.experimental import pallas as pl
from jax.experimental.pallas import tpu as pltpu
from jax.sharding import PartitionSpec as P

TIME_SLOTS = 16384
SIDE = 128
BEAMS = 8
SLOTS = 8
GROUP = 16
HALF = 8
EARLY_ORDER = (1, 0, 7, 6, 3, 2, 5, 4)
LATE_ORDER = (8, 9, 14, 15, 10, 11, 12, 13)
SIDE_AZ = 4
MESH = pl.DeviceIdType.MESH
F32 = jnp.float32
BF16 = jnp.bfloat16


def iota(shape, dim):
    return lax.broadcasted_iota(jnp.int32, shape, dim)


def cos_sin(turns):
    x = (turns - jnp.round(turns)) * math.pi
    y = x * x
    s = -1.0 / 39916800 * y + 1.0 / 362880
    s = s * y - 1.0 / 5040
    s = s * y + 1.0 / 120
    s = s * y - 1.0 / 6
    s = (s * y + 1.0) * x
    c = 1.0 / 479001600 * y - 1.0 / 3628800
    c = c * y + 1.0 / 40320
    c = c * y - 1.0 / 720
    c = c * y + 1.0 / 24
    c = c * y - 0.5
    c = c * y + 1.0
    return 1.0 - 2.0 * s * s, 2.0 * s * c


def split(x):
    hi = x.astype(BF16)
    return hi, (x - hi.astype(F32)).astype(BF16)


def dot(a, b):
    return jnp.dot(a, b, preferred_element_type=F32)


def blocks(a, b, c, d):
    return jnp.concatenate(
        [jnp.concatenate([a, b], axis=1), jnp.concatenate([c, d], axis=1)], axis=0
    )


def dft_tables():
    row, col = iota((SIDE, SIDE), 0), iota((SIDE, SIDE), 1)
    c, s = cos_sin(((row * col) & (SIDE - 1)).astype(F32) * (1.0 / SIDE))
    left = split(blocks(c, -s, s, c))
    right = split(blocks(c, s, -s, c))
    twist = cos_sin((row * col).astype(F32) * (1.0 / TIME_SLOTS))
    return left, right, twist


def prefix_tables():
    row, col = iota((SIDE, SIDE), 0), iota((SIDE, SIDE), 1)
    upper = jnp.where(row < col, 1.0, 0.0).astype(F32)
    ones = jnp.ones((SIDE, SIDE), F32)
    lower = jnp.where(col < row, 1.0, 0.0).astype(F32)
    inner = blocks(upper, ones, upper, ones).astype(BF16)
    outer = jnp.concatenate([lower, lower], axis=1).astype(BF16)
    return inner, outer


def as_column(rows, lane):
    return jnp.sum(jnp.where(iota(rows.shape, 1) == lane, rows, 0.0), axis=1, keepdims=True)


def as_row(column):
    row, col = iota((SIDE, SIDE), 0), iota((SIDE, SIDE), 1)
    wide = jnp.broadcast_to(column, (SIDE, SIDE))
    return jnp.sum(jnp.where(row == col, wide, 0.0), axis=0, keepdims=True)


def phase_tables(delay, frac, amp):
    delay, frac, amp = [jnp.concatenate([v, v], axis=0) for v in (delay, frac, amp)]
    row, col = iota((SIDE, SIDE), 0), iota((SIDE, SIDE), 1)
    whole = (col * delay.astype(jnp.int32)) & (TIME_SLOTS - 1)
    c, s = cos_sin((whole.astype(F32) + col.astype(F32) * frac) * (1.0 / TIME_SLOTS))
    inner = jnp.where(row < SIDE // 2, c, s) * amp
    near_row = (row & SLOTS) == 0
    right = split(
        jnp.concatenate([jnp.where(near_row, inner, 0.0), jnp.where(near_row, 0.0, inner)], axis=1)
    )
    signed = row - jnp.where(row >= SIDE // 2, SIDE, 0)
    whole = (signed * as_row(delay).astype(jnp.int32)) & (SIDE - 1)
    c, s = cos_sin((whole.astype(F32) + signed.astype(F32) * as_row(frac)) * (1.0 / SIDE))
    cosines = col < SIDE // 2
    hi, lo = split(jnp.concatenate([jnp.where(cosines, c, -s), jnp.where(cosines, -s, -c)], axis=0))
    return jnp.concatenate([hi, hi, lo], axis=1), right


def spectrum(left, right, column):
    mine = ((iota((SIDE, 2 * SIDE), 0) & (SIDE // 2 - 1)) >> 4) == column
    hi, lo = [jnp.where(mine, x.astype(F32), 0.0).astype(BF16) for x in right]
    return dot(left, jnp.concatenate([hi, lo, hi], axis=0))


def side_by_side(*parts):
    return jnp.concatenate(parts, axis=1)


def stacked(*parts):
    return jnp.concatenate(parts, axis=0)


def group_histogram(specs, pulses, ambients, left, right, twist, inner, outer):
    count = len(specs)
    rows = []
    for spec, (pulse_real, pulse_imag) in zip(specs, pulses):
        real, imag = spec[:SIDE], spec[SIDE:]
        wide_real, wide_imag = side_by_side(pulse_real, pulse_real), side_by_side(pulse_imag, pulse_imag)
        hi, lo = split(stacked(wide_real * real - wide_imag * imag, wide_real * imag + wide_imag * real))
        section = dot(left, stacked(hi, lo, hi))
        for trip in range(2):
            real = section[:SIDE, trip * SIDE : (trip + 1) * SIDE]
            imag = section[SIDE:, trip * SIDE : (trip + 1) * SIDE]
            rows.append(side_by_side(real * twist[0] - imag * twist[1], real * twist[1] + imag * twist[0]))
    hi, lo = split(stacked(*rows))
    field = dot(side_by_side(hi, lo, hi), right)
    fluxes = []
    for j in range(count):
        power = field[2 * SIDE * j : 2 * SIDE * (j + 1)]
        power = power * power
        power = power[:SIDE] + power[SIDE:]
        power = power[:, :SIDE] + power[:, SIDE:]
        fluxes.append(jnp.transpose((power * (1.0 / TIME_SLOTS) + ambients[j]) * (1.0 / TIME_SLOTS)))
    flux = stacked(*fluxes)
    hi, lo = split(flux)
    sums = dot(side_by_side(hi, lo), inner)
    hi, lo = split(side_by_side(*[sums[SIDE * j : SIDE * (j + 1), SIDE:] for j in range(count)]))
    carried = dot(outer, stacked(hi, lo))
    before = stacked(
        *[sums[SIDE * j : SIDE * (j + 1), :SIDE] + carried[:, SIDE * j : SIDE * (j + 1)] for j in range(count)]
    )
    series = 1.0 - flux * 0.25
    series = 1.0 - flux * (1.0 / 3) * series
    series = 1.0 - flux * 0.5 * series
    detected = jnp.where(flux < 1.0 / 32, flux * series, 1.0 - jnp.exp(-flux))
    return TIME_SLOTS * detected * jnp.exp(-before)


def kernel(
    lag_hbm, frac_hbm, amp_hbm, packed_hbm, ambient_hbm, pulse_hbm,
    out_ref,
    lag_ref, frac_ref, amp_ref, packed_ref, ambient_ref, pulse_ref,
    own, gathered, extra, left_tab, right_tab, twist_tab, inner_tab, outer_tab,
    ready, arrived,
    in_sem, extra_send, extra_recv, pulse_send, pulse_recv, hist_send, hist_recv, go_sem, near_sem,
):
    me_range, me_az = lax.axis_index("range"), lax.axis_index("az")
    y, x = me_az // SIDE_AZ, lax.rem(me_az, SIDE_AZ)
    chief = GROUP - 1
    early = me_range < HALF
    late = jnp.logical_not(early)
    partner = lax.rem(me_range + HALF, GROUP)

    def remote(src, dst, send, recv, **where):
        return pltpu.make_async_remote_copy(
            src_ref=src, dst_ref=dst, send_sem=send, recv_sem=recv, device_id=where, device_id_type=MESH
        )

    fetches = [
        pltpu.make_async_copy(src, dst, in_sem.at[i])
        for i, (src, dst) in enumerate(
            (
                (pulse_hbm, pulse_ref), (lag_hbm, lag_ref), (frac_hbm, frac_ref), (amp_hbm, amp_ref),
                (packed_hbm, packed_ref), (ambient_hbm, ambient_ref),
            )
        )
    ]
    for fetch in fetches:
        fetch.start()

    barrier = pltpu.get_barrier_semaphore()

    def greet(k, carry):
        pl.semaphore_signal(
            barrier, inc=1, device_id={"az": lax.rem(me_az + k, GROUP)}, device_id_type=MESH
        )
        return carry

    lax.fori_loop(1, GROUP, greet, 0)

    @pl.when(me_range != chief)
    def _():
        pl.semaphore_signal(barrier, inc=1, device_id={"range": chief}, device_id_type=MESH)

    @pl.when(early)
    def _():
        pl.semaphore_signal(barrier, inc=1, device_id={"range": partner}, device_id_type=MESH)

    fetches[0].wait()
    for b in range(BEAMS):
        for part in range(2):
            for q in range(8):
                own[b % 2, b // 2, part, q : q + 1, :] = pulse_ref[b, part : part + 1, q * SIDE : (q + 1) * SIDE]
    for fetch in fetches[1:]:
        fetch.wait()
    first = me_range * BEAMS
    delay = (lag_ref[0] + (packed_ref[...] >> 4)).astype(F32)
    live = iota((SLOTS, SIDE), 0) < (packed_ref[...] & 15)
    amp = jnp.where(live, amp_ref[0], 0.0)
    delay, frac, amp = [
        pltpu.roll(v, lax.rem(2 * SIDE + BEAMS * i - first, SIDE), 1)
        for i, v in enumerate((delay, frac_ref[0], amp))
    ]
    lane = iota((SLOTS, SIDE), 1) & (SIDE // 2 - 1)
    echo = jnp.where(lane < BEAMS, delay, jnp.where(lane < 2 * BEAMS, frac, amp))
    for b in range(SIDE_AZ):
        own[0, b, 2] = echo

    pl.semaphore_wait(
        barrier,
        GROUP - 1 + jnp.where(early, 0, 1) + jnp.where(me_range == chief, GROUP - 1, 0),
    )
    parts = pl.ds(0, 2)
    extra_copy = remote(own.at[1, :, parts], extra, extra_send, extra_recv, range=partner)

    @pl.when(late)
    def _():
        extra_copy.start()

    def share(k, carry):
        peer = lax.rem(me_az + k, GROUP)
        mine = own.at[0, lax.rem(peer, SIDE_AZ)]
        remote(mine, gathered.at[0, me_az], pulse_send, pulse_recv.at[0], az=peer).start()
        return carry

    def share_next(k, carry):
        peer = lax.rem(me_az + k, GROUP)
        mine = own.at[1, lax.rem(peer, SIDE_AZ), parts]
        remote(mine, gathered.at[1, me_az, parts], pulse_send, pulse_recv.at[1], az=peer).start()
        return carry

    def share_extra(k, carry):
        peer = lax.rem(me_az + k, GROUP)
        mine = extra.at[lax.rem(peer, SIDE_AZ)]
        remote(mine, gathered.at[2, me_az, parts], pulse_send, pulse_recv.at[2], az=peer).start()
        return carry

    lax.fori_loop(1, GROUP, share, 0)
    lax.fori_loop(1, GROUP, share_next, 0)

    @pl.when(me_range == chief)
    def _():
        def tell(k, carry):
            pl.semaphore_signal(go_sem, inc=1, device_id={"range": k}, device_id_type=MESH)
            return carry

        lax.fori_loop(0, GROUP - 1, tell, 0)

    gathered[0, me_az] = own[0, x]
    gathered[1, me_az] = own[1, x]

    left, right, twist = dft_tables()
    left_tab[...] = side_by_side(left[0], left[0], left[1])
    right_tab[...] = stacked(right[0], right[0], right[1])
    twist_tab[0], twist_tab[1] = twist
    inner_tab[...], outer_tab[...] = prefix_tables()

    @pl.when(me_range != chief)
    def _():
        pl.semaphore_wait(go_sem, 1)

    for k in range(1, SIDE_AZ):
        pl.semaphore_signal(
            near_sem, inc=1, device_id={"az": y * SIDE_AZ + lax.rem(x + k, SIDE_AZ)}, device_id_type=MESH
        )

    some = gathered.at[0, pl.ds(0, GROUP - 1)]
    remote(some, some, pulse_send, pulse_recv.at[0], az=me_az).wait_recv()
    def phases(j):
        rows = []
        for i in range(SIDE_AZ):
            rows.append(gathered[0, y * SIDE_AZ + i, 2])
            rows.append(gathered[0, lax.rem(y * SIDE_AZ + i + GROUP - 1, GROUP), 2])
        rows = stacked(*rows)
        place = 2 * x + jnp.where(j == 0, 0, 1) + jnp.where(j == 2, SIDE // 2, 0)
        delay, frac, amp = [as_column(rows, place + BEAMS * i) for i in range(3)]
        far = (iota(delay.shape, 0) & SLOTS) != 0
        return phase_tables(delay, frac, jnp.where(far == (delay >= TIME_SLOTS), amp, 0.0))

    def tiles_of(row, count):
        return pl.ds(pl.multiple_of(row * 8, 8), count * 8)

    def tiles(ref, row, count):
        return ref.at[tiles_of(row, count)]

    def beam_of(j):
        block = jnp.where(j == 2, partner, me_range)
        return block * BEAMS + 2 * x + jnp.where(j == 0, 0, 1)

    def send_tile(j, i, peer):
        @pl.when((peer != me_range) | (i != x))
        def _():
            remote(
                tiles(ready, (j * SIDE_AZ + i) * GROUP + peer, 1),
                tiles(arrived, beam_of(j), 1),
                hist_send, hist_recv, range=peer, az=y * SIDE_AZ + i,
            ).start()

    def send_tiles(j, order):
        def column(k, carry):
            i = lax.rem(x + k, SIDE_AZ)
            for peer in order:
                send_tile(j, i, peer)
            return carry

        lax.fori_loop(0, SIDE_AZ, column, 0)

    def work(j, carry):
        @pl.when(j > 0)
        def _():
            some = gathered.at[1, pl.ds(0, GROUP - 1), parts]
            remote(some, some, pulse_send, pulse_recv.at[j], az=me_az).wait_recv()

        e_left, e_right = phases(j)
        specs = [spectrum(e_left, e_right, i) for i in range(SIDE_AZ)]
        pulse = [gathered[j, :, part].reshape(SIDE, SIDE) for part in range(2)]
        mine = iota((1, SIDE), 1) == beam_of(j)
        ambient = jnp.sum(jnp.where(mine, ambient_ref[...], 0.0), axis=1, keepdims=True)
        hist = group_histogram(
            specs, [pulse] * SIDE_AZ, [ambient] * SIDE_AZ, left_tab[...], right_tab[...],
            (twist_tab[0], twist_tab[1]), inner_tab[...], outer_tab[...],
        )
        ready[tiles_of(j * SIDE_AZ * GROUP, SIDE_AZ * GROUP), :] = hist

        @pl.when(j == 0)
        def _():
            pl.semaphore_wait(near_sem, SIDE_AZ - 1)

        @pl.when(early | (j == 0))
        def _():
            send_tiles(j, EARLY_ORDER)

        @pl.when(early & (j == 0))
        def _():
            extra_copy.wait_recv()
            lax.fori_loop(1, GROUP, share_extra, 0)
            gathered[2, me_az, :2] = extra[x]

        @pl.when(j == 1)
        def _():
            send_tiles(0, LATE_ORDER)
            send_tiles(1, LATE_ORDER)

        return carry

    lax.fori_loop(0, jnp.where(early, 3, 2), work, 0)

    def keep(j):
        arrived[tiles_of(beam_of(j), 1), :] = ready[tiles_of((j * SIDE_AZ + x) * GROUP + me_range, 1), :]

    def settled(ref, send, recv, count):
        some = tiles(ref, 0, count)
        return remote(some, some, send, recv, az=me_az)

    keep(0)
    keep(1)

    @pl.when(early)
    def _():
        keep(2)
        settled(arrived, hist_send, hist_recv, GROUP * BEAMS - 3).wait_recv()

    @pl.when(late)
    def _():
        settled(arrived, hist_send, hist_recv, GROUP * BEAMS - 2).wait_recv()

    for g in range(GROUP):
        for s in range(8):
            out_ref[0, g * 8 : (g + 1) * 8, s * SIDE : (s + 1) * SIDE] = arrived[
                pl.ds(g * 64 + s, 8, stride=8), :
            ]
    some = gathered.at[0, pl.ds(0, GROUP - 1)]
    remote(some, some, pulse_send, pulse_recv.at[0], az=me_az).wait_send()
    some = gathered.at[1, pl.ds(0, GROUP - 1), parts]
    remote(some, some, pulse_send, pulse_recv.at[1], az=me_az).wait_send()
    tiles_all, tiles_half = SIDE_AZ * GROUP - 1, SIDE_AZ * HALF - 1

    @pl.when(early)
    def _():
        remote(some, some, pulse_send, pulse_recv.at[1], az=me_az).wait_send()
        settled(ready, hist_send, hist_recv, 2 * tiles_all + tiles_half).wait_send()

    @pl.when(late)
    def _():
        extra_copy.wait_send()
        settled(ready, hist_send, hist_recv, tiles_all + tiles_half).wait_send()


def per_device(lag, frac, amp, offset, count, ambient, pulse):
    lag, frac, amp = [jnp.swapaxes(v, 1, 2) for v in (lag, frac, amp)]
    hbm = pl.BlockSpec(memory_space=pltpu.HBM)
    dma = pltpu.SemaphoreType.DMA
    return pl.pallas_call(
        kernel,
        out_shape=jax.ShapeDtypeStruct((1, GROUP * BEAMS, TIME_SLOTS // GROUP), F32),
        in_specs=[hbm] * 6,
        out_specs=pl.BlockSpec(memory_space=pltpu.VMEM),
        scratch_shapes=[
            pltpu.VMEM((1, SLOTS, SIDE), jnp.int32),
            pltpu.VMEM((1, SLOTS, SIDE), F32),
            pltpu.VMEM((1, SLOTS, SIDE), F32),
            pltpu.VMEM((1, 1), jnp.int32),
            pltpu.VMEM((1, SIDE), F32),
            pltpu.VMEM((BEAMS, 2, TIME_SLOTS // GROUP), F32),
            pltpu.VMEM((2, SIDE_AZ, 3, 8, SIDE), F32),
            pltpu.VMEM((3, GROUP, 3, 8, SIDE), F32),
            pltpu.VMEM((SIDE_AZ, 2, 8, SIDE), F32),
            pltpu.VMEM((2 * SIDE, 6 * SIDE), BF16),
            pltpu.VMEM((6 * SIDE, 2 * SIDE), BF16),
            pltpu.VMEM((2, SIDE, SIDE), F32),
            pltpu.VMEM((2 * SIDE, 2 * SIDE), BF16),
            pltpu.VMEM((SIDE, 2 * SIDE), BF16),
            pltpu.VMEM((3 * SIDE_AZ * SIDE, SIDE), F32),
            pltpu.VMEM((GROUP * BEAMS * 8, SIDE), F32),
            dma((6,)), dma, dma, dma, dma((3,)), dma, dma,
            pltpu.SemaphoreType.REGULAR, pltpu.SemaphoreType.REGULAR,
        ],
        compiler_params=pltpu.CompilerParams(
            collective_id=0, has_side_effects=True, vmem_limit_bytes=40 * 1024 * 1024
        ),
    )(lag, frac, amp, (offset * 16 + count).reshape(1, 1), ambient.reshape(1, SIDE), pulse)


def solution(mesh):
    in_specs = (
        P("az", None, None),
        P("az", None, None),
        P("az", None, None),
        P("az"),
        P("az"),
        P(),
        P("range", None, "az"),
    )
    out_specs = P("az", None, "range")
    return jax.shard_map(
        per_device, mesh=mesh, in_specs=in_specs, out_specs=out_specs, check_vma=False
    )
```

```python
import math

import jax
import jax.numpy as jnp
from jax import lax
from jax.experimental import pallas as pl
from jax.experimental.pallas import tpu as pltpu
from jax.sharding import PartitionSpec as P

TIME_SLOTS = 16384
SIDE = 128
BEAMS = 8
SLOTS = 8
GROUP = 16
HALF = 8
SIDE_AZ = 4
MESH = pl.DeviceIdType.MESH
F32 = jnp.float32
BF16 = jnp.bfloat16


def iota(shape, dim):
    return lax.broadcasted_iota(jnp.int32, shape, dim)


def cos_sin(turns):
    x = (turns - jnp.round(turns)) * math.pi
    y = x * x
    s = -1.0 / 39916800 * y + 1.0 / 362880
    s = s * y - 1.0 / 5040
    s = s * y + 1.0 / 120
    s = s * y - 1.0 / 6
    s = (s * y + 1.0) * x
    c = 1.0 / 479001600 * y - 1.0 / 3628800
    c = c * y + 1.0 / 40320
    c = c * y - 1.0 / 720
    c = c * y + 1.0 / 24
    c = c * y - 0.5
    c = c * y + 1.0
    return 1.0 - 2.0 * s * s, 2.0 * s * c


def split(x):
    hi = x.astype(BF16)
    return hi, (x - hi.astype(F32)).astype(BF16)


def dot(a, b):
    return jnp.dot(a, b, preferred_element_type=F32)


def blocks(a, b, c, d):
    return jnp.concatenate(
        [jnp.concatenate([a, b], axis=1), jnp.concatenate([c, d], axis=1)], axis=0
    )


def dft_tables():
    row, col = iota((SIDE, SIDE), 0), iota((SIDE, SIDE), 1)
    c, s = cos_sin(((row * col) & (SIDE - 1)).astype(F32) * (1.0 / SIDE))
    left = split(blocks(c, -s, s, c))
    right = split(blocks(c, s, -s, c))
    twist = cos_sin((row * col).astype(F32) * (1.0 / TIME_SLOTS))
    return left, right, twist


def prefix_tables():
    row, col = iota((SIDE, SIDE), 0), iota((SIDE, SIDE), 1)
    upper = jnp.where(row < col, 1.0, 0.0).astype(F32)
    ones = jnp.ones((SIDE, SIDE), F32)
    lower = jnp.where(col < row, 1.0, 0.0).astype(F32)
    inner = blocks(upper, ones, upper, ones).astype(BF16)
    outer = jnp.concatenate([lower, lower], axis=1).astype(BF16)
    return inner, outer


def as_column(rows, lane):
    return jnp.sum(jnp.where(iota(rows.shape, 1) == lane, rows, 0.0), axis=1, keepdims=True)


def as_row(column):
    row, col = iota((SIDE, SIDE), 0), iota((SIDE, SIDE), 1)
    wide = jnp.broadcast_to(column, (SIDE, SIDE))
    return jnp.sum(jnp.where(row == col, wide, 0.0), axis=0, keepdims=True)


def phase_tables(delay, frac, amp):
    delay, frac, amp = [jnp.concatenate([v, v], axis=0) for v in (delay, frac, amp)]
    row, col = iota((SIDE, SIDE), 0), iota((SIDE, SIDE), 1)
    whole = (col * delay.astype(jnp.int32)) & (TIME_SLOTS - 1)
    c, s = cos_sin((whole.astype(F32) + col.astype(F32) * frac) * (1.0 / TIME_SLOTS))
    inner = jnp.where(row < SIDE // 2, c, s) * amp
    near_row = (row & SLOTS) == 0
    right = split(
        jnp.concatenate([jnp.where(near_row, inner, 0.0), jnp.where(near_row, 0.0, inner)], axis=1)
    )
    signed = row - jnp.where(row >= SIDE // 2, SIDE, 0)
    whole = (signed * as_row(delay).astype(jnp.int32)) & (SIDE - 1)
    c, s = cos_sin((whole.astype(F32) + signed.astype(F32) * as_row(frac)) * (1.0 / SIDE))
    cosines = col < SIDE // 2
    hi, lo = split(jnp.concatenate([jnp.where(cosines, c, -s), jnp.where(cosines, -s, -c)], axis=0))
    return jnp.concatenate([hi, hi, lo], axis=1), right


def spectrum(left, right, column):
    mine = ((iota((SIDE, 2 * SIDE), 0) & (SIDE // 2 - 1)) >> 4) == column
    hi, lo = [jnp.where(mine, x.astype(F32), 0.0).astype(BF16) for x in right]
    return dot(left, jnp.concatenate([hi, lo, hi], axis=0))


def side_by_side(*parts):
    return jnp.concatenate(parts, axis=1)


def stacked(*parts):
    return jnp.concatenate(parts, axis=0)


def group_histogram(specs, pulses, ambients, left, right, twist, inner, outer):
    count = len(specs)
    rows = []
    for spec, (pulse_real, pulse_imag) in zip(specs, pulses):
        real, imag = spec[:SIDE], spec[SIDE:]
        wide_real, wide_imag = side_by_side(pulse_real, pulse_real), side_by_side(pulse_imag, pulse_imag)
        hi, lo = split(stacked(wide_real * real - wide_imag * imag, wide_real * imag + wide_imag * real))
        section = dot(left, stacked(hi, lo, hi))
        for trip in range(2):
            real = section[:SIDE, trip * SIDE : (trip + 1) * SIDE]
            imag = section[SIDE:, trip * SIDE : (trip + 1) * SIDE]
            rows.append(side_by_side(real * twist[0] - imag * twist[1], real * twist[1] + imag * twist[0]))
    hi, lo = split(stacked(*rows))
    field = dot(side_by_side(hi, lo, hi), right)
    fluxes = []
    for j in range(count):
        power = field[2 * SIDE * j : 2 * SIDE * (j + 1)]
        power = power * power
        power = power[:SIDE] + power[SIDE:]
        power = power[:, :SIDE] + power[:, SIDE:]
        fluxes.append(jnp.transpose((power * (1.0 / TIME_SLOTS) + ambients[j]) * (1.0 / TIME_SLOTS)))
    flux = stacked(*fluxes)
    hi, lo = split(flux)
    sums = dot(side_by_side(hi, lo), inner)
    hi, lo = split(side_by_side(*[sums[SIDE * j : SIDE * (j + 1), SIDE:] for j in range(count)]))
    carried = dot(outer, stacked(hi, lo))
    before = stacked(
        *[sums[SIDE * j : SIDE * (j + 1), :SIDE] + carried[:, SIDE * j : SIDE * (j + 1)] for j in range(count)]
    )
    series = 1.0 - flux * 0.25
    series = 1.0 - flux * (1.0 / 3) * series
    series = 1.0 - flux * 0.5 * series
    detected = jnp.where(flux < 1.0 / 32, flux * series, 1.0 - jnp.exp(-flux))
    return TIME_SLOTS * detected * jnp.exp(-before)


def kernel(
    lag_hbm, frac_hbm, amp_hbm, packed_hbm, ambient_hbm, pulse_hbm,
    out_ref,
    lag_ref, frac_ref, amp_ref, packed_ref, ambient_ref, pulse_ref,
    own, echoes, gathered, extra, left_tab, right_tab, twist_tab, inner_tab, outer_tab,
    ready, arrived,
    in_sem, echo_send, echo_recv, extra_send, extra_recv, pulse_send, pulse_recv, hist_send, hist_recv, go_sem, near_sem,
):
    me_range, me_az = lax.axis_index("range"), lax.axis_index("az")
    y, x = me_az // SIDE_AZ, lax.rem(me_az, SIDE_AZ)
    odd = lax.rem(y, 2)
    row_pair = y - odd
    pair_place = lax.rem(me_az, HALF)
    chief = GROUP - 1
    early = me_range < HALF
    late = jnp.logical_not(early)
    partner = lax.rem(me_range + HALF, GROUP)

    def remote(src, dst, send, recv, **where):
        return pltpu.make_async_remote_copy(
            src_ref=src, dst_ref=dst, send_sem=send, recv_sem=recv, device_id=where, device_id_type=MESH
        )

    fetches = [
        pltpu.make_async_copy(src, dst, in_sem.at[i])
        for i, (src, dst) in enumerate(
            (
                (pulse_hbm, pulse_ref), (lag_hbm, lag_ref), (frac_hbm, frac_ref), (amp_hbm, amp_ref),
                (packed_hbm, packed_ref), (ambient_hbm, ambient_ref),
            )
        )
    ]
    for fetch in fetches:
        fetch.start()

    barrier = pltpu.get_barrier_semaphore()

    def greet(k, carry):
        pl.semaphore_signal(
            barrier, inc=1, device_id={"az": lax.rem(me_az + k, GROUP)}, device_id_type=MESH
        )
        return carry

    lax.fori_loop(1, GROUP, greet, 0)

    @pl.when(me_range != chief)
    def _():
        pl.semaphore_signal(barrier, inc=1, device_id={"range": chief}, device_id_type=MESH)

    @pl.when(early)
    def _():
        pl.semaphore_signal(barrier, inc=1, device_id={"range": partner}, device_id_type=MESH)

    fetches[0].wait()
    for b in range(BEAMS):
        for part in range(2):
            for q in range(8):
                own[b, part, q : q + 1, :] = pulse_ref[b, part : part + 1, q * SIDE : (q + 1) * SIDE]
    for fetch in fetches[1:]:
        fetch.wait()
    first = me_range * BEAMS
    delay = (lag_ref[0] + (packed_ref[...] >> 4)).astype(F32)
    live = iota((SLOTS, SIDE), 0) < (packed_ref[...] & 15)
    amp = jnp.where(live, amp_ref[0], 0.0)
    delay, frac, amp = [
        pltpu.roll(v, lax.rem(2 * SIDE + BEAMS * i - first, SIDE), 1)
        for i, v in enumerate((delay, frac_ref[0], amp))
    ]
    lane = iota((SLOTS, SIDE), 1) & (SIDE // 2 - 1)
    echoes[me_az] = jnp.where(lane < BEAMS, delay, jnp.where(lane < 2 * BEAMS, frac, amp))

    pl.semaphore_wait(
        barrier,
        GROUP - 1 + jnp.where(early, 0, 1) + jnp.where(me_range == chief, GROUP - 1, 0),
    )
    extra_copy = remote(own, extra, extra_send, extra_recv, range=partner)

    @pl.when(late)
    def _():
        extra_copy.start()

    def share_echo(peer):
        mine = echoes.at[me_az]
        remote(mine, mine, echo_send, echo_recv, az=peer).start()

    def share_near(k, carry):
        share_echo(row_pair * SIDE_AZ + lax.rem(pair_place + k, HALF))
        return carry

    lax.fori_loop(1, HALF, share_near, 0)

    @pl.when(pair_place == HALF - 1)
    def _():
        def share_far(k, carry):
            share_echo(lax.rem(me_az + 1 + k, GROUP))
            return carry

        lax.fori_loop(0, HALF, share_far, 0)

    def share(k, carry):
        peer = lax.rem(me_az + k, GROUP)
        beam = lax.rem(peer, HALF)
        remote(own.at[beam], gathered.at[0, me_az], pulse_send, pulse_recv.at[0], az=peer).start()
        return carry

    def share_extra(k, carry):
        peer = lax.rem(me_az + k, GROUP)
        beam = lax.rem(peer + SIDE_AZ, HALF)
        remote(extra.at[beam], gathered.at[1, me_az], pulse_send, pulse_recv.at[1], az=peer).start()
        return carry

    lax.fori_loop(1, GROUP, share, 0)

    @pl.when(me_range == chief)
    def _():
        def tell(k, carry):
            pl.semaphore_signal(go_sem, inc=1, device_id={"range": k}, device_id_type=MESH)
            return carry

        lax.fori_loop(0, GROUP - 1, tell, 0)

    gathered[0, me_az] = own[pair_place]

    left, right, twist = dft_tables()
    left_tab[...] = side_by_side(left[0], left[0], left[1])
    right_tab[...] = stacked(right[0], right[0], right[1])
    twist_tab[0], twist_tab[1] = twist
    inner_tab[...], outer_tab[...] = prefix_tables()

    def pass_on():
        @pl.when(me_range != chief)
        def _():
            pl.semaphore_wait(go_sem, 1)

        for k in range(1, HALF):
            peer = row_pair * SIDE_AZ + lax.rem(pair_place + k, HALF)
            pl.semaphore_signal(near_sem, inc=1, device_id={"az": peer}, device_id_type=MESH)

    pl.when(late)(pass_on)

    some_echoes = echoes.at[pl.ds(0, HALF)]
    remote(some_echoes, some_echoes, echo_send, echo_recv, az=me_az).wait_recv()
    fifteen = gathered.at[0, pl.ds(0, GROUP - 1)]
    remote(fifteen, fifteen, pulse_send, pulse_recv.at[0], az=me_az).wait_recv()

    def row_of(j):
        return y + jnp.where(j == 1, 1 - 2 * odd, 0)

    def beam_of(j):
        return x + SIDE_AZ * jnp.where(j == 2, 1 - odd, odd)

    def phases(j):
        rows = []
        for i in range(SIDE_AZ):
            column = row_of(j) * SIDE_AZ + i
            rows.append(echoes[column])
            rows.append(echoes[lax.rem(column + GROUP - 1, GROUP)])
        rows = stacked(*rows)
        place = beam_of(j) + jnp.where(j == 2, SIDE // 2, 0)
        delay, frac, amp = [as_column(rows, place + BEAMS * i) for i in range(3)]
        far = (iota(delay.shape, 0) & SLOTS) != 0
        return phase_tables(delay, frac, jnp.where(far == (delay >= TIME_SLOTS), amp, 0.0))

    def tiles_of(row, count):
        return pl.ds(pl.multiple_of(row * 8, 8), count * 8)

    def tiles(ref, row, count):
        return ref.at[tiles_of(row, count)]

    def whole_beam(j):
        return jnp.where(j == 2, partner, me_range) * BEAMS + beam_of(j)

    def send_tile(j, i, peer):
        column = row_of(j) * SIDE_AZ + i

        @pl.when((peer != me_range) | (column != me_az))
        def _():
            remote(
                tiles(ready, (j * SIDE_AZ + i) * GROUP + peer, 1), tiles(arrived, whole_beam(j), 1),
                hist_send, hist_recv, range=peer, az=column,
            ).start()

    def send_tiles(j, half):
        away = half != me_range // HALF
        high, low = me_range // 4 - 2 * (me_range // HALF), lax.rem(me_range // 2, 2)
        for turn in range(4):
            t1, t0 = jnp.where(away, turn // 2, 1 - turn // 2), jnp.where(away, turn % 2, 1 - turn % 2)
            plane = 2 * (high + t1 - 2 * high * t1) + low + t0 - 2 * low * t0

            def column(k, carry):
                for c in (1, 0):
                    send_tile(j, lax.rem(x + k, SIDE_AZ), half * HALF + 2 * plane + c)
                return carry

            lax.fori_loop(0, SIDE_AZ, column, 0)

    def work(j, carry):
        @pl.when(j == 2)
        def _():
            remote(fifteen, fifteen, pulse_send, pulse_recv.at[1], az=me_az).wait_recv()

        e_left, e_right = phases(j)
        specs = [spectrum(e_left, e_right, i) for i in range(SIDE_AZ)]
        source = jnp.where(j == 2, 1, 0)
        pulse = [gathered[source, :, part].reshape(SIDE, SIDE) for part in range(2)]
        mine = iota((1, SIDE), 1) == whole_beam(j)
        ambient = jnp.sum(jnp.where(mine, ambient_ref[...], 0.0), axis=1, keepdims=True)
        hist = group_histogram(
            specs, [pulse] * SIDE_AZ, [ambient] * SIDE_AZ, left_tab[...], right_tab[...],
            (twist_tab[0], twist_tab[1]), inner_tab[...], outer_tab[...],
        )
        ready[tiles_of(j * SIDE_AZ * GROUP, SIDE_AZ * GROUP), :] = hist

        @pl.when(early & (j == 0))
        def _():
            extra_copy.wait_recv()
            lax.fori_loop(1, GROUP, share_extra, 0)
            gathered[1, me_az] = extra[beam_of(2)]

        @pl.when(j == 0)
        def _():
            pl.when(early)(pass_on)
            pl.semaphore_wait(near_sem, HALF - 1)

        @pl.when(early | (j == 0))
        def _():
            send_tiles(j, 0)

        @pl.when(j == 0)
        def _():
            send_tiles(0, 1)

        @pl.when((j == jnp.where(early, 2, 1)))
        def _():
            send_tiles(1, 1)

        return carry

    lax.fori_loop(0, jnp.where(early, 3, 2), work, 0)

    def keep(j):
        arrived[tiles_of(whole_beam(j), 1), :] = ready[
            tiles_of((j * SIDE_AZ + x) * GROUP + me_range, 1), :
        ]

    def settled(ref, send, recv, count):
        some = tiles(ref, 0, count)
        return remote(some, some, send, recv, az=me_az)

    keep(0)

    @pl.when(early)
    def _():
        keep(2)
        settled(arrived, hist_send, hist_recv, GROUP * BEAMS - 2).wait_recv()

    @pl.when(late)
    def _():
        settled(arrived, hist_send, hist_recv, GROUP * BEAMS - 1).wait_recv()

    for g in range(GROUP):
        for s in range(8):
            out_ref[0, g * 8 : (g + 1) * 8, s * SIDE : (s + 1) * SIDE] = arrived[
                pl.ds(g * 64 + s, 8, stride=8), :
            ]
    remote(fifteen, fifteen, pulse_send, pulse_recv.at[0], az=me_az).wait_send()
    seven = echoes.at[pl.ds(0, HALF - 1)]
    remote(seven, seven, echo_send, echo_recv, az=me_az).wait_send()

    @pl.when(pair_place == HALF - 1)
    def _():
        remote(some_echoes, some_echoes, echo_send, echo_recv, az=me_az).wait_send()

    tiles_all, tiles_half = SIDE_AZ * GROUP, SIDE_AZ * HALF

    @pl.when(early)
    def _():
        remote(fifteen, fifteen, pulse_send, pulse_recv.at[1], az=me_az).wait_send()
        settled(ready, hist_send, hist_recv, 2 * tiles_all + tiles_half - 2).wait_send()

    @pl.when(late)
    def _():
        extra_copy.wait_send()
        settled(ready, hist_send, hist_recv, tiles_all + tiles_half - 1).wait_send()


def per_device(lag, frac, amp, offset, count, ambient, pulse):
    lag, frac, amp = [jnp.swapaxes(v, 1, 2) for v in (lag, frac, amp)]
    hbm = pl.BlockSpec(memory_space=pltpu.HBM)
    dma = pltpu.SemaphoreType.DMA
    return pl.pallas_call(
        kernel,
        out_shape=jax.ShapeDtypeStruct((1, GROUP * BEAMS, TIME_SLOTS // GROUP), F32),
        in_specs=[hbm] * 6,
        out_specs=pl.BlockSpec(memory_space=pltpu.VMEM),
        scratch_shapes=[
            pltpu.VMEM((1, SLOTS, SIDE), jnp.int32),
            pltpu.VMEM((1, SLOTS, SIDE), F32),
            pltpu.VMEM((1, SLOTS, SIDE), F32),
            pltpu.VMEM((1, 1), jnp.int32),
            pltpu.VMEM((1, SIDE), F32),
            pltpu.VMEM((BEAMS, 2, TIME_SLOTS // GROUP), F32),
            pltpu.VMEM((BEAMS, 2, 8, SIDE), F32),
            pltpu.VMEM((GROUP, SLOTS, SIDE), F32),
            pltpu.VMEM((2, GROUP, 2, 8, SIDE), F32),
            pltpu.VMEM((BEAMS, 2, 8, SIDE), F32),
            pltpu.VMEM((2 * SIDE, 6 * SIDE), BF16),
            pltpu.VMEM((6 * SIDE, 2 * SIDE), BF16),
            pltpu.VMEM((2, SIDE, SIDE), F32),
            pltpu.VMEM((2 * SIDE, 2 * SIDE), BF16),
            pltpu.VMEM((SIDE, 2 * SIDE), BF16),
            pltpu.VMEM((3 * SIDE_AZ * SIDE, SIDE), F32),
            pltpu.VMEM((GROUP * BEAMS * 8, SIDE), F32),
            dma((6,)), dma, dma, dma, dma, dma, dma((2,)), dma, dma,
            pltpu.SemaphoreType.REGULAR, pltpu.SemaphoreType.REGULAR,
        ],
        compiler_params=pltpu.CompilerParams(
            collective_id=0, has_side_effects=True, vmem_limit_bytes=40 * 1024 * 1024
        ),
    )(lag, frac, amp, (offset * 16 + count).reshape(1, 1), ambient.reshape(1, SIDE), pulse)


def solution(mesh):
    in_specs = (
        P("az", None, None),
        P("az", None, None),
        P("az", None, None),
        P("az"),
        P("az"),
        P(),
        P("range", None, "az"),
    )
    out_specs = P("az", None, "range")
    return jax.shard_map(
        per_device, mesh=mesh, in_specs=in_specs, out_specs=out_specs, check_vma=False
    )
```

```python
import math

import jax
import jax.numpy as jnp
from jax import lax
from jax.experimental import pallas as pl
from jax.experimental.pallas import tpu as pltpu
from jax.sharding import PartitionSpec as P

TIME_SLOTS = 16384
SIDE = 128
BEAMS = 8
SLOTS = 8
GROUP = 16
HALF = 8
PIECES = 4
VMEM_LIMIT = 56 * 1024 * 1024
SIDE_AZ = 4
MESH = pl.DeviceIdType.MESH
F32 = jnp.float32
BF16 = jnp.bfloat16


def iota(shape, dim):
    return lax.broadcasted_iota(jnp.int32, shape, dim)


def cos_sin(turns):
    x = (turns - jnp.round(turns)) * math.pi
    y = x * x
    s = -1.0 / 39916800 * y + 1.0 / 362880
    s = s * y - 1.0 / 5040
    s = s * y + 1.0 / 120
    s = s * y - 1.0 / 6
    s = (s * y + 1.0) * x
    c = 1.0 / 479001600 * y - 1.0 / 3628800
    c = c * y + 1.0 / 40320
    c = c * y - 1.0 / 720
    c = c * y + 1.0 / 24
    c = c * y - 0.5
    c = c * y + 1.0
    return 1.0 - 2.0 * s * s, 2.0 * s * c


def split(x):
    hi = x.astype(BF16)
    return hi, (x - hi.astype(F32)).astype(BF16)


def dot(a, b):
    return jnp.dot(a, b, preferred_element_type=F32)


def blocks(a, b, c, d):
    return jnp.concatenate(
        [jnp.concatenate([a, b], axis=1), jnp.concatenate([c, d], axis=1)], axis=0
    )


def dft_tables():
    row, col = iota((SIDE, SIDE), 0), iota((SIDE, SIDE), 1)
    c, s = cos_sin(((row * col) & (SIDE - 1)).astype(F32) * (1.0 / SIDE))
    left = split(blocks(c, -s, s, c))
    right = split(blocks(c, s, -s, c))
    twist = cos_sin((row * col).astype(F32) * (1.0 / TIME_SLOTS))
    return left, right, twist


def prefix_tables():
    row, col = iota((SIDE, SIDE), 0), iota((SIDE, SIDE), 1)
    upper = jnp.where(row < col, 1.0, 0.0).astype(F32)
    ones = jnp.ones((SIDE, SIDE), F32)
    lower = jnp.where(col < row, 1.0, 0.0).astype(F32)
    inner = blocks(upper, ones, upper, ones).astype(BF16)
    outer = jnp.concatenate([lower, lower], axis=1).astype(BF16)
    return inner, outer


def as_column(rows, lane):
    return jnp.sum(jnp.where(iota(rows.shape, 1) == lane, rows, 0.0), axis=1, keepdims=True)


def as_row(column):
    row, col = iota((SIDE, SIDE), 0), iota((SIDE, SIDE), 1)
    wide = jnp.broadcast_to(column, (SIDE, SIDE))
    return jnp.sum(jnp.where(row == col, wide, 0.0), axis=0, keepdims=True)


def phase_tables(delay, frac, amp):
    delay, frac, amp = [jnp.concatenate([v, v], axis=0) for v in (delay, frac, amp)]
    row, col = iota((SIDE, SIDE), 0), iota((SIDE, SIDE), 1)
    whole = (col * delay.astype(jnp.int32)) & (TIME_SLOTS - 1)
    c, s = cos_sin((whole.astype(F32) + col.astype(F32) * frac) * (1.0 / TIME_SLOTS))
    inner = jnp.where(row < SIDE // 2, c, s) * amp
    near_row = (row & SLOTS) == 0
    right = split(
        jnp.concatenate([jnp.where(near_row, inner, 0.0), jnp.where(near_row, 0.0, inner)], axis=1)
    )
    signed = row - jnp.where(row >= SIDE // 2, SIDE, 0)
    whole = (signed * as_row(delay).astype(jnp.int32)) & (SIDE - 1)
    c, s = cos_sin((whole.astype(F32) + signed.astype(F32) * as_row(frac)) * (1.0 / SIDE))
    cosines = col < SIDE // 2
    hi, lo = split(jnp.concatenate([jnp.where(cosines, c, -s), jnp.where(cosines, -s, -c)], axis=0))
    return jnp.concatenate([hi, hi, lo], axis=1), right


def spectrum(left, right, column):
    mine = ((iota((SIDE, 2 * SIDE), 0) & (SIDE // 2 - 1)) >> 4) == column
    hi, lo = [jnp.where(mine, x.astype(F32), 0.0).astype(BF16) for x in right]
    return dot(left, jnp.concatenate([hi, lo, hi], axis=0))


def side_by_side(*parts):
    return jnp.concatenate(parts, axis=1)


def stacked(*parts):
    return jnp.concatenate(parts, axis=0)


def group_histogram(specs, pulses, ambients, left, right, twist, inner, outer):
    count = len(specs)
    rows = []
    for spec, (pulse_real, pulse_imag) in zip(specs, pulses):
        real, imag = spec[:SIDE], spec[SIDE:]
        wide_real, wide_imag = side_by_side(pulse_real, pulse_real), side_by_side(pulse_imag, pulse_imag)
        hi, lo = split(stacked(wide_real * real - wide_imag * imag, wide_real * imag + wide_imag * real))
        section = dot(left, stacked(hi, lo, hi))
        for trip in range(2):
            real = section[:SIDE, trip * SIDE : (trip + 1) * SIDE]
            imag = section[SIDE:, trip * SIDE : (trip + 1) * SIDE]
            rows.append(side_by_side(real * twist[0] - imag * twist[1], real * twist[1] + imag * twist[0]))
    hi, lo = split(stacked(*rows))
    field = dot(side_by_side(hi, lo, hi), right)
    fluxes = []
    for j in range(count):
        power = field[2 * SIDE * j : 2 * SIDE * (j + 1)]
        power = power * power
        power = power[:SIDE] + power[SIDE:]
        power = power[:, :SIDE] + power[:, SIDE:]
        fluxes.append(jnp.transpose((power * (1.0 / TIME_SLOTS) + ambients[j]) * (1.0 / TIME_SLOTS)))
    flux = stacked(*fluxes)
    hi, lo = split(flux)
    sums = dot(side_by_side(hi, lo), inner)
    hi, lo = split(side_by_side(*[sums[SIDE * j : SIDE * (j + 1), SIDE:] for j in range(count)]))
    carried = dot(outer, stacked(hi, lo))
    before = stacked(
        *[sums[SIDE * j : SIDE * (j + 1), :SIDE] + carried[:, SIDE * j : SIDE * (j + 1)] for j in range(count)]
    )
    series = 1.0 - flux * 0.25
    series = 1.0 - flux * (1.0 / 3) * series
    series = 1.0 - flux * 0.5 * series
    detected = jnp.where(flux < 1.0 / 32, flux * series, 1.0 - jnp.exp(-flux))
    return TIME_SLOTS * detected * jnp.exp(-before)


def kernel(
    lag_hbm, frac_hbm, amp_hbm, packed_hbm, ambient_hbm, pulse_hbm,
    arrived,
    lag_ref, frac_ref, amp_ref, packed_ref, ambient_ref, pulse_ref,
    own, echoes, gathered, extra, spec, left_tab, right_tab, twist_tab, inner_tab, outer_tab,
    ready,
    in_sem, keep_sem, echo_send, echo_recv, extra_send, extra_recv, pulse_send, pulse_recv, hist_send, hist_recv, go_sem, near_sem,
):
    me_range, me_az = lax.axis_index("range"), lax.axis_index("az")
    y, x = me_az // SIDE_AZ, lax.rem(me_az, SIDE_AZ)
    odd = lax.rem(y, 2)
    row_pair = y - odd
    pair_place = lax.rem(me_az, HALF)
    chief = GROUP - 1
    z, core = me_range // 2, lax.rem(me_range, 2)
    early = me_range < HALF
    late = jnp.logical_not(early)
    partner = lax.rem(me_range + HALF, GROUP)

    def remote(src, dst, send, recv, **where):
        return pltpu.make_async_remote_copy(
            src_ref=src, dst_ref=dst, send_sem=send, recv_sem=recv, device_id=where, device_id_type=MESH
        )

    fetches = [
        pltpu.make_async_copy(src, dst, in_sem.at[i])
        for i, (src, dst) in enumerate(
            (
                (pulse_hbm, pulse_ref), (lag_hbm, lag_ref), (frac_hbm, frac_ref), (amp_hbm, amp_ref),
                (packed_hbm, packed_ref), (ambient_hbm, ambient_ref),
            )
        )
    ]
    for fetch in fetches:
        fetch.start()

    barrier = pltpu.get_barrier_semaphore()

    def greet(k, carry):
        pl.semaphore_signal(
            barrier, inc=1, device_id={"az": lax.rem(me_az + k, GROUP)}, device_id_type=MESH
        )
        return carry

    lax.fori_loop(1, GROUP, greet, 0)

    @pl.when(me_range != chief)
    def _():
        pl.semaphore_signal(barrier, inc=1, device_id={"range": chief}, device_id_type=MESH)

    @pl.when(early)
    def _():
        pl.semaphore_signal(barrier, inc=1, device_id={"range": partner}, device_id_type=MESH)

    fetches[0].wait()
    for b in range(BEAMS):
        for part in range(2):
            for q in range(8):
                own[b, part, q : q + 1, :] = pulse_ref[b, part : part + 1, q * SIDE : (q + 1) * SIDE]
    for fetch in fetches[1:]:
        fetch.wait()
    first = me_range * BEAMS
    delay = (lag_ref[0] + (packed_ref[...] >> 4)).astype(F32)
    live = iota((SLOTS, SIDE), 0) < (packed_ref[...] & 15)
    amp = jnp.where(live, amp_ref[0], 0.0)
    delay, frac, amp = [
        pltpu.roll(v, lax.rem(2 * SIDE + BEAMS * i - first, SIDE), 1)
        for i, v in enumerate((delay, frac_ref[0], amp))
    ]
    lane = iota((SLOTS, SIDE), 1) & (SIDE // 2 - 1)
    echoes[me_az] = jnp.where(lane < BEAMS, delay, jnp.where(lane < 2 * BEAMS, frac, amp))

    pl.semaphore_wait(
        barrier,
        GROUP - 1 + jnp.where(early, 0, 1) + jnp.where(me_range == chief, GROUP - 1, 0),
    )
    extra_copy = remote(own, extra, extra_send, extra_recv, range=partner)
    pl.when(late)(lambda: extra_copy.start())

    def share_echo(peer):
        mine = echoes.at[me_az]
        remote(mine, mine, echo_send, echo_recv, az=peer).start()

    def share_near(k, carry):
        share_echo(row_pair * SIDE_AZ + lax.rem(pair_place + k, HALF))
        return carry

    lax.fori_loop(1, HALF, share_near, 0)

    @pl.when(pair_place == HALF - 1)
    def _():
        def share_far(k, carry):
            share_echo(lax.rem(me_az + 1 + k, GROUP))
            return carry

        lax.fori_loop(0, HALF, share_far, 0)

    def share_step(source, which, dy, dx):
        peer = lax.rem(y + dy, SIDE_AZ) * SIDE_AZ + lax.rem(x + dx, SIDE_AZ)
        beam = lax.rem(peer, HALF)
        remote(source.at[beam], gathered.at[which, me_az], pulse_send, pulse_recv.at[which], az=peer).start()

    def share(source, which):
        for dy, dx in sorted(
            [(i // SIDE_AZ, i % SIDE_AZ) for i in range(1, GROUP)],
            key=lambda d: -(min(d[0], SIDE_AZ - d[0]) + min(d[1], SIDE_AZ - d[1])),
        ):
            share_step(source, which, dy, dx)

    share(own, 0)

    @pl.when(me_range == chief)
    def _():
        def tell(k, carry):
            pl.semaphore_signal(go_sem, inc=1, device_id={"range": k}, device_id_type=MESH)
            return carry

        lax.fori_loop(0, GROUP - 1, tell, 0)

    gathered[0, me_az] = own[pair_place]

    left, right, twist = dft_tables()
    left_tab[...] = side_by_side(left[0], left[0], left[1])
    right_tab[...] = stacked(right[0], right[0], right[1])
    twist_tab[0], twist_tab[1] = twist
    inner_tab[...], outer_tab[...] = prefix_tables()

    some_echoes = echoes.at[pl.ds(0, HALF)]
    remote(some_echoes, some_echoes, echo_send, echo_recv, az=me_az).wait_recv()

    def row_of(j):
        return y + lax.rem(j, 2) * (1 - 2 * odd)

    def phases(j):
        rows = []
        for i in range(SIDE_AZ):
            column = row_of(j) * SIDE_AZ + i
            rows.append(echoes[column])
            rows.append(echoes[lax.rem(column + GROUP - 1, GROUP)])
        rows = stacked(*rows)
        delay, frac, amp = [as_column(rows, pair_place + SIDE // 2 * (j // 2) + BEAMS * i) for i in range(3)]
        far = (iota(delay.shape, 0) & SLOTS) != 0
        return phase_tables(delay, frac, jnp.where(far == (delay >= TIME_SLOTS), amp, 0.0))

    def prepare(j, carry):
        e_left, e_right = phases(j)
        for i in range(SIDE_AZ):
            spec[j * SIDE_AZ + i] = spectrum(e_left, e_right, i)
        return carry

    lax.fori_loop(0, 2, prepare, 0)
    @pl.when(me_range != chief)
    def _():
        pl.semaphore_wait(go_sem, 1)

    pl.when(early)(lambda: extra_copy.start())
    for k in range(1, HALF):
        peer = row_pair * SIDE_AZ + lax.rem(pair_place + k, HALF)
        pl.semaphore_signal(near_sem, inc=1, device_id={"az": peer}, device_id_type=MESH)

    fifteen = gathered.at[0, pl.ds(0, GROUP - 1)]

    def wait_pulses(which):
        remote(fifteen, fifteen, pulse_send, pulse_recv.at[which], az=me_az).wait_recv()

    wait_pulses(0)

    def tiles_of(row, count):
        return pl.ds(pl.multiple_of(row * 8, 8), count * 8)

    def tiles(ref, row, count):
        return ref.at[tiles_of(row, count)]

    def beam_of(j):
        return (me_range + j // 2 * (partner - me_range)) * BEAMS + pair_place

    def send_tile(j, i, peer):
        column = row_of(j) * SIDE_AZ + i

        @pl.when((peer != me_range) | (column != me_az))
        def _():
            remote(
                tiles(ready, (j * SIDE_AZ + i) * GROUP + peer, 1), tiles(arrived, beam_of(j), 1),
                hist_send, hist_recv, range=peer, az=column,
            ).start()

    def send_tiles(j):
        own_block = j < 2

        def column(k, carry):
            i = lax.rem(x + k, SIDE_AZ)
            for step in (3, -3, 2, -2, 1, -1, 0):
                plane = lax.rem(z + step + 8, 8)
                close = jnp.where(core == 0, step in (-1, 0, 1, 2), step in (-2, -1, 0, 1))
                to_early = plane < 4
                wanted = (own_block & (close | (early & to_early))) | (
                    jnp.logical_not(own_block) & close & (early | jnp.logical_not(to_early))
                )

                @pl.when(wanted)
                def _():
                    for c in (1, 0):
                        send_tile(j, i, 2 * plane + c)

            return carry

        lax.fori_loop(0, SIDE_AZ, column, 0)

    def work(j, carry):
        @pl.when(j == 2)
        def _():
            wait_pulses(1)

        specs = [spec[j * SIDE_AZ + i] for i in range(SIDE_AZ)]
        pulse = [gathered[j // 2, :, part].reshape(SIDE, SIDE) for part in range(2)]
        mine = iota((1, SIDE), 1) == beam_of(j)
        ambient = jnp.sum(jnp.where(mine, ambient_ref[...], 0.0), axis=1, keepdims=True)
        hist = group_histogram(
            specs, [pulse] * SIDE_AZ, [ambient] * SIDE_AZ, left_tab[...], right_tab[...],
            (twist_tab[0], twist_tab[1]), inner_tab[...], outer_tab[...],
        )
        ready[tiles_of(j * SIDE_AZ * GROUP, SIDE_AZ * GROUP), :] = hist

        @pl.when(j == 0)
        def _():
            pl.semaphore_wait(near_sem, HALF - 1)

        send_tiles(j)

        @pl.when(j == 0)
        def _():
            extra_copy.wait_recv()
            share(extra, 1)
            gathered[1, me_az] = extra[pair_place]

        @pl.when(j == 1)
        def _():
            lax.fori_loop(2, 4, prepare, 0)

        return carry

    lax.fori_loop(0, 4, work, 0)
    kept = [
        pltpu.make_async_copy(
            tiles(ready, (j * SIDE_AZ + x) * GROUP + me_range, 1), tiles(arrived, beam_of(j), 1),
            keep_sem.at[j // 2],
        )
        for j in (0, 2)
    ]
    for copy in kept:
        copy.start()

    def settled(ref, send, recv, count):
        some = tiles(ref, 0, count)
        return remote(some, some, send, recv, az=me_az)

    settled(arrived, hist_send, hist_recv, GROUP * BEAMS - 2).wait_recv()
    for copy in kept:
        copy.wait()
    for which in range(2):
        remote(fifteen, fifteen, pulse_send, pulse_recv.at[which], az=me_az).wait_send()
    extra_copy.wait_send()
    seven = echoes.at[pl.ds(0, HALF - 1)]
    remote(seven, seven, echo_send, echo_recv, az=me_az).wait_send()

    @pl.when(pair_place == HALF - 1)
    def _():
        remote(some_echoes, some_echoes, echo_send, echo_recv, az=me_az).wait_send()

    settled(ready, hist_send, hist_recv, 14).wait_send()
    aside = jnp.abs(lax.rem(z, 4) - 1 - core)

    def sent(i, carry):
        settled(ready, hist_send, hist_recv, 16).wait_send()
        return carry

    lax.fori_loop(0, 7 + jnp.where(early, aside, -aside), sent, 0)


def spread(arrived, out_ref, tiles, rows, in_sem, out_sem):
    step = GROUP * BEAMS // PIECES
    fetches = [
        pltpu.make_async_copy(
            arrived.at[pl.ds(k * step * 8, step * 8)], tiles.at[pl.ds(k * step * 8, step * 8)], in_sem.at[k]
        )
        for k in range(PIECES)
    ]
    for fetch in fetches:
        fetch.start()
    stores = []
    for k, fetch in enumerate(fetches):
        fetch.wait()
        for g in range(k * step // 8, (k + 1) * step // 8):
            for s in range(8):
                rows[0, g * 8 : (g + 1) * 8, s * SIDE : (s + 1) * SIDE] = tiles[
                    pl.ds(g * 64 + s, 8, stride=8), :
                ]
        some = pl.ds(k * step, step)
        stores.append(pltpu.make_async_copy(rows.at[:, some], out_ref.at[:, some], out_sem.at[k]))
        stores[-1].start()
    for store in stores:
        store.wait()


def per_device(lag, frac, amp, offset, count, ambient, pulse):
    lag, frac, amp = [jnp.swapaxes(v, 1, 2) for v in (lag, frac, amp)]
    hbm = pl.BlockSpec(memory_space=pltpu.HBM)
    dma = pltpu.SemaphoreType.DMA
    arrived = pl.pallas_call(
        kernel,
        out_shape=jax.ShapeDtypeStruct((GROUP * BEAMS * 8, SIDE), F32),
        in_specs=[hbm] * 6,
        out_specs=hbm,
        scratch_shapes=[
            pltpu.VMEM((1, SLOTS, SIDE), jnp.int32),
            pltpu.VMEM((1, SLOTS, SIDE), F32),
            pltpu.VMEM((1, SLOTS, SIDE), F32),
            pltpu.VMEM((1, 1), jnp.int32),
            pltpu.VMEM((1, SIDE), F32),
            pltpu.VMEM((BEAMS, 2, TIME_SLOTS // GROUP), F32),
            pltpu.VMEM((BEAMS, 2, 8, SIDE), F32),
            pltpu.VMEM((GROUP, SLOTS, SIDE), F32),
            pltpu.VMEM((2, GROUP, 2, 8, SIDE), F32),
            pltpu.VMEM((BEAMS, 2, 8, SIDE), F32),
            pltpu.VMEM((2 * BEAMS, 2 * SIDE, 2 * SIDE), F32),
            pltpu.VMEM((2 * SIDE, 6 * SIDE), BF16),
            pltpu.VMEM((6 * SIDE, 2 * SIDE), BF16),
            pltpu.VMEM((2, SIDE, SIDE), F32),
            pltpu.VMEM((2 * SIDE, 2 * SIDE), BF16),
            pltpu.VMEM((SIDE, 2 * SIDE), BF16),
            pltpu.VMEM((4 * SIDE_AZ * SIDE, SIDE), F32),
            dma((6,)), dma((2,)), dma, dma, dma, dma, dma, dma((2,)), dma, dma,
            pltpu.SemaphoreType.REGULAR, pltpu.SemaphoreType.REGULAR,
        ],
        compiler_params=pltpu.CompilerParams(
            collective_id=0, has_side_effects=True, vmem_limit_bytes=VMEM_LIMIT
        ),
    )(lag, frac, amp, (offset * 16 + count).reshape(1, 1), ambient.reshape(1, SIDE), pulse)
    return pl.pallas_call(
        spread,
        out_shape=jax.ShapeDtypeStruct((1, GROUP * BEAMS, TIME_SLOTS // GROUP), F32),
        in_specs=[hbm],
        out_specs=hbm,
        scratch_shapes=[
            pltpu.VMEM((GROUP * BEAMS * 8, SIDE), F32),
            pltpu.VMEM((1, GROUP * BEAMS, TIME_SLOTS // GROUP), F32),
            dma((PIECES,)), dma((PIECES,)),
        ],
        compiler_params=pltpu.CompilerParams(vmem_limit_bytes=VMEM_LIMIT),
    )(arrived)


def solution(mesh):
    in_specs = (
        P("az", None, None),
        P("az", None, None),
        P("az", None, None),
        P("az"),
        P("az"),
        P(),
        P("range", None, "az"),
    )
    out_specs = P("az", None, "range")
    return jax.shard_map(
        per_device, mesh=mesh, in_specs=in_specs, out_specs=out_specs, check_vma=False
    )
```

```python
import math

import jax
import jax.numpy as jnp
from jax import lax
from jax.experimental import pallas as pl
from jax.experimental.pallas import tpu as pltpu
from jax.sharding import PartitionSpec as P

TIME_SLOTS = 16384
SIDE = 128
BEAMS = 8
SLOTS = 8
GROUP = 16
HALF = 8
PIECES = 4
VMEM_LIMIT = 56 * 1024 * 1024
EARLY_ORDER = (1, 0, 3, 2, 7, 6, 5, 4)
LATE_ORDER = (8, 9, 14, 15, 10, 11, 12, 13)
SIDE_AZ = 4
MESH = pl.DeviceIdType.MESH
F32 = jnp.float32
BF16 = jnp.bfloat16


def iota(shape, dim):
    return lax.broadcasted_iota(jnp.int32, shape, dim)


def cos_sin(turns):
    x = (turns - jnp.round(turns)) * math.pi
    y = x * x
    s = -1.0 / 39916800 * y + 1.0 / 362880
    s = s * y - 1.0 / 5040
    s = s * y + 1.0 / 120
    s = s * y - 1.0 / 6
    s = (s * y + 1.0) * x
    c = 1.0 / 479001600 * y - 1.0 / 3628800
    c = c * y + 1.0 / 40320
    c = c * y - 1.0 / 720
    c = c * y + 1.0 / 24
    c = c * y - 0.5
    c = c * y + 1.0
    return 1.0 - 2.0 * s * s, 2.0 * s * c


def split(x):
    hi = x.astype(BF16)
    return hi, (x - hi.astype(F32)).astype(BF16)


def dot(a, b):
    return jnp.dot(a, b, preferred_element_type=F32)


def blocks(a, b, c, d):
    return jnp.concatenate(
        [jnp.concatenate([a, b], axis=1), jnp.concatenate([c, d], axis=1)], axis=0
    )


def dft_tables():
    row, col = iota((SIDE, SIDE), 0), iota((SIDE, SIDE), 1)
    c, s = cos_sin(((row * col) & (SIDE - 1)).astype(F32) * (1.0 / SIDE))
    left = split(blocks(c, -s, s, c))
    right = split(blocks(c, s, -s, c))
    twist = cos_sin((row * col).astype(F32) * (1.0 / TIME_SLOTS))
    return left, right, twist


def prefix_tables():
    row, col = iota((SIDE, SIDE), 0), iota((SIDE, SIDE), 1)
    upper = jnp.where(row < col, 1.0, 0.0).astype(F32)
    ones = jnp.ones((SIDE, SIDE), F32)
    lower = jnp.where(col < row, 1.0, 0.0).astype(F32)
    inner = blocks(upper, ones, upper, ones).astype(BF16)
    outer = jnp.concatenate([lower, lower], axis=1).astype(BF16)
    return inner, outer


def as_column(rows, lane):
    return jnp.sum(jnp.where(iota(rows.shape, 1) == lane, rows, 0.0), axis=1, keepdims=True)


def as_row(column):
    row, col = iota((SIDE, SIDE), 0), iota((SIDE, SIDE), 1)
    wide = jnp.broadcast_to(column, (SIDE, SIDE))
    return jnp.sum(jnp.where(row == col, wide, 0.0), axis=0, keepdims=True)


def phase_tables(delay, frac, amp):
    delay, frac, amp = [jnp.concatenate([v, v], axis=0) for v in (delay, frac, amp)]
    row, col = iota((SIDE, SIDE), 0), iota((SIDE, SIDE), 1)
    whole = (col * delay.astype(jnp.int32)) & (TIME_SLOTS - 1)
    c, s = cos_sin((whole.astype(F32) + col.astype(F32) * frac) * (1.0 / TIME_SLOTS))
    inner = jnp.where(row < SIDE // 2, c, s) * amp
    near_row = (row & SLOTS) == 0
    right = split(
        jnp.concatenate([jnp.where(near_row, inner, 0.0), jnp.where(near_row, 0.0, inner)], axis=1)
    )
    signed = row - jnp.where(row >= SIDE // 2, SIDE, 0)
    whole = (signed * as_row(delay).astype(jnp.int32)) & (SIDE - 1)
    c, s = cos_sin((whole.astype(F32) + signed.astype(F32) * as_row(frac)) * (1.0 / SIDE))
    cosines = col < SIDE // 2
    hi, lo = split(jnp.concatenate([jnp.where(cosines, c, -s), jnp.where(cosines, -s, -c)], axis=0))
    return jnp.concatenate([hi, hi, lo], axis=1), right


def spectrum(left, right, column):
    mine = ((iota((SIDE, 2 * SIDE), 0) & (SIDE // 2 - 1)) >> 4) == column
    hi, lo = [jnp.where(mine, x.astype(F32), 0.0).astype(BF16) for x in right]
    return dot(left, jnp.concatenate([hi, lo, hi], axis=0))


def side_by_side(*parts):
    return jnp.concatenate(parts, axis=1)


def stacked(*parts):
    return jnp.concatenate(parts, axis=0)


def group_histogram(specs, pulses, ambients, left, right, twist, inner, outer):
    count = len(specs)
    rows = []
    for spec, (pulse_real, pulse_imag) in zip(specs, pulses):
        real, imag = spec[:SIDE], spec[SIDE:]
        wide_real, wide_imag = side_by_side(pulse_real, pulse_real), side_by_side(pulse_imag, pulse_imag)
        hi, lo = split(stacked(wide_real * real - wide_imag * imag, wide_real * imag + wide_imag * real))
        section = dot(left, stacked(hi, lo, hi))
        for trip in range(2):
            real = section[:SIDE, trip * SIDE : (trip + 1) * SIDE]
            imag = section[SIDE:, trip * SIDE : (trip + 1) * SIDE]
            rows.append(side_by_side(real * twist[0] - imag * twist[1], real * twist[1] + imag * twist[0]))
    hi, lo = split(stacked(*rows))
    field = dot(side_by_side(hi, lo, hi), right)
    fluxes = []
    for j in range(count):
        power = field[2 * SIDE * j : 2 * SIDE * (j + 1)]
        power = power * power
        power = power[:SIDE] + power[SIDE:]
        power = power[:, :SIDE] + power[:, SIDE:]
        fluxes.append(jnp.transpose((power * (1.0 / TIME_SLOTS) + ambients[j]) * (1.0 / TIME_SLOTS)))
    flux = stacked(*fluxes)
    hi, lo = split(flux)
    sums = dot(side_by_side(hi, lo), inner)
    hi, lo = split(side_by_side(*[sums[SIDE * j : SIDE * (j + 1), SIDE:] for j in range(count)]))
    carried = dot(outer, stacked(hi, lo))
    before = stacked(
        *[sums[SIDE * j : SIDE * (j + 1), :SIDE] + carried[:, SIDE * j : SIDE * (j + 1)] for j in range(count)]
    )
    series = 1.0 - flux * 0.25
    series = 1.0 - flux * (1.0 / 3) * series
    series = 1.0 - flux * 0.5 * series
    detected = jnp.where(flux < 1.0 / 32, flux * series, 1.0 - jnp.exp(-flux))
    return TIME_SLOTS * detected * jnp.exp(-before)


def kernel(
    lag_hbm, frac_hbm, amp_hbm, packed_hbm, ambient_hbm, pulse_hbm,
    arrived,
    lag_ref, frac_ref, amp_ref, packed_ref, ambient_ref, pulse_ref,
    own, gathered, extra, left_tab, right_tab, twist_tab, inner_tab, outer_tab,
    ready,
    in_sem, keep_sem, extra_send, extra_recv, pulse_send, pulse_recv, hist_send, hist_recv, go_sem, near_sem,
):
    me_range, me_az = lax.axis_index("range"), lax.axis_index("az")
    y, x = me_az // SIDE_AZ, lax.rem(me_az, SIDE_AZ)
    chief = GROUP - 1
    early = me_range < HALF
    late = jnp.logical_not(early)
    partner = lax.rem(me_range + HALF, GROUP)

    def remote(src, dst, send, recv, **where):
        return pltpu.make_async_remote_copy(
            src_ref=src, dst_ref=dst, send_sem=send, recv_sem=recv, device_id=where, device_id_type=MESH
        )

    fetches = [
        pltpu.make_async_copy(src, dst, in_sem.at[i])
        for i, (src, dst) in enumerate(
            (
                (pulse_hbm, pulse_ref), (lag_hbm, lag_ref), (frac_hbm, frac_ref), (amp_hbm, amp_ref),
                (packed_hbm, packed_ref), (ambient_hbm, ambient_ref),
            )
        )
    ]
    for fetch in fetches:
        fetch.start()

    barrier = pltpu.get_barrier_semaphore()

    def greet(k, carry):
        pl.semaphore_signal(
            barrier, inc=1, device_id={"az": lax.rem(me_az + k, GROUP)}, device_id_type=MESH
        )
        return carry

    lax.fori_loop(1, GROUP, greet, 0)

    @pl.when(me_range != chief)
    def _():
        pl.semaphore_signal(barrier, inc=1, device_id={"range": chief}, device_id_type=MESH)

    @pl.when(early)
    def _():
        pl.semaphore_signal(barrier, inc=1, device_id={"range": partner}, device_id_type=MESH)

    fetches[0].wait()
    for b in range(BEAMS):
        for part in range(2):
            for q in range(8):
                own[b % 2, b // 2, part, q : q + 1, :] = pulse_ref[b, part : part + 1, q * SIDE : (q + 1) * SIDE]
    for fetch in fetches[1:]:
        fetch.wait()
    first = me_range * BEAMS
    delay = (lag_ref[0] + (packed_ref[...] >> 4)).astype(F32)
    live = iota((SLOTS, SIDE), 0) < (packed_ref[...] & 15)
    amp = jnp.where(live, amp_ref[0], 0.0)
    delay, frac, amp = [
        pltpu.roll(v, lax.rem(2 * SIDE + BEAMS * i - first, SIDE), 1)
        for i, v in enumerate((delay, frac_ref[0], amp))
    ]
    lane = iota((SLOTS, SIDE), 1) & (SIDE // 2 - 1)
    echo = jnp.where(lane < BEAMS, delay, jnp.where(lane < 2 * BEAMS, frac, amp))
    for b in range(SIDE_AZ):
        own[0, b, 2] = echo

    pl.semaphore_wait(
        barrier,
        GROUP - 1 + jnp.where(early, 0, 1) + jnp.where(me_range == chief, GROUP - 1, 0),
    )
    parts = pl.ds(0, 2)
    extra_copy = remote(own.at[1, :, parts], extra, extra_send, extra_recv, range=partner)

    @pl.when(late)
    def _():
        extra_copy.start()

    def share(k, carry):
        peer = lax.rem(me_az + k, GROUP)
        mine = own.at[0, lax.rem(peer, SIDE_AZ)]
        remote(mine, gathered.at[0, me_az], pulse_send, pulse_recv.at[0], az=peer).start()
        return carry

    def share_next(k, carry):
        peer = lax.rem(me_az + k, GROUP)
        mine = own.at[1, lax.rem(peer, SIDE_AZ), parts]
        remote(mine, gathered.at[1, me_az, parts], pulse_send, pulse_recv.at[1], az=peer).start()
        return carry

    def share_extra(k, carry):
        peer = lax.rem(me_az + k, GROUP)
        mine = extra.at[lax.rem(peer, SIDE_AZ)]
        remote(mine, gathered.at[2, me_az, parts], pulse_send, pulse_recv.at[2], az=peer).start()
        return carry

    lax.fori_loop(1, GROUP, share, 0)
    lax.fori_loop(1, GROUP, share_next, 0)

    @pl.when(me_range == chief)
    def _():
        def tell(k, carry):
            pl.semaphore_signal(go_sem, inc=1, device_id={"range": k}, device_id_type=MESH)
            return carry

        lax.fori_loop(0, GROUP - 1, tell, 0)

    gathered[0, me_az] = own[0, x]
    gathered[1, me_az] = own[1, x]

    left, right, twist = dft_tables()
    left_tab[...] = side_by_side(left[0], left[0], left[1])
    right_tab[...] = stacked(right[0], right[0], right[1])
    twist_tab[0], twist_tab[1] = twist
    inner_tab[...], outer_tab[...] = prefix_tables()

    @pl.when(me_range != chief)
    def _():
        pl.semaphore_wait(go_sem, 1)

    for k in range(1, SIDE_AZ):
        pl.semaphore_signal(
            near_sem, inc=1, device_id={"az": y * SIDE_AZ + lax.rem(x + k, SIDE_AZ)}, device_id_type=MESH
        )

    some = gathered.at[0, pl.ds(0, GROUP - 1)]
    remote(some, some, pulse_send, pulse_recv.at[0], az=me_az).wait_recv()
    def phases(j):
        rows = []
        for i in range(SIDE_AZ):
            rows.append(gathered[0, y * SIDE_AZ + i, 2])
            rows.append(gathered[0, lax.rem(y * SIDE_AZ + i + GROUP - 1, GROUP), 2])
        rows = stacked(*rows)
        place = 2 * x + jnp.where(j == 0, 0, 1) + jnp.where(j == 2, SIDE // 2, 0)
        delay, frac, amp = [as_column(rows, place + BEAMS * i) for i in range(3)]
        far = (iota(delay.shape, 0) & SLOTS) != 0
        return phase_tables(delay, frac, jnp.where(far == (delay >= TIME_SLOTS), amp, 0.0))

    def tiles_of(row, count):
        return pl.ds(pl.multiple_of(row * 8, 8), count * 8)

    def tiles(ref, row, count):
        return ref.at[tiles_of(row, count)]

    def beam_of(j):
        block = jnp.where(j == 2, partner, me_range)
        return block * BEAMS + 2 * x + jnp.where(j == 0, 0, 1)

    def send_tile(j, i, peer):
        @pl.when((peer != me_range) | (i != x))
        def _():
            remote(
                tiles(ready, (j * SIDE_AZ + i) * GROUP + peer, 1),
                tiles(arrived, beam_of(j), 1),
                hist_send, hist_recv, range=peer, az=y * SIDE_AZ + i,
            ).start()

    def send_tiles(j, order):
        for peer in order:
            for k in range(SIDE_AZ):
                send_tile(j, lax.rem(x + k, SIDE_AZ), peer)

    def work(j, carry):
        @pl.when(j > 0)
        def _():
            some = gathered.at[1, pl.ds(0, GROUP - 1), parts]
            remote(some, some, pulse_send, pulse_recv.at[j], az=me_az).wait_recv()

        e_left, e_right = phases(j)
        specs = [spectrum(e_left, e_right, i) for i in range(SIDE_AZ)]
        pulse = [gathered[j, :, part].reshape(SIDE, SIDE) for part in range(2)]
        mine = iota((1, SIDE), 1) == beam_of(j)
        ambient = jnp.sum(jnp.where(mine, ambient_ref[...], 0.0), axis=1, keepdims=True)
        hist = group_histogram(
            specs, [pulse] * SIDE_AZ, [ambient] * SIDE_AZ, left_tab[...], right_tab[...],
            (twist_tab[0], twist_tab[1]), inner_tab[...], outer_tab[...],
        )
        ready[tiles_of(j * SIDE_AZ * GROUP, SIDE_AZ * GROUP), :] = hist

        @pl.when(j == 0)
        def _():
            pl.semaphore_wait(near_sem, SIDE_AZ - 1)

        @pl.when(early & (j == 0))
        def _():
            extra_copy.wait_recv()
            lax.fori_loop(1, GROUP, share_extra, 0)
            gathered[2, me_az, :2] = extra[x]

        @pl.when(early | (j == 0))
        def _():
            send_tiles(j, EARLY_ORDER)

        @pl.when(j == 0)
        def _():
            send_tiles(0, LATE_ORDER)

        @pl.when((j == jnp.where(early, 2, 1)))
        def _():
            send_tiles(1, LATE_ORDER)

        return carry

    lax.fori_loop(0, jnp.where(early, 3, 2), work, 0)

    def keep(j):
        return pltpu.make_async_copy(
            tiles(ready, (j * SIDE_AZ + x) * GROUP + me_range, 1), tiles(arrived, beam_of(j), 1),
            keep_sem.at[j],
        )

    def settled(ref, send, recv, count):
        some = tiles(ref, 0, count)
        return remote(some, some, send, recv, az=me_az)

    keep(0).start()
    keep(1).start()

    @pl.when(early)
    def _():
        keep(2).start()
        settled(arrived, hist_send, hist_recv, GROUP * BEAMS - 3).wait_recv()
        keep(2).wait()

    @pl.when(late)
    def _():
        settled(arrived, hist_send, hist_recv, GROUP * BEAMS - 2).wait_recv()

    keep(0).wait()
    keep(1).wait()

    some = gathered.at[0, pl.ds(0, GROUP - 1)]
    remote(some, some, pulse_send, pulse_recv.at[0], az=me_az).wait_send()
    some = gathered.at[1, pl.ds(0, GROUP - 1), parts]
    remote(some, some, pulse_send, pulse_recv.at[1], az=me_az).wait_send()
    tiles_all, tiles_half = SIDE_AZ * GROUP - 1, SIDE_AZ * HALF - 1

    @pl.when(early)
    def _():
        remote(some, some, pulse_send, pulse_recv.at[1], az=me_az).wait_send()
        settled(ready, hist_send, hist_recv, 2 * tiles_all + tiles_half).wait_send()

    @pl.when(late)
    def _():
        extra_copy.wait_send()
        settled(ready, hist_send, hist_recv, tiles_all + tiles_half).wait_send()


def spread(arrived, out_ref, tiles, rows, in_sem, out_sem):
    step = GROUP * BEAMS // PIECES
    fetches = [
        pltpu.make_async_copy(
            arrived.at[pl.ds(k * step * 8, step * 8)], tiles.at[pl.ds(k * step * 8, step * 8)], in_sem.at[k]
        )
        for k in range(PIECES)
    ]
    for fetch in fetches:
        fetch.start()
    stores = []
    for k, fetch in enumerate(fetches):
        fetch.wait()
        for g in range(k * step // 8, (k + 1) * step // 8):
            for s in range(8):
                rows[0, g * 8 : (g + 1) * 8, s * SIDE : (s + 1) * SIDE] = tiles[
                    pl.ds(g * 64 + s, 8, stride=8), :
                ]
        some = pl.ds(k * step, step)
        stores.append(pltpu.make_async_copy(rows.at[:, some], out_ref.at[:, some], out_sem.at[k]))
        stores[-1].start()
    for store in stores:
        store.wait()


def per_device(lag, frac, amp, offset, count, ambient, pulse):
    lag, frac, amp = [jnp.swapaxes(v, 1, 2) for v in (lag, frac, amp)]
    hbm = pl.BlockSpec(memory_space=pltpu.HBM)
    dma = pltpu.SemaphoreType.DMA
    arrived = pl.pallas_call(
        kernel,
        out_shape=jax.ShapeDtypeStruct((GROUP * BEAMS * 8, SIDE), F32),
        in_specs=[hbm] * 6,
        out_specs=hbm,
        scratch_shapes=[
            pltpu.VMEM((1, SLOTS, SIDE), jnp.int32),
            pltpu.VMEM((1, SLOTS, SIDE), F32),
            pltpu.VMEM((1, SLOTS, SIDE), F32),
            pltpu.VMEM((1, 1), jnp.int32),
            pltpu.VMEM((1, SIDE), F32),
            pltpu.VMEM((BEAMS, 2, TIME_SLOTS // GROUP), F32),
            pltpu.VMEM((2, SIDE_AZ, 3, 8, SIDE), F32),
            pltpu.VMEM((3, GROUP, 3, 8, SIDE), F32),
            pltpu.VMEM((SIDE_AZ, 2, 8, SIDE), F32),
            pltpu.VMEM((2 * SIDE, 6 * SIDE), BF16),
            pltpu.VMEM((6 * SIDE, 2 * SIDE), BF16),
            pltpu.VMEM((2, SIDE, SIDE), F32),
            pltpu.VMEM((2 * SIDE, 2 * SIDE), BF16),
            pltpu.VMEM((SIDE, 2 * SIDE), BF16),
            pltpu.VMEM((3 * SIDE_AZ * SIDE, SIDE), F32),
            dma((6,)), dma((3,)), dma, dma, dma, dma((3,)), dma, dma,
            pltpu.SemaphoreType.REGULAR, pltpu.SemaphoreType.REGULAR,
        ],
        compiler_params=pltpu.CompilerParams(
            collective_id=0, has_side_effects=True, vmem_limit_bytes=VMEM_LIMIT
        ),
    )(lag, frac, amp, (offset * 16 + count).reshape(1, 1), ambient.reshape(1, SIDE), pulse)
    return pl.pallas_call(
        spread,
        out_shape=jax.ShapeDtypeStruct((1, GROUP * BEAMS, TIME_SLOTS // GROUP), F32),
        in_specs=[hbm],
        out_specs=hbm,
        scratch_shapes=[
            pltpu.VMEM((GROUP * BEAMS * 8, SIDE), F32),
            pltpu.VMEM((1, GROUP * BEAMS, TIME_SLOTS // GROUP), F32),
            dma((PIECES,)), dma((PIECES,)),
        ],
        compiler_params=pltpu.CompilerParams(vmem_limit_bytes=VMEM_LIMIT),
    )(arrived)


def solution(mesh):
    in_specs = (
        P("az", None, None),
        P("az", None, None),
        P("az", None, None),
        P("az"),
        P("az"),
        P(),
        P("range", None, "az"),
    )
    out_specs = P("az", None, "range")
    return jax.shard_map(
        per_device, mesh=mesh, in_specs=in_specs, out_specs=out_specs, check_vma=False
    )
```

```python
import math

import jax
import jax.numpy as jnp
from jax import lax
from jax.experimental import pallas as pl
from jax.experimental.pallas import tpu as pltpu
from jax.sharding import PartitionSpec as P

TIME_SLOTS = 16384
SIDE = 128
BEAMS = 8
SLOTS = 8
GROUP = 16
HALF = 8
FAR_FIRST = (10, 6, 9, 11, 14, 2, 8, 5, 7, 13, 15, 1, 3, 4, 12)
PIECES = 4
VMEM_LIMIT = 56 * 1024 * 1024
EARLY_ORDER = (1, 0, 3, 2, 7, 6, 5, 4)
LATE_ORDER = (8, 9, 14, 15, 10, 11, 12, 13)
SIDE_AZ = 4
MESH = pl.DeviceIdType.MESH
F32 = jnp.float32
BF16 = jnp.bfloat16


def iota(shape, dim):
    return lax.broadcasted_iota(jnp.int32, shape, dim)


def cos_sin(turns):
    x = (turns - jnp.round(turns)) * math.pi
    y = x * x
    s = -1.0 / 39916800 * y + 1.0 / 362880
    s = s * y - 1.0 / 5040
    s = s * y + 1.0 / 120
    s = s * y - 1.0 / 6
    s = (s * y + 1.0) * x
    c = 1.0 / 479001600 * y - 1.0 / 3628800
    c = c * y + 1.0 / 40320
    c = c * y - 1.0 / 720
    c = c * y + 1.0 / 24
    c = c * y - 0.5
    c = c * y + 1.0
    return 1.0 - 2.0 * s * s, 2.0 * s * c


def split(x):
    hi = x.astype(BF16)
    return hi, (x - hi.astype(F32)).astype(BF16)


def dot(a, b):
    return jnp.dot(a, b, preferred_element_type=F32)


def blocks(a, b, c, d):
    return jnp.concatenate(
        [jnp.concatenate([a, b], axis=1), jnp.concatenate([c, d], axis=1)], axis=0
    )


def dft_tables():
    row, col = iota((SIDE, SIDE), 0), iota((SIDE, SIDE), 1)
    c, s = cos_sin(((row * col) & (SIDE - 1)).astype(F32) * (1.0 / SIDE))
    left = split(blocks(c, -s, s, c))
    right = split(blocks(c, s, -s, c))
    twist = cos_sin((row * col).astype(F32) * (1.0 / TIME_SLOTS))
    return left, right, twist


def prefix_tables():
    row, col = iota((SIDE, SIDE), 0), iota((SIDE, SIDE), 1)
    upper = jnp.where(row < col, 1.0, 0.0).astype(F32)
    ones = jnp.ones((SIDE, SIDE), F32)
    lower = jnp.where(col < row, 1.0, 0.0).astype(F32)
    inner = blocks(upper, ones, upper, ones).astype(BF16)
    outer = jnp.concatenate([lower, lower], axis=1).astype(BF16)
    return inner, outer


def as_column(rows, lane):
    return jnp.sum(jnp.where(iota(rows.shape, 1) == lane, rows, 0.0), axis=1, keepdims=True)


def as_row(column):
    row, col = iota((SIDE, SIDE), 0), iota((SIDE, SIDE), 1)
    wide = jnp.broadcast_to(column, (SIDE, SIDE))
    return jnp.sum(jnp.where(row == col, wide, 0.0), axis=0, keepdims=True)


def phase_tables(delay, frac, amp):
    delay, frac, amp = [jnp.concatenate([v, v], axis=0) for v in (delay, frac, amp)]
    row, col = iota((SIDE, SIDE), 0), iota((SIDE, SIDE), 1)
    whole = (col * delay.astype(jnp.int32)) & (TIME_SLOTS - 1)
    c, s = cos_sin((whole.astype(F32) + col.astype(F32) * frac) * (1.0 / TIME_SLOTS))
    inner = jnp.where(row < SIDE // 2, c, s) * amp
    near_row = (row & SLOTS) == 0
    right = split(
        jnp.concatenate([jnp.where(near_row, inner, 0.0), jnp.where(near_row, 0.0, inner)], axis=1)
    )
    signed = row - jnp.where(row >= SIDE // 2, SIDE, 0)
    whole = (signed * as_row(delay).astype(jnp.int32)) & (SIDE - 1)
    c, s = cos_sin((whole.astype(F32) + signed.astype(F32) * as_row(frac)) * (1.0 / SIDE))
    cosines = col < SIDE // 2
    hi, lo = split(jnp.concatenate([jnp.where(cosines, c, -s), jnp.where(cosines, -s, -c)], axis=0))
    return jnp.concatenate([hi, hi, lo], axis=1), right


def spectrum(left, right, column):
    mine = ((iota((SIDE, 2 * SIDE), 0) & (SIDE // 2 - 1)) >> 4) == column
    hi, lo = [jnp.where(mine, x.astype(F32), 0.0).astype(BF16) for x in right]
    return dot(left, jnp.concatenate([hi, lo, hi], axis=0))


def side_by_side(*parts):
    return jnp.concatenate(parts, axis=1)


def stacked(*parts):
    return jnp.concatenate(parts, axis=0)


def group_histogram(specs, pulses, ambients, left, right, twist, inner, outer):
    count = len(specs)
    rows = []
    for spec, (pulse_real, pulse_imag) in zip(specs, pulses):
        real, imag = spec[:SIDE], spec[SIDE:]
        wide_real, wide_imag = side_by_side(pulse_real, pulse_real), side_by_side(pulse_imag, pulse_imag)
        hi, lo = split(stacked(wide_real * real - wide_imag * imag, wide_real * imag + wide_imag * real))
        section = dot(left, stacked(hi, lo, hi))
        for trip in range(2):
            real = section[:SIDE, trip * SIDE : (trip + 1) * SIDE]
            imag = section[SIDE:, trip * SIDE : (trip + 1) * SIDE]
            rows.append(side_by_side(real * twist[0] - imag * twist[1], real * twist[1] + imag * twist[0]))
    hi, lo = split(stacked(*rows))
    field = dot(side_by_side(hi, lo, hi), right)
    fluxes = []
    for j in range(count):
        power = field[2 * SIDE * j : 2 * SIDE * (j + 1)]
        power = power * power
        power = power[:SIDE] + power[SIDE:]
        power = power[:, :SIDE] + power[:, SIDE:]
        fluxes.append(jnp.transpose((power * (1.0 / TIME_SLOTS) + ambients[j]) * (1.0 / TIME_SLOTS)))
    flux = stacked(*fluxes)
    hi, lo = split(flux)
    sums = dot(side_by_side(hi, lo), inner)
    hi, lo = split(side_by_side(*[sums[SIDE * j : SIDE * (j + 1), SIDE:] for j in range(count)]))
    carried = dot(outer, stacked(hi, lo))
    before = stacked(
        *[sums[SIDE * j : SIDE * (j + 1), :SIDE] + carried[:, SIDE * j : SIDE * (j + 1)] for j in range(count)]
    )
    series = 1.0 - flux * 0.25
    series = 1.0 - flux * (1.0 / 3) * series
    series = 1.0 - flux * 0.5 * series
    detected = jnp.where(flux < 1.0 / 32, flux * series, 1.0 - jnp.exp(-flux))
    return TIME_SLOTS * detected * jnp.exp(-before)


def kernel(
    lag_hbm, frac_hbm, amp_hbm, packed_hbm, ambient_hbm, pulse_hbm,
    arrived,
    lag_ref, frac_ref, amp_ref, packed_ref, ambient_ref, pulse_ref,
    own, gathered, extra, spec, left_tab, right_tab, twist_tab, inner_tab, outer_tab,
    ready,
    in_sem, keep_sem, extra_send, extra_recv, pulse_send, pulse_recv, hist_send, hist_recv, go_sem, near_sem,
):
    me_range, me_az = lax.axis_index("range"), lax.axis_index("az")
    y, x = me_az // SIDE_AZ, lax.rem(me_az, SIDE_AZ)
    chief = GROUP - 1
    early = me_range < HALF
    late = jnp.logical_not(early)
    partner = lax.rem(me_range + HALF, GROUP)

    def remote(src, dst, send, recv, **where):
        return pltpu.make_async_remote_copy(
            src_ref=src, dst_ref=dst, send_sem=send, recv_sem=recv, device_id=where, device_id_type=MESH
        )

    fetches = [
        pltpu.make_async_copy(src, dst, in_sem.at[i])
        for i, (src, dst) in enumerate(
            (
                (pulse_hbm, pulse_ref), (lag_hbm, lag_ref), (frac_hbm, frac_ref), (amp_hbm, amp_ref),
                (packed_hbm, packed_ref), (ambient_hbm, ambient_ref),
            )
        )
    ]
    for fetch in fetches:
        fetch.start()

    barrier = pltpu.get_barrier_semaphore()

    def greet(k, carry):
        pl.semaphore_signal(
            barrier, inc=1, device_id={"az": lax.rem(me_az + k, GROUP)}, device_id_type=MESH
        )
        return carry

    lax.fori_loop(1, GROUP, greet, 0)

    @pl.when(me_range != chief)
    def _():
        pl.semaphore_signal(barrier, inc=1, device_id={"range": chief}, device_id_type=MESH)

    @pl.when(early)
    def _():
        pl.semaphore_signal(barrier, inc=1, device_id={"range": partner}, device_id_type=MESH)

    fetches[0].wait()
    for b in range(BEAMS):
        for part in range(2):
            for q in range(8):
                own[b % 2, b // 2, part, q : q + 1, :] = pulse_ref[b, part : part + 1, q * SIDE : (q + 1) * SIDE]
    for fetch in fetches[1:]:
        fetch.wait()
    first = me_range * BEAMS
    delay = (lag_ref[0] + (packed_ref[...] >> 4)).astype(F32)
    live = iota((SLOTS, SIDE), 0) < (packed_ref[...] & 15)
    amp = jnp.where(live, amp_ref[0], 0.0)
    delay, frac, amp = [
        pltpu.roll(v, lax.rem(2 * SIDE + BEAMS * i - first, SIDE), 1)
        for i, v in enumerate((delay, frac_ref[0], amp))
    ]
    lane = iota((SLOTS, SIDE), 1) & (SIDE // 2 - 1)
    echo = jnp.where(lane < BEAMS, delay, jnp.where(lane < 2 * BEAMS, frac, amp))
    for b in range(SIDE_AZ):
        own[0, b, 2] = echo

    pl.semaphore_wait(
        barrier,
        GROUP - 1 + jnp.where(early, 0, 1) + jnp.where(me_range == chief, GROUP - 1, 0),
    )
    parts = pl.ds(0, 2)
    extra_copy = remote(own.at[1, :, parts], extra, extra_send, extra_recv, range=partner)

    @pl.when(late)
    def _():
        extra_copy.start()

    def share(k, carry):
        peer = lax.rem(me_az + k, GROUP)
        mine = own.at[0, lax.rem(peer, SIDE_AZ)]
        remote(mine, gathered.at[0, me_az], pulse_send, pulse_recv.at[0], az=peer).start()
        return carry

    def share_next(k, carry):
        peer = lax.rem(me_az + k, GROUP)
        mine = own.at[1, lax.rem(peer, SIDE_AZ), parts]
        remote(mine, gathered.at[1, me_az, parts], pulse_send, pulse_recv.at[1], az=peer).start()
        return carry

    def share_extra(k, carry):
        peer = lax.rem(me_az + k, GROUP)
        mine = extra.at[lax.rem(peer, SIDE_AZ)]
        remote(mine, gathered.at[2, me_az, parts], pulse_send, pulse_recv.at[2], az=peer).start()
        return carry

    for k in FAR_FIRST:
        share(k, 0)
    for k in FAR_FIRST:
        share_next(k, 0)

    @pl.when(me_range == chief)
    def _():
        def tell(k, carry):
            pl.semaphore_signal(go_sem, inc=1, device_id={"range": k}, device_id_type=MESH)
            return carry

        lax.fori_loop(0, GROUP - 1, tell, 0)

    gathered[0, me_az] = own[0, x]
    gathered[1, me_az] = own[1, x]

    left, right, twist = dft_tables()
    left_tab[...] = side_by_side(left[0], left[0], left[1])
    right_tab[...] = stacked(right[0], right[0], right[1])
    twist_tab[0], twist_tab[1] = twist
    inner_tab[...], outer_tab[...] = prefix_tables()

    @pl.when(me_range != chief)
    def _():
        pl.semaphore_wait(go_sem, 1)

    for k in range(1, SIDE_AZ):
        pl.semaphore_signal(
            near_sem, inc=1, device_id={"az": y * SIDE_AZ + lax.rem(x + k, SIDE_AZ)}, device_id_type=MESH
        )

    some = gathered.at[0, pl.ds(0, GROUP - 1)]
    remote(some, some, pulse_send, pulse_recv.at[0], az=me_az).wait_recv()
    def phases(j):
        rows = []
        for i in range(SIDE_AZ):
            rows.append(gathered[0, y * SIDE_AZ + i, 2])
            rows.append(gathered[0, lax.rem(y * SIDE_AZ + i + GROUP - 1, GROUP), 2])
        rows = stacked(*rows)
        place = 2 * x + jnp.where(j == 0, 0, 1) + jnp.where(j == 2, SIDE // 2, 0)
        delay, frac, amp = [as_column(rows, place + BEAMS * i) for i in range(3)]
        far = (iota(delay.shape, 0) & SLOTS) != 0
        return phase_tables(delay, frac, jnp.where(far == (delay >= TIME_SLOTS), amp, 0.0))

    def tiles_of(row, count):
        return pl.ds(pl.multiple_of(row * 8, 8), count * 8)

    def tiles(ref, row, count):
        return ref.at[tiles_of(row, count)]

    def beam_of(j):
        block = jnp.where(j == 2, partner, me_range)
        return block * BEAMS + 2 * x + jnp.where(j == 0, 0, 1)

    def send_tile(j, i, peer):
        @pl.when((peer != me_range) | (i != x))
        def _():
            remote(
                tiles(ready, (j * SIDE_AZ + i) * GROUP + peer, 1),
                tiles(arrived, beam_of(j), 1),
                hist_send, hist_recv, range=peer, az=y * SIDE_AZ + i,
            ).start()

    def send_tiles(j, order):
        for peer in order:
            for k in range(SIDE_AZ):
                send_tile(j, lax.rem(x + k, SIDE_AZ), peer)

    def work(j, carry):
        e_left, e_right = phases(j)
        for i in range(SIDE_AZ):
            spec[i] = spectrum(e_left, e_right, i)

        @pl.when(j > 0)
        def _():
            some = gathered.at[1, pl.ds(0, GROUP - 1), parts]
            remote(some, some, pulse_send, pulse_recv.at[j], az=me_az).wait_recv()

        specs = [spec[i] for i in range(SIDE_AZ)]
        pulse = [gathered[j, :, part].reshape(SIDE, SIDE) for part in range(2)]
        mine = iota((1, SIDE), 1) == beam_of(j)
        ambient = jnp.sum(jnp.where(mine, ambient_ref[...], 0.0), axis=1, keepdims=True)
        hist = group_histogram(
            specs, [pulse] * SIDE_AZ, [ambient] * SIDE_AZ, left_tab[...], right_tab[...],
            (twist_tab[0], twist_tab[1]), inner_tab[...], outer_tab[...],
        )
        ready[tiles_of(j * SIDE_AZ * GROUP, SIDE_AZ * GROUP), :] = hist

        @pl.when(j == 0)
        def _():
            pl.semaphore_wait(near_sem, SIDE_AZ - 1)

        @pl.when(early & (j == 0))
        def _():
            extra_copy.wait_recv()
            for k in FAR_FIRST:
                share_extra(k, 0)
            gathered[2, me_az, :2] = extra[x]

        @pl.when(early | (j == 0))
        def _():
            send_tiles(j, EARLY_ORDER)

        @pl.when(j == 0)
        def _():
            send_tiles(0, LATE_ORDER)

        @pl.when((j == jnp.where(early, 2, 1)))
        def _():
            send_tiles(1, LATE_ORDER)

        return carry

    lax.fori_loop(0, jnp.where(early, 3, 2), work, 0)

    def keep(j):
        return pltpu.make_async_copy(
            tiles(ready, (j * SIDE_AZ + x) * GROUP + me_range, 1), tiles(arrived, beam_of(j), 1),
            keep_sem.at[j],
        )

    def settled(ref, send, recv, count):
        some = tiles(ref, 0, count)
        return remote(some, some, send, recv, az=me_az)

    keep(0).start()
    keep(1).start()

    @pl.when(early)
    def _():
        keep(2).start()
        settled(arrived, hist_send, hist_recv, GROUP * BEAMS - 3).wait_recv()
        keep(2).wait()

    @pl.when(late)
    def _():
        settled(arrived, hist_send, hist_recv, GROUP * BEAMS - 2).wait_recv()

    keep(0).wait()
    keep(1).wait()

    some = gathered.at[0, pl.ds(0, GROUP - 1)]
    remote(some, some, pulse_send, pulse_recv.at[0], az=me_az).wait_send()
    some = gathered.at[1, pl.ds(0, GROUP - 1), parts]
    remote(some, some, pulse_send, pulse_recv.at[1], az=me_az).wait_send()
    tiles_all, tiles_half = SIDE_AZ * GROUP - 1, SIDE_AZ * HALF - 1

    @pl.when(early)
    def _():
        remote(some, some, pulse_send, pulse_recv.at[1], az=me_az).wait_send()
        settled(ready, hist_send, hist_recv, 2 * tiles_all + tiles_half).wait_send()

    @pl.when(late)
    def _():
        extra_copy.wait_send()
        settled(ready, hist_send, hist_recv, tiles_all + tiles_half).wait_send()


def spread(arrived, out_ref, tiles, rows, in_sem, out_sem):
    step = GROUP * BEAMS // PIECES
    fetches = [
        pltpu.make_async_copy(
            arrived.at[pl.ds(k * step * 8, step * 8)], tiles.at[pl.ds(k * step * 8, step * 8)], in_sem.at[k]
        )
        for k in range(PIECES)
    ]
    for fetch in fetches:
        fetch.start()
    stores = []
    for k, fetch in enumerate(fetches):
        fetch.wait()
        for g in range(k * step // 8, (k + 1) * step // 8):
            for s in range(8):
                rows[0, g * 8 : (g + 1) * 8, s * SIDE : (s + 1) * SIDE] = tiles[
                    pl.ds(g * 64 + s, 8, stride=8), :
                ]
        some = pl.ds(k * step, step)
        stores.append(pltpu.make_async_copy(rows.at[:, some], out_ref.at[:, some], out_sem.at[k]))
        stores[-1].start()
    for store in stores:
        store.wait()


def per_device(lag, frac, amp, offset, count, ambient, pulse):
    lag, frac, amp = [jnp.swapaxes(v, 1, 2) for v in (lag, frac, amp)]
    hbm = pl.BlockSpec(memory_space=pltpu.HBM)
    dma = pltpu.SemaphoreType.DMA
    arrived = pl.pallas_call(
        kernel,
        out_shape=jax.ShapeDtypeStruct((GROUP * BEAMS * 8, SIDE), F32),
        in_specs=[hbm] * 6,
        out_specs=hbm,
        scratch_shapes=[
            pltpu.VMEM((1, SLOTS, SIDE), jnp.int32),
            pltpu.VMEM((1, SLOTS, SIDE), F32),
            pltpu.VMEM((1, SLOTS, SIDE), F32),
            pltpu.VMEM((1, 1), jnp.int32),
            pltpu.VMEM((1, SIDE), F32),
            pltpu.VMEM((BEAMS, 2, TIME_SLOTS // GROUP), F32),
            pltpu.VMEM((2, SIDE_AZ, 3, 8, SIDE), F32),
            pltpu.VMEM((3, GROUP, 3, 8, SIDE), F32),
            pltpu.VMEM((SIDE_AZ, 2, 8, SIDE), F32),
            pltpu.VMEM((SIDE_AZ, 2 * SIDE, 2 * SIDE), F32),
            pltpu.VMEM((2 * SIDE, 6 * SIDE), BF16),
            pltpu.VMEM((6 * SIDE, 2 * SIDE), BF16),
            pltpu.VMEM((2, SIDE, SIDE), F32),
            pltpu.VMEM((2 * SIDE, 2 * SIDE), BF16),
            pltpu.VMEM((SIDE, 2 * SIDE), BF16),
            pltpu.VMEM((3 * SIDE_AZ * SIDE, SIDE), F32),
            dma((6,)), dma((3,)), dma, dma, dma, dma((3,)), dma, dma,
            pltpu.SemaphoreType.REGULAR, pltpu.SemaphoreType.REGULAR,
        ],
        compiler_params=pltpu.CompilerParams(
            collective_id=0, has_side_effects=True, vmem_limit_bytes=VMEM_LIMIT
        ),
    )(lag, frac, amp, (offset * 16 + count).reshape(1, 1), ambient.reshape(1, SIDE), pulse)
    return pl.pallas_call(
        spread,
        out_shape=jax.ShapeDtypeStruct((1, GROUP * BEAMS, TIME_SLOTS // GROUP), F32),
        in_specs=[hbm],
        out_specs=hbm,
        scratch_shapes=[
            pltpu.VMEM((GROUP * BEAMS * 8, SIDE), F32),
            pltpu.VMEM((1, GROUP * BEAMS, TIME_SLOTS // GROUP), F32),
            dma((PIECES,)), dma((PIECES,)),
        ],
        compiler_params=pltpu.CompilerParams(vmem_limit_bytes=VMEM_LIMIT),
    )(arrived)


def solution(mesh):
    in_specs = (
        P("az", None, None),
        P("az", None, None),
        P("az", None, None),
        P("az"),
        P("az"),
        P(),
        P("range", None, "az"),
    )
    out_specs = P("az", None, "range")
    return jax.shard_map(
        per_device, mesh=mesh, in_specs=in_specs, out_specs=out_specs, check_vma=False
    )
```

```python
import math

import jax
import jax.numpy as jnp
from jax import lax
from jax.experimental import pallas as pl
from jax.experimental.pallas import tpu as pltpu
from jax.sharding import PartitionSpec as P

TIME_SLOTS = 16384
SIDE = 128
BEAMS = 8
SLOTS = 8
GROUP = 16
HALF = 8
FAR_FIRST = (10, 6, 9, 11, 14, 2, 8, 5, 7, 13, 15, 1, 3, 4, 12)
PIECES = 4
VMEM_LIMIT = 56 * 1024 * 1024
EARLY_ORDER = (1, 0, 3, 2, 7, 6, 5, 4)
LATE_ORDER = (8, 9, 14, 15, 10, 11, 12, 13)
SIDE_AZ = 4
MESH = pl.DeviceIdType.MESH
F32 = jnp.float32
BF16 = jnp.bfloat16


def iota(shape, dim):
    return lax.broadcasted_iota(jnp.int32, shape, dim)


def cos_sin(turns):
    x = (turns - jnp.round(turns)) * math.pi
    y = x * x
    s = -1.0 / 39916800 * y + 1.0 / 362880
    s = s * y - 1.0 / 5040
    s = s * y + 1.0 / 120
    s = s * y - 1.0 / 6
    s = (s * y + 1.0) * x
    c = 1.0 / 479001600 * y - 1.0 / 3628800
    c = c * y + 1.0 / 40320
    c = c * y - 1.0 / 720
    c = c * y + 1.0 / 24
    c = c * y - 0.5
    c = c * y + 1.0
    return 1.0 - 2.0 * s * s, 2.0 * s * c


def split(x):
    hi = x.astype(BF16)
    return hi, (x - hi.astype(F32)).astype(BF16)


def dot(a, b):
    return jnp.dot(a, b, preferred_element_type=F32)


def blocks(a, b, c, d):
    return jnp.concatenate(
        [jnp.concatenate([a, b], axis=1), jnp.concatenate([c, d], axis=1)], axis=0
    )


def dft_tables():
    row, col = iota((SIDE, SIDE), 0), iota((SIDE, SIDE), 1)
    c, s = cos_sin(((row * col) & (SIDE - 1)).astype(F32) * (1.0 / SIDE))
    left = split(blocks(c, -s, s, c))
    right = split(blocks(c, s, -s, c))
    twist = cos_sin((row * col).astype(F32) * (1.0 / TIME_SLOTS))
    return left, right, twist


def prefix_tables():
    row, col = iota((SIDE, SIDE), 0), iota((SIDE, SIDE), 1)
    upper = jnp.where(row < col, 1.0, 0.0).astype(F32)
    ones = jnp.ones((SIDE, SIDE), F32)
    lower = jnp.where(col < row, 1.0, 0.0).astype(F32)
    inner = blocks(upper, ones, upper, ones).astype(BF16)
    outer = jnp.concatenate([lower, lower], axis=1).astype(BF16)
    return inner, outer


def as_column(rows, lane):
    return jnp.sum(jnp.where(iota(rows.shape, 1) == lane, rows, 0.0), axis=1, keepdims=True)


def as_row(column):
    row, col = iota((SIDE, SIDE), 0), iota((SIDE, SIDE), 1)
    wide = jnp.broadcast_to(column, (SIDE, SIDE))
    return jnp.sum(jnp.where(row == col, wide, 0.0), axis=0, keepdims=True)


def phase_tables(delay, frac, amp):
    delay, frac, amp = [jnp.concatenate([v, v], axis=0) for v in (delay, frac, amp)]
    row, col = iota((SIDE, SIDE), 0), iota((SIDE, SIDE), 1)
    whole = (col * delay.astype(jnp.int32)) & (TIME_SLOTS - 1)
    c, s = cos_sin((whole.astype(F32) + col.astype(F32) * frac) * (1.0 / TIME_SLOTS))
    inner = jnp.where(row < SIDE // 2, c, s) * amp
    near_row = (row & SLOTS) == 0
    right = split(
        jnp.concatenate([jnp.where(near_row, inner, 0.0), jnp.where(near_row, 0.0, inner)], axis=1)
    )
    signed = row - jnp.where(row >= SIDE // 2, SIDE, 0)
    whole = (signed * as_row(delay).astype(jnp.int32)) & (SIDE - 1)
    c, s = cos_sin((whole.astype(F32) + signed.astype(F32) * as_row(frac)) * (1.0 / SIDE))
    cosines = col < SIDE // 2
    hi, lo = split(jnp.concatenate([jnp.where(cosines, c, -s), jnp.where(cosines, -s, -c)], axis=0))
    return jnp.concatenate([hi, hi, lo], axis=1), right


def spectrum(left, right, column):
    mine = ((iota((SIDE, 2 * SIDE), 0) & (SIDE // 2 - 1)) >> 4) == column
    hi, lo = [jnp.where(mine, x.astype(F32), 0.0).astype(BF16) for x in right]
    return dot(left, jnp.concatenate([hi, lo, hi], axis=0))


def side_by_side(*parts):
    return jnp.concatenate(parts, axis=1)


def stacked(*parts):
    return jnp.concatenate(parts, axis=0)


def group_histogram(specs, pulses, ambients, left, right, twist, inner, outer):
    count = len(specs)
    rows = []
    for spec, (pulse_real, pulse_imag) in zip(specs, pulses):
        real, imag = spec[:SIDE], spec[SIDE:]
        wide_real, wide_imag = side_by_side(pulse_real, pulse_real), side_by_side(pulse_imag, pulse_imag)
        hi, lo = split(stacked(wide_real * real - wide_imag * imag, wide_real * imag + wide_imag * real))
        section = dot(left, stacked(hi, lo, hi))
        for trip in range(2):
            real = section[:SIDE, trip * SIDE : (trip + 1) * SIDE]
            imag = section[SIDE:, trip * SIDE : (trip + 1) * SIDE]
            rows.append(side_by_side(real * twist[0] - imag * twist[1], real * twist[1] + imag * twist[0]))
    hi, lo = split(stacked(*rows))
    field = dot(side_by_side(hi, lo, hi), right)
    fluxes = []
    for j in range(count):
        power = field[2 * SIDE * j : 2 * SIDE * (j + 1)]
        power = power * power
        power = power[:SIDE] + power[SIDE:]
        power = power[:, :SIDE] + power[:, SIDE:]
        fluxes.append(jnp.transpose((power * (1.0 / TIME_SLOTS) + ambients[j]) * (1.0 / TIME_SLOTS)))
    flux = stacked(*fluxes)
    hi, lo = split(flux)
    sums = dot(side_by_side(hi, lo), inner)
    hi, lo = split(side_by_side(*[sums[SIDE * j : SIDE * (j + 1), SIDE:] for j in range(count)]))
    carried = dot(outer, stacked(hi, lo))
    before = stacked(
        *[sums[SIDE * j : SIDE * (j + 1), :SIDE] + carried[:, SIDE * j : SIDE * (j + 1)] for j in range(count)]
    )
    series = 1.0 - flux * 0.25
    series = 1.0 - flux * (1.0 / 3) * series
    series = 1.0 - flux * 0.5 * series
    detected = jnp.where(flux < 1.0 / 32, flux * series, 1.0 - jnp.exp(-flux))
    return TIME_SLOTS * detected * jnp.exp(-before)


def kernel(
    lag_hbm, frac_hbm, amp_hbm, packed_hbm, ambient_hbm, pulse_hbm,
    arrived,
    lag_ref, frac_ref, amp_ref, packed_ref, ambient_ref, pulse_ref,
    own, gathered, extra, spec, left_tab, right_tab, twist_tab, inner_tab, outer_tab,
    ready,
    in_sem, keep_sem, extra_send, extra_recv, pulse_send, pulse_recv, hist_send, hist_recv, go_sem, near_sem,
):
    me_range, me_az = lax.axis_index("range"), lax.axis_index("az")
    y, x = me_az // SIDE_AZ, lax.rem(me_az, SIDE_AZ)
    chief = GROUP - 1
    early = me_range < HALF
    late = jnp.logical_not(early)
    partner = lax.rem(me_range + HALF, GROUP)

    def remote(src, dst, send, recv, **where):
        return pltpu.make_async_remote_copy(
            src_ref=src, dst_ref=dst, send_sem=send, recv_sem=recv, device_id=where, device_id_type=MESH
        )

    fetches = [
        pltpu.make_async_copy(src, dst, in_sem.at[i])
        for i, (src, dst) in enumerate(
            (
                (pulse_hbm, pulse_ref), (lag_hbm, lag_ref), (frac_hbm, frac_ref), (amp_hbm, amp_ref),
                (packed_hbm, packed_ref), (ambient_hbm, ambient_ref),
            )
        )
    ]
    for fetch in fetches:
        fetch.start()

    barrier = pltpu.get_barrier_semaphore()

    def greet(k, carry):
        pl.semaphore_signal(
            barrier, inc=1, device_id={"az": lax.rem(me_az + k, GROUP)}, device_id_type=MESH
        )
        return carry

    lax.fori_loop(1, GROUP, greet, 0)

    @pl.when(me_range != chief)
    def _():
        pl.semaphore_signal(barrier, inc=1, device_id={"range": chief}, device_id_type=MESH)

    @pl.when(early)
    def _():
        pl.semaphore_signal(barrier, inc=1, device_id={"range": partner}, device_id_type=MESH)

    fetches[0].wait()
    for b in range(BEAMS):
        for part in range(2):
            for q in range(8):
                own[b % 2, b // 2, part, q : q + 1, :] = pulse_ref[b, part : part + 1, q * SIDE : (q + 1) * SIDE]
    for fetch in fetches[1:]:
        fetch.wait()
    first = me_range * BEAMS
    delay = (lag_ref[0] + (packed_ref[...] >> 4)).astype(F32)
    live = iota((SLOTS, SIDE), 0) < (packed_ref[...] & 15)
    amp = jnp.where(live, amp_ref[0], 0.0)
    delay, frac, amp = [
        pltpu.roll(v, lax.rem(2 * SIDE + BEAMS * i - first, SIDE), 1)
        for i, v in enumerate((delay, frac_ref[0], amp))
    ]
    lane = iota((SLOTS, SIDE), 1) & (SIDE // 2 - 1)
    echo = jnp.where(lane < BEAMS, delay, jnp.where(lane < 2 * BEAMS, frac, amp))
    for b in range(SIDE_AZ):
        own[0, b, 2] = echo

    pl.semaphore_wait(
        barrier,
        GROUP - 1 + jnp.where(early, 0, 1) + jnp.where(me_range == chief, GROUP - 1, 0),
    )

    @pl.when(me_range == chief)
    def _():
        def tell(k, carry):
            pl.semaphore_signal(go_sem, inc=1, device_id={"range": k}, device_id_type=MESH)
            return carry

        lax.fori_loop(0, GROUP - 1, tell, 0)

    parts = pl.ds(0, 2)
    extra_copy = remote(own.at[1, :, parts], extra, extra_send, extra_recv, range=partner)

    @pl.when(late)
    def _():
        extra_copy.start()

    def share(k, carry):
        peer = lax.rem(me_az + k, GROUP)
        mine = own.at[0, lax.rem(peer, SIDE_AZ)]
        remote(mine, gathered.at[0, me_az], pulse_send, pulse_recv.at[0], az=peer).start()
        return carry

    def share_next(k, carry):
        peer = lax.rem(me_az + k, GROUP)
        mine = own.at[1, lax.rem(peer, SIDE_AZ), parts]
        remote(mine, gathered.at[1, me_az, parts], pulse_send, pulse_recv.at[1], az=peer).start()
        return carry

    def share_extra(k, carry):
        peer = lax.rem(me_az + k, GROUP)
        mine = extra.at[lax.rem(peer, SIDE_AZ)]
        remote(mine, gathered.at[2, me_az, parts], pulse_send, pulse_recv.at[2], az=peer).start()
        return carry

    for k in FAR_FIRST:
        share(k, 0)
    for k in FAR_FIRST:
        share_next(k, 0)

    gathered[0, me_az] = own[0, x]
    gathered[1, me_az] = own[1, x]

    left, right, twist = dft_tables()
    left_tab[...] = side_by_side(left[0], left[0], left[1])
    right_tab[...] = stacked(right[0], right[0], right[1])
    twist_tab[0], twist_tab[1] = twist
    inner_tab[...], outer_tab[...] = prefix_tables()

    @pl.when(me_range != chief)
    def _():
        pl.semaphore_wait(go_sem, 1)

    for k in range(1, SIDE_AZ):
        pl.semaphore_signal(
            near_sem, inc=1, device_id={"az": y * SIDE_AZ + lax.rem(x + k, SIDE_AZ)}, device_id_type=MESH
        )

    some = gathered.at[0, pl.ds(0, GROUP - 1)]
    remote(some, some, pulse_send, pulse_recv.at[0], az=me_az).wait_recv()
    def phases(j):
        rows = []
        for i in range(SIDE_AZ):
            rows.append(gathered[0, y * SIDE_AZ + i, 2])
            rows.append(gathered[0, lax.rem(y * SIDE_AZ + i + GROUP - 1, GROUP), 2])
        rows = stacked(*rows)
        place = 2 * x + jnp.where(j == 0, 0, 1) + jnp.where(j == 2, SIDE // 2, 0)
        delay, frac, amp = [as_column(rows, place + BEAMS * i) for i in range(3)]
        far = (iota(delay.shape, 0) & SLOTS) != 0
        return phase_tables(delay, frac, jnp.where(far == (delay >= TIME_SLOTS), amp, 0.0))

    def tiles_of(row, count):
        return pl.ds(pl.multiple_of(row * 8, 8), count * 8)

    def tiles(ref, row, count):
        return ref.at[tiles_of(row, count)]

    def beam_of(j):
        block = jnp.where(j == 2, partner, me_range)
        return block * BEAMS + 2 * x + jnp.where(j == 0, 0, 1)

    def send_tile(j, i, peer):
        @pl.when((peer != me_range) | (i != x))
        def _():
            remote(
                tiles(ready, (j * SIDE_AZ + i) * GROUP + peer, 1),
                tiles(arrived, beam_of(j), 1),
                hist_send, hist_recv, range=peer, az=y * SIDE_AZ + i,
            ).start()

    def send_tiles(j, order):
        for peer in order:
            for k in range(SIDE_AZ):
                send_tile(j, lax.rem(x + k, SIDE_AZ), peer)

    def work(j, carry):
        e_left, e_right = phases(j)
        for i in range(SIDE_AZ):
            spec[i] = spectrum(e_left, e_right, i)

        @pl.when(j > 0)
        def _():
            some = gathered.at[1, pl.ds(0, GROUP - 1), parts]
            remote(some, some, pulse_send, pulse_recv.at[j], az=me_az).wait_recv()

        specs = [spec[i] for i in range(SIDE_AZ)]
        pulse = [gathered[j, :, part].reshape(SIDE, SIDE) for part in range(2)]
        mine = iota((1, SIDE), 1) == beam_of(j)
        ambient = jnp.sum(jnp.where(mine, ambient_ref[...], 0.0), axis=1, keepdims=True)
        hist = group_histogram(
            specs, [pulse] * SIDE_AZ, [ambient] * SIDE_AZ, left_tab[...], right_tab[...],
            (twist_tab[0], twist_tab[1]), inner_tab[...], outer_tab[...],
        )
        ready[tiles_of(j * SIDE_AZ * GROUP, SIDE_AZ * GROUP), :] = hist

        @pl.when(j == 0)
        def _():
            pl.semaphore_wait(near_sem, SIDE_AZ - 1)

        @pl.when(early & (j == 0))
        def _():
            extra_copy.wait_recv()
            for k in FAR_FIRST:
                share_extra(k, 0)
            gathered[2, me_az, :2] = extra[x]

        @pl.when(early | (j == 0))
        def _():
            send_tiles(j, EARLY_ORDER)

        @pl.when(j == 0)
        def _():
            send_tiles(0, LATE_ORDER)

        @pl.when((j == jnp.where(early, 2, 1)))
        def _():
            send_tiles(1, LATE_ORDER)

        return carry

    lax.fori_loop(0, jnp.where(early, 3, 2), work, 0)

    def keep(j):
        return pltpu.make_async_copy(
            tiles(ready, (j * SIDE_AZ + x) * GROUP + me_range, 1), tiles(arrived, beam_of(j), 1),
            keep_sem.at[j],
        )

    def settled(ref, send, recv, count):
        some = tiles(ref, 0, count)
        return remote(some, some, send, recv, az=me_az)

    keep(0).start()
    keep(1).start()

    @pl.when(early)
    def _():
        keep(2).start()
        settled(arrived, hist_send, hist_recv, GROUP * BEAMS - 3).wait_recv()
        keep(2).wait()

    @pl.when(late)
    def _():
        settled(arrived, hist_send, hist_recv, GROUP * BEAMS - 2).wait_recv()

    keep(0).wait()
    keep(1).wait()

    some = gathered.at[0, pl.ds(0, GROUP - 1)]
    remote(some, some, pulse_send, pulse_recv.at[0], az=me_az).wait_send()
    some = gathered.at[1, pl.ds(0, GROUP - 1), parts]
    remote(some, some, pulse_send, pulse_recv.at[1], az=me_az).wait_send()
    tiles_all, tiles_half = SIDE_AZ * GROUP - 1, SIDE_AZ * HALF - 1

    @pl.when(early)
    def _():
        remote(some, some, pulse_send, pulse_recv.at[1], az=me_az).wait_send()
        settled(ready, hist_send, hist_recv, 2 * tiles_all + tiles_half).wait_send()

    @pl.when(late)
    def _():
        extra_copy.wait_send()
        settled(ready, hist_send, hist_recv, tiles_all + tiles_half).wait_send()


def spread(arrived, out_ref, tiles, rows, in_sem, out_sem):
    step = GROUP * BEAMS // PIECES
    fetches = [
        pltpu.make_async_copy(
            arrived.at[pl.ds(k * step * 8, step * 8)], tiles.at[pl.ds(k * step * 8, step * 8)], in_sem.at[k]
        )
        for k in range(PIECES)
    ]
    for fetch in fetches:
        fetch.start()
    stores = []
    for k, fetch in enumerate(fetches):
        fetch.wait()
        for g in range(k * step // 8, (k + 1) * step // 8):
            for s in range(8):
                rows[0, g * 8 : (g + 1) * 8, s * SIDE : (s + 1) * SIDE] = tiles[
                    pl.ds(g * 64 + s, 8, stride=8), :
                ]
        some = pl.ds(k * step, step)
        stores.append(pltpu.make_async_copy(rows.at[:, some], out_ref.at[:, some], out_sem.at[k]))
        stores[-1].start()
    for store in stores:
        store.wait()


def per_device(lag, frac, amp, offset, count, ambient, pulse):
    lag, frac, amp = [jnp.swapaxes(v, 1, 2) for v in (lag, frac, amp)]
    hbm = pl.BlockSpec(memory_space=pltpu.HBM)
    dma = pltpu.SemaphoreType.DMA
    arrived = pl.pallas_call(
        kernel,
        out_shape=jax.ShapeDtypeStruct((GROUP * BEAMS * 8, SIDE), F32),
        in_specs=[hbm] * 6,
        out_specs=hbm,
        scratch_shapes=[
            pltpu.VMEM((1, SLOTS, SIDE), jnp.int32),
            pltpu.VMEM((1, SLOTS, SIDE), F32),
            pltpu.VMEM((1, SLOTS, SIDE), F32),
            pltpu.VMEM((1, 1), jnp.int32),
            pltpu.VMEM((1, SIDE), F32),
            pltpu.VMEM((BEAMS, 2, TIME_SLOTS // GROUP), F32),
            pltpu.VMEM((2, SIDE_AZ, 3, 8, SIDE), F32),
            pltpu.VMEM((3, GROUP, 3, 8, SIDE), F32),
            pltpu.VMEM((SIDE_AZ, 2, 8, SIDE), F32),
            pltpu.VMEM((SIDE_AZ, 2 * SIDE, 2 * SIDE), F32),
            pltpu.VMEM((2 * SIDE, 6 * SIDE), BF16),
            pltpu.VMEM((6 * SIDE, 2 * SIDE), BF16),
            pltpu.VMEM((2, SIDE, SIDE), F32),
            pltpu.VMEM((2 * SIDE, 2 * SIDE), BF16),
            pltpu.VMEM((SIDE, 2 * SIDE), BF16),
            pltpu.VMEM((3 * SIDE_AZ * SIDE, SIDE), F32),
            dma((6,)), dma((3,)), dma, dma, dma, dma((3,)), dma, dma,
            pltpu.SemaphoreType.REGULAR, pltpu.SemaphoreType.REGULAR,
        ],
        compiler_params=pltpu.CompilerParams(
            collective_id=0, has_side_effects=True, vmem_limit_bytes=VMEM_LIMIT
        ),
    )(lag, frac, amp, (offset * 16 + count).reshape(1, 1), ambient.reshape(1, SIDE), pulse)
    return pl.pallas_call(
        spread,
        out_shape=jax.ShapeDtypeStruct((1, GROUP * BEAMS, TIME_SLOTS // GROUP), F32),
        in_specs=[hbm],
        out_specs=hbm,
        scratch_shapes=[
            pltpu.VMEM((GROUP * BEAMS * 8, SIDE), F32),
            pltpu.VMEM((1, GROUP * BEAMS, TIME_SLOTS // GROUP), F32),
            dma((PIECES,)), dma((PIECES,)),
        ],
        compiler_params=pltpu.CompilerParams(vmem_limit_bytes=VMEM_LIMIT),
    )(arrived)


def solution(mesh):
    in_specs = (
        P("az", None, None),
        P("az", None, None),
        P("az", None, None),
        P("az"),
        P("az"),
        P(),
        P("range", None, "az"),
    )
    out_specs = P("az", None, "range")
    return jax.shard_map(
        per_device, mesh=mesh, in_specs=in_specs, out_specs=out_specs, check_vma=False
    )
```

```python
import math

import jax
import jax.numpy as jnp
from jax import lax
from jax.experimental import pallas as pl
from jax.experimental.pallas import tpu as pltpu
from jax.sharding import PartitionSpec as P

TIME_SLOTS = 16384
SIDE = 128
BEAMS = 8
SLOTS = 8
GROUP = 16
HALF = 8
FAR_FIRST = (10, 6, 9, 11, 14, 2, 8, 5, 7, 13, 15, 1, 3, 4, 12)
PIECES = 4
VMEM_LIMIT = 56 * 1024 * 1024
EARLY_ORDER = (1, 0, 3, 2, 7, 6, 5, 4)
LATE_ORDER = (8, 9, 14, 15, 10, 11, 12, 13)
SIDE_AZ = 4
MESH = pl.DeviceIdType.MESH
F32 = jnp.float32
BF16 = jnp.bfloat16


def iota(shape, dim):
    return lax.broadcasted_iota(jnp.int32, shape, dim)


def cos_sin(turns):
    x = (turns - jnp.round(turns)) * math.pi
    y = x * x
    s = -1.0 / 39916800 * y + 1.0 / 362880
    s = s * y - 1.0 / 5040
    s = s * y + 1.0 / 120
    s = s * y - 1.0 / 6
    s = (s * y + 1.0) * x
    c = 1.0 / 479001600 * y - 1.0 / 3628800
    c = c * y + 1.0 / 40320
    c = c * y - 1.0 / 720
    c = c * y + 1.0 / 24
    c = c * y - 0.5
    c = c * y + 1.0
    return 1.0 - 2.0 * s * s, 2.0 * s * c


def split(x):
    hi = x.astype(BF16)
    return hi, (x - hi.astype(F32)).astype(BF16)


def dot(a, b):
    return jnp.dot(a, b, preferred_element_type=F32)


def blocks(a, b, c, d):
    return jnp.concatenate(
        [jnp.concatenate([a, b], axis=1), jnp.concatenate([c, d], axis=1)], axis=0
    )


def dft_tables():
    row, col = iota((SIDE, SIDE), 0), iota((SIDE, SIDE), 1)
    c, s = cos_sin(((row * col) & (SIDE - 1)).astype(F32) * (1.0 / SIDE))
    left = split(blocks(c, -s, s, c))
    right = split(blocks(c, s, -s, c))
    twist = cos_sin((row * col).astype(F32) * (1.0 / TIME_SLOTS))
    return left, right, twist


def prefix_tables():
    row, col = iota((SIDE, SIDE), 0), iota((SIDE, SIDE), 1)
    upper = jnp.where(row < col, 1.0, 0.0).astype(F32)
    ones = jnp.ones((SIDE, SIDE), F32)
    lower = jnp.where(col < row, 1.0, 0.0).astype(F32)
    inner = blocks(upper, ones, upper, ones).astype(BF16)
    outer = jnp.concatenate([lower, lower], axis=1).astype(BF16)
    return inner, outer


def as_column(rows, lane):
    return jnp.sum(jnp.where(iota(rows.shape, 1) == lane, rows, 0.0), axis=1, keepdims=True)


def as_row(column):
    row, col = iota((SIDE, SIDE), 0), iota((SIDE, SIDE), 1)
    wide = jnp.broadcast_to(column, (SIDE, SIDE))
    return jnp.sum(jnp.where(row == col, wide, 0.0), axis=0, keepdims=True)


def phase_tables(delay, frac, amp):
    delay, frac, amp = [jnp.concatenate([v, v], axis=0) for v in (delay, frac, amp)]
    row, col = iota((SIDE, SIDE), 0), iota((SIDE, SIDE), 1)
    whole = (col * delay.astype(jnp.int32)) & (TIME_SLOTS - 1)
    c, s = cos_sin((whole.astype(F32) + col.astype(F32) * frac) * (1.0 / TIME_SLOTS))
    inner = jnp.where(row < SIDE // 2, c, s) * amp
    near_row = (row & SLOTS) == 0
    right = split(
        jnp.concatenate([jnp.where(near_row, inner, 0.0), jnp.where(near_row, 0.0, inner)], axis=1)
    )
    signed = row - jnp.where(row >= SIDE // 2, SIDE, 0)
    whole = (signed * as_row(delay).astype(jnp.int32)) & (SIDE - 1)
    c, s = cos_sin((whole.astype(F32) + signed.astype(F32) * as_row(frac)) * (1.0 / SIDE))
    cosines = col < SIDE // 2
    hi, lo = split(jnp.concatenate([jnp.where(cosines, c, -s), jnp.where(cosines, -s, -c)], axis=0))
    return jnp.concatenate([hi, hi, lo], axis=1), right


def spectrum(left, right, column):
    mine = ((iota((SIDE, 2 * SIDE), 0) & (SIDE // 2 - 1)) >> 4) == column
    hi, lo = [jnp.where(mine, x.astype(F32), 0.0).astype(BF16) for x in right]
    return dot(left, jnp.concatenate([hi, lo, hi], axis=0))


def side_by_side(*parts):
    return jnp.concatenate(parts, axis=1)


def stacked(*parts):
    return jnp.concatenate(parts, axis=0)


def group_histogram(specs, pulses, ambients, left, right, twist, inner, outer):
    count = len(specs)
    rows = []
    for spec, (pulse_real, pulse_imag) in zip(specs, pulses):
        real, imag = spec[:SIDE], spec[SIDE:]
        wide_real, wide_imag = side_by_side(pulse_real, pulse_real), side_by_side(pulse_imag, pulse_imag)
        hi, lo = split(stacked(wide_real * real - wide_imag * imag, wide_real * imag + wide_imag * real))
        section = dot(left, stacked(hi, lo, hi))
        for trip in range(2):
            real = section[:SIDE, trip * SIDE : (trip + 1) * SIDE]
            imag = section[SIDE:, trip * SIDE : (trip + 1) * SIDE]
            rows.append(side_by_side(real * twist[0] - imag * twist[1], real * twist[1] + imag * twist[0]))
    hi, lo = split(stacked(*rows))
    field = dot(side_by_side(hi, lo, hi), right)
    fluxes = []
    for j in range(count):
        power = field[2 * SIDE * j : 2 * SIDE * (j + 1)]
        power = power * power
        power = power[:SIDE] + power[SIDE:]
        power = power[:, :SIDE] + power[:, SIDE:]
        fluxes.append(jnp.transpose((power * (1.0 / TIME_SLOTS) + ambients[j]) * (1.0 / TIME_SLOTS)))
    flux = stacked(*fluxes)
    hi, lo = split(flux)
    sums = dot(side_by_side(hi, lo), inner)
    hi, lo = split(side_by_side(*[sums[SIDE * j : SIDE * (j + 1), SIDE:] for j in range(count)]))
    carried = dot(outer, stacked(hi, lo))
    before = stacked(
        *[sums[SIDE * j : SIDE * (j + 1), :SIDE] + carried[:, SIDE * j : SIDE * (j + 1)] for j in range(count)]
    )
    series = 1.0 - flux * 0.25
    series = 1.0 - flux * (1.0 / 3) * series
    series = 1.0 - flux * 0.5 * series
    detected = jnp.where(flux < 1.0 / 32, flux * series, 1.0 - jnp.exp(-flux))
    return TIME_SLOTS * detected * jnp.exp(-before)


def kernel(
    lag_hbm, frac_hbm, amp_hbm, packed_hbm, ambient_hbm, pulse_hbm,
    arrived,
    lag_ref, frac_ref, amp_ref, packed_ref, ambient_ref, pulse_ref,
    own, gathered, extra, spec, left_tab, right_tab, twist_tab, inner_tab, outer_tab,
    ready,
    in_sem, keep_sem, extra_send, extra_recv, pulse_send, pulse_recv, hist_send, hist_recv, go_sem, near_sem,
):
    me_range, me_az = lax.axis_index("range"), lax.axis_index("az")
    y, x = me_az // SIDE_AZ, lax.rem(me_az, SIDE_AZ)
    chief = GROUP - 1
    early = me_range < HALF
    late = jnp.logical_not(early)
    partner = lax.rem(me_range + HALF, GROUP)

    def remote(src, dst, send, recv, **where):
        return pltpu.make_async_remote_copy(
            src_ref=src, dst_ref=dst, send_sem=send, recv_sem=recv, device_id=where, device_id_type=MESH
        )

    fetches = [
        pltpu.make_async_copy(src, dst, in_sem.at[i])
        for i, (src, dst) in enumerate(
            (
                (pulse_hbm, pulse_ref), (lag_hbm, lag_ref), (frac_hbm, frac_ref), (amp_hbm, amp_ref),
                (packed_hbm, packed_ref), (ambient_hbm, ambient_ref),
            )
        )
    ]
    for fetch in fetches:
        fetch.start()

    barrier = pltpu.get_barrier_semaphore()

    def greet(k, carry):
        pl.semaphore_signal(
            barrier, inc=1, device_id={"az": lax.rem(me_az + k, GROUP)}, device_id_type=MESH
        )
        return carry

    lax.fori_loop(1, GROUP, greet, 0)

    @pl.when(me_range != chief)
    def _():
        pl.semaphore_signal(barrier, inc=1, device_id={"range": chief}, device_id_type=MESH)

    @pl.when(early)
    def _():
        pl.semaphore_signal(barrier, inc=1, device_id={"range": partner}, device_id_type=MESH)

    fetches[0].wait()
    for b in range(BEAMS):
        for part in range(2):
            for q in range(8):
                own[b % 2, b // 2, part, q : q + 1, :] = pulse_ref[b, part : part + 1, q * SIDE : (q + 1) * SIDE]
    for fetch in fetches[1:]:
        fetch.wait()
    first = me_range * BEAMS
    delay = (lag_ref[0] + (packed_ref[...] >> 4)).astype(F32)
    live = iota((SLOTS, SIDE), 0) < (packed_ref[...] & 15)
    amp = jnp.where(live, amp_ref[0], 0.0)
    delay, frac, amp = [
        pltpu.roll(v, lax.rem(2 * SIDE + BEAMS * i - first, SIDE), 1)
        for i, v in enumerate((delay, frac_ref[0], amp))
    ]
    lane = iota((SLOTS, SIDE), 1) & (SIDE // 2 - 1)
    echo = jnp.where(lane < BEAMS, delay, jnp.where(lane < 2 * BEAMS, frac, amp))
    for b in range(SIDE_AZ):
        own[0, b, 2] = echo

    pl.semaphore_wait(
        barrier,
        GROUP - 1 + jnp.where(early, 0, 1) + jnp.where(me_range == chief, GROUP - 1, 0),
    )
    parts = pl.ds(0, 2)
    extra_copy = remote(own.at[1, :, parts], extra, extra_send, extra_recv, range=partner)


    def share(k, carry):
        peer = lax.rem(me_az + k, GROUP)
        mine = own.at[0, lax.rem(peer, SIDE_AZ)]
        remote(mine, gathered.at[0, me_az], pulse_send, pulse_recv.at[0], az=peer).start()
        return carry

    def share_next(k, carry):
        peer = lax.rem(me_az + k, GROUP)
        mine = own.at[1, lax.rem(peer, SIDE_AZ), parts]
        remote(mine, gathered.at[1, me_az, parts], pulse_send, pulse_recv.at[1], az=peer).start()
        return carry

    def share_extra(k, carry):
        peer = lax.rem(me_az + k, GROUP)
        mine = extra.at[lax.rem(peer, SIDE_AZ)]
        remote(mine, gathered.at[2, me_az, parts], pulse_send, pulse_recv.at[2], az=peer).start()
        return carry

    for k in FAR_FIRST:
        share(k, 0)

    @pl.when(late)
    def _():
        extra_copy.start()

    for k in FAR_FIRST:
        share_next(k, 0)

    @pl.when(me_range == chief)
    def _():
        def tell(k, carry):
            pl.semaphore_signal(go_sem, inc=1, device_id={"range": k}, device_id_type=MESH)
            return carry

        lax.fori_loop(0, GROUP - 1, tell, 0)

    gathered[0, me_az] = own[0, x]
    gathered[1, me_az] = own[1, x]

    left, right, twist = dft_tables()
    left_tab[...] = side_by_side(left[0], left[0], left[1])
    right_tab[...] = stacked(right[0], right[0], right[1])
    twist_tab[0], twist_tab[1] = twist
    inner_tab[...], outer_tab[...] = prefix_tables()

    @pl.when(me_range != chief)
    def _():
        pl.semaphore_wait(go_sem, 1)

    for k in range(1, SIDE_AZ):
        pl.semaphore_signal(
            near_sem, inc=1, device_id={"az": y * SIDE_AZ + lax.rem(x + k, SIDE_AZ)}, device_id_type=MESH
        )

    some = gathered.at[0, pl.ds(0, GROUP - 1)]
    remote(some, some, pulse_send, pulse_recv.at[0], az=me_az).wait_recv()
    def phases(j):
        rows = []
        for i in range(SIDE_AZ):
            rows.append(gathered[0, y * SIDE_AZ + i, 2])
            rows.append(gathered[0, lax.rem(y * SIDE_AZ + i + GROUP - 1, GROUP), 2])
        rows = stacked(*rows)
        place = 2 * x + jnp.where(j == 0, 0, 1) + jnp.where(j == 2, SIDE // 2, 0)
        delay, frac, amp = [as_column(rows, place + BEAMS * i) for i in range(3)]
        far = (iota(delay.shape, 0) & SLOTS) != 0
        return phase_tables(delay, frac, jnp.where(far == (delay >= TIME_SLOTS), amp, 0.0))

    def tiles_of(row, count):
        return pl.ds(pl.multiple_of(row * 8, 8), count * 8)

    def tiles(ref, row, count):
        return ref.at[tiles_of(row, count)]

    def beam_of(j):
        block = jnp.where(j == 2, partner, me_range)
        return block * BEAMS + 2 * x + jnp.where(j == 0, 0, 1)

    def send_tile(j, i, peer):
        @pl.when((peer != me_range) | (i != x))
        def _():
            remote(
                tiles(ready, (j * SIDE_AZ + i) * GROUP + peer, 1),
                tiles(arrived, beam_of(j), 1),
                hist_send, hist_recv, range=peer, az=y * SIDE_AZ + i,
            ).start()

    def send_tiles(j, order):
        for peer in order:
            for k in range(SIDE_AZ):
                send_tile(j, lax.rem(x + k, SIDE_AZ), peer)

    def work(j, carry):
        e_left, e_right = phases(j)
        for i in range(SIDE_AZ):
            spec[i] = spectrum(e_left, e_right, i)

        @pl.when(j > 0)
        def _():
            some = gathered.at[1, pl.ds(0, GROUP - 1), parts]
            remote(some, some, pulse_send, pulse_recv.at[j], az=me_az).wait_recv()

        specs = [spec[i] for i in range(SIDE_AZ)]
        pulse = [gathered[j, :, part].reshape(SIDE, SIDE) for part in range(2)]
        mine = iota((1, SIDE), 1) == beam_of(j)
        ambient = jnp.sum(jnp.where(mine, ambient_ref[...], 0.0), axis=1, keepdims=True)
        hist = group_histogram(
            specs, [pulse] * SIDE_AZ, [ambient] * SIDE_AZ, left_tab[...], right_tab[...],
            (twist_tab[0], twist_tab[1]), inner_tab[...], outer_tab[...],
        )
        ready[tiles_of(j * SIDE_AZ * GROUP, SIDE_AZ * GROUP), :] = hist

        @pl.when(j == 0)
        def _():
            pl.semaphore_wait(near_sem, SIDE_AZ - 1)

        @pl.when(early & (j == 0))
        def _():
            extra_copy.wait_recv()
            for k in FAR_FIRST:
                share_extra(k, 0)
            gathered[2, me_az, :2] = extra[x]

        @pl.when(early | (j == 0))
        def _():
            send_tiles(j, EARLY_ORDER)

        @pl.when(j == 0)
        def _():
            send_tiles(0, LATE_ORDER)

        @pl.when((j == jnp.where(early, 2, 1)))
        def _():
            send_tiles(1, LATE_ORDER)

        return carry

    lax.fori_loop(0, jnp.where(early, 3, 2), work, 0)

    def keep(j):
        return pltpu.make_async_copy(
            tiles(ready, (j * SIDE_AZ + x) * GROUP + me_range, 1), tiles(arrived, beam_of(j), 1),
            keep_sem.at[j],
        )

    def settled(ref, send, recv, count):
        some = tiles(ref, 0, count)
        return remote(some, some, send, recv, az=me_az)

    keep(0).start()
    keep(1).start()

    @pl.when(early)
    def _():
        keep(2).start()
        settled(arrived, hist_send, hist_recv, GROUP * BEAMS - 3).wait_recv()
        keep(2).wait()

    @pl.when(late)
    def _():
        settled(arrived, hist_send, hist_recv, GROUP * BEAMS - 2).wait_recv()

    keep(0).wait()
    keep(1).wait()

    some = gathered.at[0, pl.ds(0, GROUP - 1)]
    remote(some, some, pulse_send, pulse_recv.at[0], az=me_az).wait_send()
    some = gathered.at[1, pl.ds(0, GROUP - 1), parts]
    remote(some, some, pulse_send, pulse_recv.at[1], az=me_az).wait_send()
    tiles_all, tiles_half = SIDE_AZ * GROUP - 1, SIDE_AZ * HALF - 1

    @pl.when(early)
    def _():
        remote(some, some, pulse_send, pulse_recv.at[1], az=me_az).wait_send()
        settled(ready, hist_send, hist_recv, 2 * tiles_all + tiles_half).wait_send()

    @pl.when(late)
    def _():
        extra_copy.wait_send()
        settled(ready, hist_send, hist_recv, tiles_all + tiles_half).wait_send()


def spread(arrived, out_ref, tiles, rows, in_sem, out_sem):
    step = GROUP * BEAMS // PIECES
    fetches = [
        pltpu.make_async_copy(
            arrived.at[pl.ds(k * step * 8, step * 8)], tiles.at[pl.ds(k * step * 8, step * 8)], in_sem.at[k]
        )
        for k in range(PIECES)
    ]
    for fetch in fetches:
        fetch.start()
    stores = []
    for k, fetch in enumerate(fetches):
        fetch.wait()
        for g in range(k * step // 8, (k + 1) * step // 8):
            for s in range(8):
                rows[0, g * 8 : (g + 1) * 8, s * SIDE : (s + 1) * SIDE] = tiles[
                    pl.ds(g * 64 + s, 8, stride=8), :
                ]
        some = pl.ds(k * step, step)
        stores.append(pltpu.make_async_copy(rows.at[:, some], out_ref.at[:, some], out_sem.at[k]))
        stores[-1].start()
    for store in stores:
        store.wait()


def per_device(lag, frac, amp, offset, count, ambient, pulse):
    lag, frac, amp = [jnp.swapaxes(v, 1, 2) for v in (lag, frac, amp)]
    hbm = pl.BlockSpec(memory_space=pltpu.HBM)
    dma = pltpu.SemaphoreType.DMA
    arrived = pl.pallas_call(
        kernel,
        out_shape=jax.ShapeDtypeStruct((GROUP * BEAMS * 8, SIDE), F32),
        in_specs=[hbm] * 6,
        out_specs=hbm,
        scratch_shapes=[
            pltpu.VMEM((1, SLOTS, SIDE), jnp.int32),
            pltpu.VMEM((1, SLOTS, SIDE), F32),
            pltpu.VMEM((1, SLOTS, SIDE), F32),
            pltpu.VMEM((1, 1), jnp.int32),
            pltpu.VMEM((1, SIDE), F32),
            pltpu.VMEM((BEAMS, 2, TIME_SLOTS // GROUP), F32),
            pltpu.VMEM((2, SIDE_AZ, 3, 8, SIDE), F32),
            pltpu.VMEM((3, GROUP, 3, 8, SIDE), F32),
            pltpu.VMEM((SIDE_AZ, 2, 8, SIDE), F32),
            pltpu.VMEM((SIDE_AZ, 2 * SIDE, 2 * SIDE), F32),
            pltpu.VMEM((2 * SIDE, 6 * SIDE), BF16),
            pltpu.VMEM((6 * SIDE, 2 * SIDE), BF16),
            pltpu.VMEM((2, SIDE, SIDE), F32),
            pltpu.VMEM((2 * SIDE, 2 * SIDE), BF16),
            pltpu.VMEM((SIDE, 2 * SIDE), BF16),
            pltpu.VMEM((3 * SIDE_AZ * SIDE, SIDE), F32),
            dma((6,)), dma((3,)), dma, dma, dma, dma((3,)), dma, dma,
            pltpu.SemaphoreType.REGULAR, pltpu.SemaphoreType.REGULAR,
        ],
        compiler_params=pltpu.CompilerParams(
            collective_id=0, has_side_effects=True, vmem_limit_bytes=VMEM_LIMIT
        ),
    )(lag, frac, amp, (offset * 16 + count).reshape(1, 1), ambient.reshape(1, SIDE), pulse)
    return pl.pallas_call(
        spread,
        out_shape=jax.ShapeDtypeStruct((1, GROUP * BEAMS, TIME_SLOTS // GROUP), F32),
        in_specs=[hbm],
        out_specs=hbm,
        scratch_shapes=[
            pltpu.VMEM((GROUP * BEAMS * 8, SIDE), F32),
            pltpu.VMEM((1, GROUP * BEAMS, TIME_SLOTS // GROUP), F32),
            dma((PIECES,)), dma((PIECES,)),
        ],
        compiler_params=pltpu.CompilerParams(vmem_limit_bytes=VMEM_LIMIT),
    )(arrived)


def solution(mesh):
    in_specs = (
        P("az", None, None),
        P("az", None, None),
        P("az", None, None),
        P("az"),
        P("az"),
        P(),
        P("range", None, "az"),
    )
    out_specs = P("az", None, "range")
    return jax.shard_map(
        per_device, mesh=mesh, in_specs=in_specs, out_specs=out_specs, check_vma=False
    )
```
